32 devices in a mesh: slot: 8 (over z, y), row: 2 (over core), col: 2 (over x).
Axes of the slice: x: 2, y: 2, z: 4, core: 2. Of those that a mesh axis runs over, the one named last changes fastest.
Arguments:
- hidden: bfloat16 [8, 32, 4096], P('slot', None, 'row'), may hold values from -20 to 20
- w_query: bfloat16 [4096, 4096], P('row', 'col'), may hold values from -0.09375 to 0.09375
- key_weight: bfloat16 [4096, 1024], P('row', 'col'), may hold values from -0.09375 to 0.09375
- value_weight: bfloat16 [4096, 1024], P('row', 'col'), may hold values from -0.09375 to 0.09375
- w_out: bfloat16 [4096, 4096], P('col', 'row'), may hold values from -0.09375 to 0.09375
- kv_store: bfloat16 [512, 2, 8, 1024], P(('slot', 'row'), None, None, 'col'), may hold values from -250 to 250
- stretch_offset: int32 [512], replicated, may hold values from 0 to 4095
- tile_stretch: int32 [8, 64], replicated, may hold values from 0 to 511, as said below
- slot_count: int32 [8], replicated, may hold values from 40 to 64, as said below
- recomp_pos: int32 [8, 32], P('slot'), may hold values from 0 to 511, as said below
Outputs:
- attn_out: bfloat16 [8, 32, 4096], P('slot', 'col', 'row')
The draws below stay inside these ranges and needn't reach their ends.
Inputs may be any that keep to these rules, and one draw needn't show every extreme that they name: Within each aligned block of 32 tiles of a slot, every value of tile_stretch // 32 that occurs occurs exactly 2 times, and 16 distinct such values occur. `slot_count`: one slot uses all 64 tiles. `recomp_pos`: entry i of slot s lies in [i * q, (i + 1) * q) with q = slot_count[s] * 8 // 32.
All inputs are finite; a program needn't handle non-finite values.
Results may differ from the reference program's by a relative error of at most 0.018.
The reference program's roundings to bfloat16 on the way (of `joined_keys`, `joined_values`, `probs_low` and `attended`) count: a program that leaves them out, or rounds other values in their place, can miss the bound.
Values may be sent and summed in bfloat16 or wider, within the bound.
No kernel may reach another device: no remote copies, remote signals or barrier semaphores. Data moves between devices by JAX's collectives and lax.ppermute only.
A program may use at most 128 MiB of HBM per device.

```python
import math
import jax
import jax.numpy as jnp
from jax import lax

MODEL_WIDTH = 4096
QUERY_HEADS = 32
KEY_VALUE_HEADS = 8
HEAD_WIDTH = 128
STRETCH_TOKENS = 8
SLOTS = 8
GROUP = 16
TILES_DEV = 32
SLOT_TILE_LIMIT = 64
STORE_STRETCHES = 512
CAP = 2
REDONE_TOKENS = 32


def make_plan(key):
    plan_key = jax.random.fold_in(key, 11)
    count_key, full_key, owner_key, order_key, local_key, offset_key = jax.random.split(plan_key, 6)
    counts = jax.random.randint(count_key, (SLOTS,), 5 * SLOT_TILE_LIMIT // 8, SLOT_TILE_LIMIT + 1)
    full_slot = jax.random.randint(full_key, (), 0, SLOTS)
    counts = jnp.where(jnp.arange(SLOTS) == full_slot, SLOT_TILE_LIMIT, counts).astype(jnp.int32)
    distinct = TILES_DEV // CAP
    chosen = jax.vmap(lambda sub_key: jax.random.permutation(sub_key, GROUP)[:distinct])(jax.random.split(owner_key, GROUP))
    repeated = jnp.repeat(chosen, CAP, axis=1)
    shuffle = jax.vmap(lambda sub_key: jax.random.permutation(sub_key, TILES_DEV))(jax.random.split(order_key, GROUP))
    owners = jnp.take_along_axis(repeated, shuffle, axis=1)
    locals_drawn = jax.random.randint(local_key, (GROUP, TILES_DEV), 0, TILES_DEV)
    stretches = (owners * TILES_DEV + locals_drawn).reshape(SLOTS, SLOT_TILE_LIMIT).astype(jnp.int32)
    stride = counts * STRETCH_TOKENS // REDONE_TOKENS
    offsets = jax.random.randint(offset_key, (SLOTS, REDONE_TOKENS), 0, stride[:, None])
    positions = (jnp.arange(REDONE_TOKENS, dtype=jnp.int32)[None, :] * stride[:, None] + offsets).astype(jnp.int32)
    return (counts, stretches, positions)


def draw_tile_stretch(key, part):
    return make_plan(key)[1]


def draw_slot_count(key, part):
    return make_plan(key)[0]


def draw_recomp_pos(key, part):
    return make_plan(key)[2]


def draw_hidden(key, part):
    value_random_key = jax.random.fold_in(jax.random.fold_in(key, 5), 0)
    stored_values = jnp.clip(jax.random.normal(value_random_key, (SLOTS, REDONE_TOKENS, MODEL_WIDTH), jnp.float32), -5.0, 5.0)
    return stored_values.astype(jnp.bfloat16)


def draw_kv_store(key, part):
    value_random_key = jax.random.fold_in(jax.random.fold_in(key, 3), 0)
    stored_values = jnp.clip(jax.random.normal(value_random_key, (STORE_STRETCHES, 2, STRETCH_TOKENS, KEY_VALUE_HEADS * HEAD_WIDTH), jnp.float32), -4.0, 4.0)
    return stored_values.astype(jnp.bfloat16)


def touch_ends(drawn, stream_key, least, top_value):
    longest = drawn.shape.index(max(drawn.shape))
    spots = []
    for shift in (0, 1):
        where = [jax.random.randint(jax.random.fold_in(stream_key, axis), (), 0, length) for axis, length in enumerate(drawn.shape)]
        where[longest] = (where[longest] + shift) % drawn.shape[longest]
        spots.append(tuple(where))
    return drawn.at[spots[0]].set(least).at[spots[1]].set(top_value)


def level_of(stream_key, shape, shards, low, largest):
    level = 1.0
    for position, shards_of in shards:
        heights = jax.random.uniform(jax.random.fold_in(jax.random.fold_in(stream_key, 6), position), (shards_of,), jnp.float32, low / len(shards), largest / len(shards))
        level = level * jnp.repeat(jnp.exp(heights), shape[position] // shards_of).reshape((-1,) + (1,) * (len(shape) - 1 - position))
    return level


def bell_draw(own_key, shape, width, most, shards=(), kind=jnp.bfloat16):
    entries = width * jax.random.normal(own_key, shape, jnp.float32)
    if shards:
        entries = entries * level_of(own_key, shape, shards, -0.22, 0.18)
    return jnp.clip(entries, -most, most).astype(kind)


def setup_inputs(seed: int = 0) -> dict:
    streams_of = jax.random.split(jax.random.key(seed), 11)
    return {
        "hidden": draw_hidden(jax.random.fold_in(streams_of[10], 71), 0),
        "w_query": bell_draw(streams_of[1], (MODEL_WIDTH, QUERY_HEADS * HEAD_WIDTH), MODEL_WIDTH ** -0.5, 0.09375, ((0, 2), (1, 2))),
        "key_weight": bell_draw(streams_of[2], (MODEL_WIDTH, KEY_VALUE_HEADS * HEAD_WIDTH), MODEL_WIDTH ** -0.5, 0.09375, ((0, 2), (1, 2))),
        "value_weight": bell_draw(streams_of[3], (MODEL_WIDTH, KEY_VALUE_HEADS * HEAD_WIDTH), MODEL_WIDTH ** -0.5, 0.09375, ((0, 2), (1, 2))),
        "w_out": bell_draw(streams_of[4], (QUERY_HEADS * HEAD_WIDTH, MODEL_WIDTH), (QUERY_HEADS * HEAD_WIDTH) ** -0.5, 0.09375, ((0, 2), (1, 2))),
        "kv_store": draw_kv_store(jax.random.fold_in(streams_of[10], 71), 0),
        "stretch_offset": touch_ends(jax.random.randint(streams_of[6], (STORE_STRETCHES,), 0, 4096), jax.random.fold_in(streams_of[6], 1), 0, 4095).astype(jnp.int32),
        "tile_stretch": draw_tile_stretch(jax.random.fold_in(streams_of[10], 71), 0),
        "slot_count": draw_slot_count(jax.random.fold_in(streams_of[10], 71), 0),
        "recomp_pos": draw_recomp_pos(jax.random.fold_in(streams_of[10], 71), 0),
    }


NEGATIVE = -1e+30
ROPE_BASE = 500000.0

def frequencies(head_size):
    freq_index = jnp.arange(head_size // 2, dtype=jnp.float32)
    return ROPE_BASE ** (-2.0 * freq_index / head_size)

def apply_rotation(vectors, angles):
    half_dim = vectors.shape[-1] // 2
    front_half = vectors[..., :half_dim]
    back_half = vectors[..., half_dim:]
    cosine_part = jnp.cos(angles)
    sine_part = jnp.sin(angles)
    return jnp.concatenate([front_half * cosine_part - back_half * sine_part, back_half * cosine_part + front_half * sine_part], axis=-1)

def reference(hidden, w_query, key_weight, value_weight, w_out, kv_store, stretch_offset, tile_stretch, slot_count, recomp_pos):
    freq_table = frequencies(HEAD_WIDTH)
    all_weights = jnp.concatenate([w_query, key_weight, value_weight], axis=1)
    query_columns = QUERY_HEADS * HEAD_WIDTH
    key_value_columns = KEY_VALUE_HEADS * HEAD_WIDTH
    queries_per_key_head = QUERY_HEADS // KEY_VALUE_HEADS
    total_keys = SLOT_TILE_LIMIT * STRETCH_TOKENS
    score_scale = 1.0 / math.sqrt(HEAD_WIDTH)

    def one_slot(slot_args):
        tokens, stretches, used_tiles, positions = slot_args
        gathered_rows = jnp.take(kv_store, stretches, axis=0)
        key_shift = jnp.arange(SLOT_TILE_LIMIT, dtype=jnp.int32) * STRETCH_TOKENS - jnp.take(stretch_offset, stretches)
        key_angle = key_shift.astype(jnp.float32)[:, None, None, None] * freq_table
        unrotated_keys = gathered_rows[:, 0].astype(jnp.float32).reshape(SLOT_TILE_LIMIT, STRETCH_TOKENS, KEY_VALUE_HEADS, HEAD_WIDTH)
        joined_keys = apply_rotation(unrotated_keys, key_angle).astype(jnp.bfloat16).reshape(total_keys, key_value_columns)
        joined_values = gathered_rows[:, 1].reshape(total_keys, key_value_columns)
        projected_rows = jnp.dot(tokens, all_weights, preferred_element_type=jnp.float32)
        token_angle = positions.astype(jnp.float32)[:, None, None] * freq_table
        queries = apply_rotation(projected_rows[:, :query_columns].reshape(REDONE_TOKENS, QUERY_HEADS, HEAD_WIDTH), token_angle).astype(jnp.bfloat16)
        fresh_keys = apply_rotation(projected_rows[:, query_columns:query_columns + key_value_columns].reshape(REDONE_TOKENS, KEY_VALUE_HEADS, HEAD_WIDTH), token_angle).astype(jnp.bfloat16).reshape(REDONE_TOKENS, key_value_columns)
        new_values = projected_rows[:, query_columns + key_value_columns:].astype(jnp.bfloat16)
        joined_keys = joined_keys.at[positions].set(fresh_keys)
        joined_values = joined_values.at[positions].set(new_values)
        key_pos = jnp.arange(total_keys, dtype=jnp.int32)
        allowed = jnp.logical_and(key_pos[None, :] <= positions[:, None], key_pos[None, :] < used_tiles * STRETCH_TOKENS)

        def query_head_group(group_index):
            group_queries = lax.dynamic_slice_in_dim(queries, group_index * queries_per_key_head, queries_per_key_head, 1).astype(jnp.float32)
            group_keys = lax.dynamic_slice_in_dim(joined_keys, group_index * HEAD_WIDTH, HEAD_WIDTH, 1).astype(jnp.float32)
            group_values = lax.dynamic_slice_in_dim(joined_values, group_index * HEAD_WIDTH, HEAD_WIDTH, 1).astype(jnp.float32)
            scores = jnp.einsum('qjd,kd->qjk', group_queries, group_keys) * score_scale
            scores = jnp.where(allowed[:, None, :], scores, NEGATIVE)
            peak_score = lax.optimization_barrier(jnp.max(scores, axis=2, keepdims=True))
            probs = jnp.where(allowed[:, None, :], jnp.exp(scores - peak_score), 0.0)
            totals = lax.optimization_barrier(jnp.sum(probs, axis=2))
            probs_low = lax.optimization_barrier(probs.astype(jnp.bfloat16)).astype(jnp.float32)
            weighted = jnp.einsum('qjk,kd->qjd', probs_low, group_values)
            return (weighted / totals[..., None]).astype(jnp.bfloat16)
        group_count = lax.map(query_head_group, jnp.arange(KEY_VALUE_HEADS, dtype=jnp.int32))
        attended = jnp.transpose(group_count, (1, 0, 2, 3)).reshape(REDONE_TOKENS, query_columns)
        return jnp.dot(attended, w_out, preferred_element_type=jnp.float32).astype(jnp.bfloat16)
    return lax.map(one_slot, (hidden, tile_stretch, slot_count, recomp_pos))
```

```python
import functools
import math

import jax
import jax.numpy as jnp
import numpy as np
from jax import lax
from jax.experimental import pallas as pl
from jax.experimental.pallas import tpu as pltpu
from jax.sharding import PartitionSpec as P

HEAD_WIDTH = 128
NEGATIVE = -1e30
ROPE_BASE = 500000.0
MIB = 1024 * 1024
FAR = 1 << 28
F32 = jnp.float32
BF16 = jnp.bfloat16
VMEM = pl.BlockSpec(memory_space=pltpu.VMEM)
ANY = pl.BlockSpec(memory_space=pl.ANY)
SMEM = pl.BlockSpec(memory_space=pltpu.SMEM)


def iota(shape, dim):
    return lax.broadcasted_iota(jnp.int32, shape, dim)


def divide(value, by):
    if by & (by - 1) == 0:
        shift = by.bit_length() - 1
        return lax.shift_right_logical(value, jnp.full_like(value, shift)), value & (by - 1)
    quotient = jnp.floor((value.astype(F32) + 0.5) * (1.0 / by)).astype(jnp.int32)
    return quotient, value - quotient * by


def earlier_count(flags):
    n = flags.shape[1]
    before = (iota((n, n), 0) < iota((n, n), 1)).astype(BF16)
    return jnp.dot(flags.astype(BF16), before, preferred_element_type=F32)


def pack_kernel(tiles, ranks, stretch_len, stretches_ref, store_ref, out_ref):
    own = lax.axis_index("slot") * lax.axis_size("row") + lax.axis_index("row")
    slots, slot_tiles = stretches_ref.shape
    owner, local = divide(stretches_ref[...], tiles)
    mine = (owner == own).astype(F32)
    rank = earlier_count(mine)
    lane = iota((slots, 128), 1)
    ids = jnp.zeros((slots, 128), F32)
    for k in range(ranks):
        picked = jnp.where(rank == k, mine * local.astype(F32), 0.0)
        ids = jnp.where(lane == k, jnp.sum(picked, axis=1, keepdims=True), ids)
    per_slot = ranks * 2 * stretch_len
    rows = slots * per_slot
    ids = jnp.broadcast_to(ids[:, None, :], (slots, per_slot, 128)).reshape(rows, 128)
    part, token = divide(iota((rows, 128), 0), stretch_len)
    part, rank_of_row = divide(part, ranks)
    kind = part & 1
    stretch = jnp.sum(
        jnp.where(iota((rows, 128), 1) == rank_of_row, ids, 0.0), axis=1, keepdims=True
    ).astype(jnp.int32)
    source = stretch * (2 * stretch_len) + kind[:, :1] * stretch_len + token[:, :1]
    store_rows = tiles * 2 * stretch_len
    pick = (iota((rows, store_rows), 1) == source).astype(F32).astype(BF16)
    out_ref[...] = jnp.dot(pick, store_ref[...], preferred_element_type=F32).astype(BF16)


def project_kernel(step, hidden_ref, wq_ref, wk_ref, wv_ref, out_ref, wq, wk, wv, sems):
    pieces = []
    for source, target in ((wk_ref, wk), (wv_ref, wv), (wq_ref, wq)):
        for start in range(0, source.shape[1], step):
            pieces.append((source, target, start))
    offsets = {id(wq): 0, id(wk): wq_ref.shape[1], id(wv): wq_ref.shape[1] + wk_ref.shape[1]}
    copies = []
    for i, (source, target, start) in enumerate(pieces):
        cols = pl.ds(start, step)
        copy = pltpu.make_async_copy(source.at[:, cols], target.at[:, cols], sems.at[i])
        copy.start()
        copies.append(copy)
    tokens = hidden_ref[...]
    for (source, target, start), copy in zip(pieces, copies):
        copy.wait()
        base = offsets[id(target)] + start
        out_ref[:, base : base + step] = jnp.dot(
            tokens, target[:, start : start + step], preferred_element_type=F32
        )


def angle_tables(shift, freq):
    angle = shift.astype(F32) * freq
    low = iota(angle.shape, 1) < HEAD_WIDTH // 2
    sine = jnp.sin(angle)
    return jnp.cos(angle), jnp.where(low, -sine, sine)


def rotated(vectors, cosine, sine):
    return vectors * cosine + pltpu.roll(vectors, HEAD_WIDTH // 2, 1) * sine


def prepare_kernel(
    tiles,
    ranks,
    stretch_len,
    row_total,
    own_ref,
    other_ref,
    stretches_ref,
    offsets_ref,
    counts_ref,
    positions_ref,
    freq_ref,
    q_ref,
    keys_ref,
    values_ref,
    cos_ref,
    sin_ref,
    bias_ref,
):
    slot = lax.axis_index("slot")
    row = lax.axis_index("row")
    freq = freq_ref[...]
    count = counts_ref[slot]
    arriving = tiles
    slot_tiles = stretches_ref.shape[1]
    stretches = stretches_ref[pl.ds(slot, 1), :]
    owner, _ = divide(stretches, tiles)
    from_slot, rank_wanted = divide(iota((arriving, slot_tiles), 0), ranks)
    match = (owner == from_slot * row_total + row).astype(F32)
    rank = earlier_count(match)
    picked = jnp.where(rank == rank_wanted.astype(F32), match, 0.0)
    tile = jnp.sum(picked * iota((arriving, slot_tiles), 1).astype(F32), axis=1, keepdims=True)
    stretch = jnp.sum(picked * stretches.astype(F32), axis=1, keepdims=True)
    tile = tile.astype(jnp.int32)
    stretch = stretch.astype(jnp.int32)
    page_count = offsets_ref.shape[0]
    page, lane = divide(stretch, 128)
    in_lane = (iota((arriving, 128), 1) == lane).astype(BF16)
    offsets = offsets_ref[...]
    upper, lower = divide(offsets, 64)
    nt = (((1,), (1,)), ((), ()))
    upper = lax.dot_general(in_lane, upper.astype(BF16), nt, preferred_element_type=F32)
    lower = lax.dot_general(in_lane, lower.astype(BF16), nt, preferred_element_type=F32)
    in_page = (iota((arriving, page_count), 1) == page).astype(F32)
    offset = jnp.sum(in_page * (upper * 64.0 + lower), axis=1, keepdims=True).astype(jnp.int32)
    cosine, sine = angle_tables(tile * stretch_len - offset, freq)
    local_keys = arriving * stretch_len
    spread = lambda x: jnp.broadcast_to(
        x[:, None, :], (arriving, stretch_len, x.shape[1])
    ).reshape(local_keys, x.shape[1])
    cos_ref[...] = spread(cosine)
    sin_ref[...] = spread(sine)
    token_total = positions_ref.shape[1]
    share = token_total // row_total
    positions = positions_ref[...]
    group = q_ref.shape[1] // token_total
    query_positions = jnp.concatenate([positions] * group, axis=1)
    wide = jnp.broadcast_to(tile, (arriving, 128))
    _, token = divide(iota((local_keys, 1), 0), stretch_len)
    key_positions = spread(wide)[:, :1] * stretch_len + token
    redone = jnp.sum(
        (key_positions == positions).astype(F32), axis=1, keepdims=True
    )
    usable = jnp.logical_and(key_positions < count * stretch_len, redone == 0.0)
    key_positions = jnp.where(usable, key_positions, FAR)
    bias_ref[:local_keys, :] = jnp.where(key_positions <= query_positions, 0.0, NEGATIVE)
    square = iota((token_total, token_total), 0) == iota((token_total, token_total), 1)
    column = jnp.sum(
        jnp.where(square, positions.astype(F32), 0.0), axis=1, keepdims=True
    ).astype(jnp.int32)
    at_row = lambda x: functools.reduce(
        lambda kept, r: jnp.where(row == r, x[r * share : (r + 1) * share], kept),
        range(1, row_total),
        x[:share],
    )
    new_positions = at_row(column)
    new_usable = new_positions < count * stretch_len
    new_positions = jnp.where(new_usable, new_positions, FAR)
    bias_ref[local_keys:, :] = jnp.where(new_positions <= query_positions, 0.0, NEGATIVE)
    cosine, sine = angle_tables(column, freq)
    key_heads = q_ref.shape[0]
    query_columns = key_heads * group * HEAD_WIDTH
    key_columns = key_heads * HEAD_WIDTH
    for head in range(key_heads * group):
        cols = slice(head * HEAD_WIDTH, (head + 1) * HEAD_WIDTH)
        vectors = own_ref[:, cols] + other_ref[:, cols]
        rows = slice((head % group) * token_total, (head % group + 1) * token_total)
        q_ref[head // group, rows, :] = rotated(vectors, cosine, sine).astype(BF16)
    for head in range(key_heads):
        start = query_columns + head * HEAD_WIDTH
        vectors = own_ref[:, start : start + HEAD_WIDTH] + other_ref[:, start : start + HEAD_WIDTH]
        keys_ref[:, head * HEAD_WIDTH : (head + 1) * HEAD_WIDTH] = at_row(
            rotated(vectors, cosine, sine)
        ).astype(BF16)
    start = query_columns + key_columns
    values_ref[...] = at_row(own_ref[:, start:] + other_ref[:, start:]).astype(BF16)


def attend_kernel(
    stretch_rows, arrived_ref, q_ref, keys_ref, values_ref, cos_ref, sin_ref, bias_ref, out_ref
):
    key_heads = q_ref.shape[0]
    local_keys = cos_ref.shape[0]
    scale = 1.0 / math.sqrt(HEAD_WIDTH)
    cosine = cos_ref[...]
    sine = sin_ref[...]
    bias = bias_ref[...]
    for head in range(key_heads):
        cols = slice(head * HEAD_WIDTH, (head + 1) * HEAD_WIDTH)
        keys = arrived_ref[:, :stretch_rows, cols].reshape(local_keys, HEAD_WIDTH)
        values = arrived_ref[:, stretch_rows:, cols].reshape(local_keys, HEAD_WIDTH)
        keys = rotated(keys.astype(F32), cosine, sine).astype(BF16)
        keys = jnp.concatenate([keys, keys_ref[:, cols]], axis=0)
        values = jnp.concatenate([values, values_ref[:, cols]], axis=0)
        scores = lax.dot_general(
            keys, q_ref[head], (((1,), (1,)), ((), ())), preferred_element_type=F32
        )
        scores = scores * scale + bias
        peak = jnp.max(scores, axis=0, keepdims=True)
        probs = jnp.exp(scores - peak)
        total = jnp.sum(probs, axis=0, keepdims=True)
        out_ref[cols, :] = lax.dot_general(
            values, probs.astype(BF16), (((0,), (0,)), ((), ())), preferred_element_type=F32
        )
        base = key_heads * HEAD_WIDTH
        out_ref[base + head : base + head + 1, :] = peak
        out_ref[base + key_heads + head : base + key_heads + head + 1, :] = total


def output_kernel(step, key_heads, own_ref, other_ref, w_ref, keep_ref, send_ref, w, attended, sems):
    copies = []
    for i, start in enumerate(range(0, w_ref.shape[1], step)):
        cols = pl.ds(start, step)
        copy = pltpu.make_async_copy(w_ref.at[:, cols], w.at[:, cols], sems.at[i])
        copy.start()
        copies.append(copy)
    token_total = attended.shape[0]
    group = own_ref.shape[1] // token_total
    base = key_heads * HEAD_WIDTH
    for head in range(key_heads):
        rows = slice(head * HEAD_WIDTH, (head + 1) * HEAD_WIDTH)
        at_peak = slice(base + head, base + head + 1)
        at_total = slice(base + key_heads + head, base + key_heads + head + 1)
        peak = jnp.maximum(own_ref[at_peak, :], other_ref[at_peak, :])
        own_scale = jnp.exp(own_ref[at_peak, :] - peak)
        other_scale = jnp.exp(other_ref[at_peak, :] - peak)
        total = own_ref[at_total, :] * own_scale + other_ref[at_total, :] * other_scale
        weighted = own_ref[rows, :] * own_scale + other_ref[rows, :] * other_scale
        result = jnp.transpose(weighted / total).astype(BF16)
        for j in range(group):
            start = (head * group + j) * HEAD_WIDTH
            attended[:, start : start + HEAD_WIDTH] = result[
                j * token_total : (j + 1) * token_total
            ]
    tokens = attended[...]
    share = keep_ref.shape[0]
    first = lax.axis_index("col") == 0
    for start, copy in zip(range(0, w_ref.shape[1], step), copies):
        copy.wait()
        cols = slice(start, start + step)
        part = jnp.dot(tokens, w[:, cols], preferred_element_type=F32)
        keep_ref[:, cols] = jnp.where(first, part[:share], part[share:])
        send_ref[:, cols] = jnp.where(first, part[share:], part[:share]).astype(BF16)


def params(mib):
    return pltpu.CompilerParams(vmem_limit_bytes=mib * MIB)


def on_device(
    hidden,
    w_query,
    key_weight,
    value_weight,
    w_out,
    kv_store,
    stretch_offset,
    tile_stretch,
    slot_count,
    recomp_pos,
):
    slot_total = lax.axis_size("slot")
    row_total = lax.axis_size("row")
    tiles, _, stretch_len, key_columns = kv_store.shape
    slot_tiles = tile_stretch.shape[1]
    ranks = slot_tiles // (slot_total * row_total)
    width = hidden.shape[2]
    token_total = hidden.shape[1]
    query_columns = w_query.shape[1]
    key_heads = key_columns // HEAD_WIDTH
    group = query_columns // key_columns
    query_rows = group * token_total
    per_slot = ranks * 2 * stretch_len
    local_keys = tiles * stretch_len
    share = token_total // row_total
    all_keys = local_keys + share
    swap = [(0, 1), (1, 0)]

    freq = np.arange(HEAD_WIDTH // 2, dtype=np.float64)
    freq = (ROPE_BASE ** (-2.0 * freq / HEAD_WIDTH)).astype(np.float32)
    freq = jnp.asarray(np.concatenate([freq, freq])[None, :])

    outgoing = pl.pallas_call(
        functools.partial(pack_kernel, tiles, ranks, stretch_len),
        out_shape=jax.ShapeDtypeStruct((slot_total * per_slot, key_columns), BF16),
        in_specs=[VMEM, VMEM],
        out_specs=VMEM,
        compiler_params=params(32),
        name="pack",
    )(tile_stretch, kv_store.reshape(tiles * 2 * stretch_len, key_columns))
    outgoing = outgoing.reshape(slot_total, per_slot, key_columns)
    arrived = lax.all_to_all(outgoing, "slot", split_axis=0, concat_axis=0, tiled=True)

    step = key_columns
    projected = pl.pallas_call(
        functools.partial(project_kernel, step),
        out_shape=jax.ShapeDtypeStruct((token_total, query_columns + 2 * key_columns), F32),
        in_specs=[VMEM, ANY, ANY, ANY],
        out_specs=VMEM,
        scratch_shapes=[
            pltpu.VMEM((width, query_columns), BF16),
            pltpu.VMEM((width, key_columns), BF16),
            pltpu.VMEM((width, key_columns), BF16),
            pltpu.SemaphoreType.DMA((query_columns // step + 2,)),
        ],
        compiler_params=params(32),
        name="project",
    )(hidden[0], w_query, key_weight, value_weight)
    projected_other = lax.ppermute(projected, "row", swap)

    queries, fresh_keys, new_values, cosine, sine, bias = pl.pallas_call(
        functools.partial(prepare_kernel, tiles, ranks, stretch_len, row_total),
        out_shape=(
            jax.ShapeDtypeStruct((key_heads, query_rows, HEAD_WIDTH), BF16),
            jax.ShapeDtypeStruct((share, key_columns), BF16),
            jax.ShapeDtypeStruct((share, key_columns), BF16),
            jax.ShapeDtypeStruct((local_keys, HEAD_WIDTH), F32),
            jax.ShapeDtypeStruct((local_keys, HEAD_WIDTH), F32),
            jax.ShapeDtypeStruct((all_keys, query_rows), F32),
        ),
        in_specs=[VMEM, VMEM, VMEM, VMEM, SMEM, VMEM, VMEM],
        out_specs=(VMEM,) * 6,
        compiler_params=params(32),
        name="prepare",
    )(
        projected,
        projected_other,
        tile_stretch,
        stretch_offset.reshape(-1, 128),
        slot_count,
        recomp_pos,
        freq,
    )

    partial = pl.pallas_call(
        functools.partial(attend_kernel, ranks * stretch_len),
        out_shape=jax.ShapeDtypeStruct((key_heads * HEAD_WIDTH + 2 * key_heads, query_rows), F32),
        in_specs=[VMEM] * 7,
        out_specs=VMEM,
        compiler_params=params(48),
        name="attend",
    )(arrived, queries, fresh_keys, new_values, cosine, sine, bias)
    partial_other = lax.ppermute(partial, "row", swap)

    out_columns = w_out.shape[1]
    out_share = token_total // lax.axis_size("col")
    keep, send = pl.pallas_call(
        functools.partial(output_kernel, step, key_heads),
        out_shape=(
            jax.ShapeDtypeStruct((out_share, out_columns), F32),
            jax.ShapeDtypeStruct((out_share, out_columns), BF16),
        ),
        in_specs=[VMEM, VMEM, ANY],
        out_specs=(VMEM, VMEM),
        scratch_shapes=[
            pltpu.VMEM(w_out.shape, BF16),
            pltpu.VMEM((token_total, query_columns), BF16),
            pltpu.SemaphoreType.DMA((out_columns // step,)),
        ],
        compiler_params=params(32),
        name="output",
    )(partial, partial_other, w_out)
    received = lax.ppermute(send, "col", swap)
    return (keep + received.astype(F32)).astype(BF16)[None]


def solution(mesh):
    return jax.shard_map(
        on_device,
        mesh=mesh,
        in_specs=(
            P("slot", None, "row"),
            P("row", "col"),
            P("row", "col"),
            P("row", "col"),
            P("col", "row"),
            P(("slot", "row"), None, None, "col"),
            P(),
            P(),
            P(),
            P("slot", None),
        ),
        out_specs=P("slot", "col", "row"),
        check_vma=False,
    )
```

```python
import functools
import math

import jax
import jax.numpy as jnp
import numpy as np
from jax import lax
from jax.experimental import pallas as pl
from jax.experimental.pallas import tpu as pltpu
from jax.sharding import PartitionSpec as P

HEAD_WIDTH = 128
NEGATIVE = -1e30
ROPE_BASE = 500000.0
MIB = 1024 * 1024
FAR = 1 << 28
F32 = jnp.float32
BF16 = jnp.bfloat16
VMEM = pl.BlockSpec(memory_space=pltpu.VMEM)
ANY = pl.BlockSpec(memory_space=pl.ANY)
HBM = pl.BlockSpec(memory_space=pltpu.HBM)
SMEM = pl.BlockSpec(memory_space=pltpu.SMEM)


def block_bits(place, slots):
    return (slots - place) & (slots - 1)


def iota(shape, dim):
    return lax.broadcasted_iota(jnp.int32, shape, dim)


def divide(value, by):
    if by & (by - 1) == 0:
        shift = by.bit_length() - 1
        return lax.shift_right_logical(value, jnp.full_like(value, shift)), value & (by - 1)
    quotient = jnp.floor((value.astype(F32) + 0.5) * (1.0 / by)).astype(jnp.int32)
    return quotient, value - quotient * by


def earlier_count(flags):
    n = flags.shape[1]
    before = (iota((n, n), 0) < iota((n, n), 1)).astype(BF16)
    return jnp.dot(flags.astype(BF16), before, preferred_element_type=F32)


def pack_kernel(tiles, ranks, stretch_len, stretches_hbm, store_hbm, *refs):
    *outs, stretches_ref, store_ref, ids_ref, sems = refs
    get_store = pltpu.make_async_copy(store_hbm, store_ref, sems.at[0])
    get_stretches = pltpu.make_async_copy(stretches_hbm, stretches_ref, sems.at[1])
    get_stretches.start()
    get_store.start()
    slot = lax.axis_index("slot")
    own = slot * lax.axis_size("row") + lax.axis_index("row")
    slots, slot_tiles = stretches_ref.shape
    per_slot = ranks * 2 * stretch_len
    rows = slots * per_slot
    part, token = divide(iota((rows, 128), 0), stretch_len)
    part, rank_of_row = divide(part, ranks)
    kind = part & 1
    rank_here = iota((rows, 128), 1) == rank_of_row
    within = (kind * stretch_len + token)[:, :1]
    get_stretches.wait()
    owner, local = divide(stretches_ref[...], tiles)
    mine = (owner == own).astype(F32)
    rank = earlier_count(mine)
    lane = iota((slots, 128), 1)
    ids = jnp.zeros((slots, 128), F32)
    for k in range(ranks):
        picked = jnp.where(rank == k, mine * local.astype(F32), 0.0)
        ids = jnp.where(lane == k, jnp.sum(picked, axis=1, keepdims=True), ids)
    ids_ref[...] = ids
    ids = jnp.concatenate(
        [
            jnp.broadcast_to(ids_ref[pl.ds(slot ^ k, 1), :], (per_slot, 128))
            for k in range(slots)
        ],
        axis=0,
    )
    stretch = jnp.sum(jnp.where(rank_here, ids, 0.0), axis=1, keepdims=True).astype(jnp.int32)
    source = stretch * (2 * stretch_len) + within
    store_rows = tiles * 2 * stretch_len
    pick = (iota((rows, store_rows), 1) == source).astype(F32).astype(BF16)
    get_store.wait()
    picked = jnp.dot(pick, store_ref[...], preferred_element_type=F32).astype(BF16)
    for k in range(slots):
        outs[k][...] = picked[k * per_slot : (k + 1) * per_slot]


def fetch(pieces, sems):
    copies = [pltpu.make_async_copy(a, b, sems.at[i]) for i, (a, b) in enumerate(pieces)]
    for copy in copies:
        copy.start()
    return copies


def column_pieces(source, target, step):
    return [
        (source.at[:, pl.ds(start, step)], target.at[:, pl.ds(start, step)])
        for start in range(0, source.shape[1], step)
    ]


def project_kernel(step, hidden_ref, wq_ref, wk_ref, wv_ref, out_ref):
    tokens = hidden_ref[...]
    base = 0
    for weight_ref in (wq_ref, wk_ref, wv_ref):
        for start in range(0, weight_ref.shape[1], step):
            out_ref[:, base : base + step] = jnp.dot(
                tokens, weight_ref[:, start : start + step], preferred_element_type=F32
            )
            base += step


def angle_tables(shift, freq):
    angle = shift.astype(F32) * freq
    low = iota(angle.shape, 1) < HEAD_WIDTH // 2
    sine = jnp.sin(angle)
    return jnp.cos(angle), jnp.where(low, -sine, sine)


def rotated(vectors, cosine, sine):
    return vectors * cosine + pltpu.roll(vectors, HEAD_WIDTH // 2, 1) * sine


def tables_kernel(
    tiles,
    ranks,
    stretch_len,
    row_total,
    stretches_ref,
    offsets_ref,
    counts_ref,
    positions_ref,
    freq_ref,
    cos_ref,
    sin_ref,
    bias_ref,
    token_cos_ref,
    token_sin_ref,
):
    slot = lax.axis_index("slot")
    row = lax.axis_index("row")
    freq = freq_ref[...]
    count = counts_ref[slot]
    arriving = tiles
    slot_tiles = stretches_ref.shape[1]
    stretches = stretches_ref[pl.ds(slot, 1), :]
    owner, _ = divide(stretches, tiles)
    from_slot, rank_wanted = divide(iota((arriving, slot_tiles), 0), ranks)
    from_slot = block_bits(from_slot, arriving // ranks) ^ slot
    match = (owner == from_slot * row_total + row).astype(F32)
    rank = earlier_count(match)
    picked = jnp.where(rank == rank_wanted.astype(F32), match, 0.0)
    tile = jnp.sum(picked * iota((arriving, slot_tiles), 1).astype(F32), axis=1, keepdims=True)
    stretch = jnp.sum(picked * stretches.astype(F32), axis=1, keepdims=True)
    tile = tile.astype(jnp.int32)
    stretch = stretch.astype(jnp.int32)
    page_count = offsets_ref.shape[0]
    page, lane = divide(stretch, 128)
    in_lane = (iota((arriving, 128), 1) == lane).astype(BF16)
    offsets = offsets_ref[...]
    upper, lower = divide(offsets, 64)
    nt = (((1,), (1,)), ((), ()))
    upper = lax.dot_general(in_lane, upper.astype(BF16), nt, preferred_element_type=F32)
    lower = lax.dot_general(in_lane, lower.astype(BF16), nt, preferred_element_type=F32)
    in_page = (iota((arriving, page_count), 1) == page).astype(F32)
    offset = jnp.sum(in_page * (upper * 64.0 + lower), axis=1, keepdims=True).astype(jnp.int32)
    cosine, sine = angle_tables(tile * stretch_len - offset, freq)
    local_keys = arriving * stretch_len
    spread = lambda x: jnp.broadcast_to(
        x[:, None, :], (arriving, stretch_len, x.shape[1])
    ).reshape(local_keys, x.shape[1])
    cos_ref[...] = spread(cosine)
    sin_ref[...] = spread(sine)
    token_total = positions_ref.shape[1]
    share = token_total // row_total
    positions = positions_ref[...]
    group = bias_ref.shape[1] // token_total
    query_positions = jnp.concatenate([positions] * group, axis=1)
    wide = jnp.broadcast_to(tile, (arriving, 128))
    _, token = divide(iota((local_keys, 1), 0), stretch_len)
    key_positions = spread(wide)[:, :1] * stretch_len + token
    redone = jnp.sum(
        (key_positions == positions).astype(F32), axis=1, keepdims=True
    )
    usable = jnp.logical_and(key_positions < count * stretch_len, redone == 0.0)
    key_positions = jnp.where(usable, key_positions, FAR)
    bias_ref[:local_keys, :] = jnp.where(key_positions <= query_positions, 0.0, NEGATIVE)
    square = iota((token_total, token_total), 0) == iota((token_total, token_total), 1)
    column = jnp.sum(
        jnp.where(square, positions.astype(F32), 0.0), axis=1, keepdims=True
    ).astype(jnp.int32)
    new_positions = of_row(column, row, share)
    new_usable = new_positions < count * stretch_len
    new_positions = jnp.where(new_usable, new_positions, FAR)
    bias_ref[local_keys:, :] = jnp.where(new_positions <= query_positions, 0.0, NEGATIVE)
    token_cos_ref[...], token_sin_ref[...] = angle_tables(column, freq)


def of_row(value, row, share):
    kept = value[:share]
    for r in range(1, value.shape[0] // share):
        kept = jnp.where(row == r, value[r * share : (r + 1) * share], kept)
    return kept


def attend_kernel(stretch_rows, *refs):
    *arrived, cos_ref, sin_ref, bias_ref, token_cos_ref, token_sin_ref, both_ref, out_ref = refs
    row = lax.axis_index("row")
    token_total = token_cos_ref.shape[0]
    share = bias_ref.shape[0] - cos_ref.shape[0]
    group = bias_ref.shape[1] // token_total
    key_columns = arrived[0].shape[1]
    key_heads = key_columns // HEAD_WIDTH
    query_columns = group * key_columns
    scale = 1.0 / math.sqrt(HEAD_WIDTH)
    cosine = cos_ref[...]
    sine = sin_ref[...]
    token_cosine = token_cos_ref[...]
    token_sine = token_sin_ref[...]
    bias = bias_ref[...]

    def projected(start):
        cols = slice(start, start + HEAD_WIDTH)
        return both_ref[0, :, cols] + both_ref[1, :, cols]

    for head in range(key_heads):
        at = head * HEAD_WIDTH
        cols = slice(at, at + HEAD_WIDTH)
        queries = jnp.concatenate(
            [
                rotated(projected((head * group + j) * HEAD_WIDTH), token_cosine, token_sine)
                for j in range(group)
            ],
            axis=0,
        ).astype(BF16)
        new_keys = rotated(projected(query_columns + at), token_cosine, token_sine)
        new_values = projected(query_columns + key_columns + at)
        keys = jnp.concatenate([ref[:stretch_rows, cols] for ref in arrived], axis=0)
        keys = rotated(keys.astype(F32), cosine, sine).astype(BF16)
        keys = jnp.concatenate([keys, of_row(new_keys, row, share).astype(BF16)], axis=0)
        values = [ref[stretch_rows:, cols] for ref in arrived]
        values = jnp.concatenate(values + [of_row(new_values, row, share).astype(BF16)], axis=0)
        scores = lax.dot_general(
            keys, queries, (((1,), (1,)), ((), ())), preferred_element_type=F32
        )
        scores = scores * scale + bias
        peak = jnp.max(scores, axis=0, keepdims=True)
        probs = jnp.exp(scores - peak)
        total = jnp.sum(probs, axis=0, keepdims=True)
        out_ref[cols, :] = lax.dot_general(
            values, probs.astype(BF16), (((0,), (0,)), ((), ())), preferred_element_type=F32
        )
        base = key_heads * HEAD_WIDTH
        out_ref[base + head : base + head + 1, :] = peak
        out_ref[base + key_heads + head : base + key_heads + head + 1, :] = total


def output_kernel(step, key_heads, own_ref, other_ref, w_ref, keep_ref, send_ref, attended):
    token_total = attended.shape[0]
    group = own_ref.shape[1] // token_total
    base = key_heads * HEAD_WIDTH
    for head in range(key_heads):
        rows = slice(head * HEAD_WIDTH, (head + 1) * HEAD_WIDTH)
        at_peak = slice(base + head, base + head + 1)
        at_total = slice(base + key_heads + head, base + key_heads + head + 1)
        peak = jnp.maximum(own_ref[at_peak, :], other_ref[at_peak, :])
        own_scale = jnp.exp(own_ref[at_peak, :] - peak)
        other_scale = jnp.exp(other_ref[at_peak, :] - peak)
        total = own_ref[at_total, :] * own_scale + other_ref[at_total, :] * other_scale
        weighted = own_ref[rows, :] * own_scale + other_ref[rows, :] * other_scale
        result = jnp.transpose(weighted / total).astype(BF16)
        for j in range(group):
            start = (head * group + j) * HEAD_WIDTH
            attended[:, start : start + HEAD_WIDTH] = result[
                j * token_total : (j + 1) * token_total
            ]
    tokens = attended[...]
    share = keep_ref.shape[0]
    first = lax.axis_index("col") == 0
    for start in range(0, w_ref.shape[1], step):
        cols = slice(start, start + step)
        part = jnp.dot(tokens, w_ref[:, cols], preferred_element_type=F32)
        keep_ref[:, cols] = jnp.where(first, part[:share], part[share:])
        send_ref[:, cols] = jnp.where(first, part[share:], part[:share]).astype(BF16)


def cost(us):
    return pl.CostEstimate(flops=us * 1_000_000_000, bytes_accessed=1000, transcendentals=0)


def in_hbm(value):
    return pltpu.with_memory_space_constraint(value, pltpu.HBM)


def params(mib):
    return pltpu.CompilerParams(vmem_limit_bytes=mib * MIB)


def on_device(
    hidden,
    w_query,
    key_weight,
    value_weight,
    w_out,
    kv_store,
    stretch_offset,
    tile_stretch,
    slot_count,
    recomp_pos,
):
    slot_total = lax.axis_size("slot")
    row_total = lax.axis_size("row")
    tiles, _, stretch_len, key_columns = kv_store.shape
    slot_tiles = tile_stretch.shape[1]
    ranks = slot_tiles // (slot_total * row_total)
    width = hidden.shape[2]
    token_total = hidden.shape[1]
    query_columns = w_query.shape[1]
    key_heads = key_columns // HEAD_WIDTH
    group = query_columns // key_columns
    query_rows = group * token_total
    per_slot = ranks * 2 * stretch_len
    local_keys = tiles * stretch_len
    share = token_total // row_total
    all_keys = local_keys + share
    swap = [(0, 1), (1, 0)]
    grant = 16 if slot_total <= 8 else 40

    freq = np.arange(HEAD_WIDTH // 2, dtype=np.float64)
    freq = (ROPE_BASE ** (-2.0 * freq / HEAD_WIDTH)).astype(np.float32)
    freq = jnp.asarray(np.concatenate([freq, freq])[None, :])

    store_shape = (tiles * 2 * stretch_len, key_columns)
    outgoing = pl.pallas_call(
        functools.partial(pack_kernel, tiles, ranks, stretch_len),
        out_shape=[jax.ShapeDtypeStruct((per_slot, key_columns), BF16)] * slot_total,
        in_specs=[HBM, HBM],
        out_specs=[VMEM] * slot_total,
        scratch_shapes=[
            pltpu.VMEM(tile_stretch.shape, jnp.int32),
            pltpu.VMEM(store_shape, BF16),
            pltpu.VMEM((slot_total, 128), F32),
            pltpu.SemaphoreType.DMA((2,)),
        ],
        compiler_params=params(grant),
        cost_estimate=cost(8),
        name="pack",
    )(in_hbm(tile_stretch), in_hbm(kv_store.reshape(store_shape)))
    step = key_columns
    order = [block_bits(place, slot_total) for place in range(slot_total)]
    blocks = [outgoing[0]] + [
        lax.ppermute(outgoing[k], "slot", [(i, i ^ k) for i in range(slot_total)])
        for k in order[1:]
    ]

    projected = pl.pallas_call(
        functools.partial(project_kernel, step),
        out_shape=jax.ShapeDtypeStruct((token_total, query_columns + 2 * key_columns), F32),
        in_specs=[VMEM] * 4,
        out_specs=VMEM,
        compiler_params=params(grant),
        cost_estimate=cost(0),
        name="project",
    )(hidden[0], w_query, key_weight, value_weight)
    both = lax.all_gather(projected, "row")

    tables = pl.pallas_call(
        functools.partial(tables_kernel, tiles, ranks, stretch_len, row_total),
        out_shape=(
            jax.ShapeDtypeStruct((local_keys, HEAD_WIDTH), F32),
            jax.ShapeDtypeStruct((local_keys, HEAD_WIDTH), F32),
            jax.ShapeDtypeStruct((all_keys, query_rows), F32),
            jax.ShapeDtypeStruct((token_total, HEAD_WIDTH), F32),
            jax.ShapeDtypeStruct((token_total, HEAD_WIDTH), F32),
        ),
        in_specs=[VMEM, VMEM, SMEM, VMEM, VMEM],
        out_specs=(VMEM,) * 5,
        compiler_params=params(grant),
        cost_estimate=cost(0),
        name="tables",
    )(tile_stretch, stretch_offset.reshape(-1, 128), slot_count, recomp_pos, freq)

    partial = pl.pallas_call(
        functools.partial(attend_kernel, ranks * stretch_len),
        out_shape=jax.ShapeDtypeStruct((key_heads * HEAD_WIDTH + 2 * key_heads, query_rows), F32),
        in_specs=[VMEM] * (slot_total + 6),
        out_specs=VMEM,
        compiler_params=params(grant),
        cost_estimate=cost(8),
        name="attend",
    )(*blocks, *tables, both)
    partial_other = lax.ppermute(partial, "row", swap)

    out_columns = w_out.shape[1]
    out_share = token_total // lax.axis_size("col")
    keep, send = pl.pallas_call(
        functools.partial(output_kernel, step, key_heads),
        out_shape=(
            jax.ShapeDtypeStruct((out_share, out_columns), F32),
            jax.ShapeDtypeStruct((out_share, out_columns), BF16),
        ),
        in_specs=[VMEM, VMEM, VMEM],
        out_specs=(VMEM, VMEM),
        scratch_shapes=[pltpu.VMEM((token_total, query_columns), BF16)],
        compiler_params=params(grant),
        name="output",
    )(partial, partial_other, w_out)
    received = lax.ppermute(send, "col", swap)
    return (keep + received.astype(F32)).astype(BF16)[None]


def solution(mesh):
    return jax.shard_map(
        on_device,
        mesh=mesh,
        in_specs=(
            P("slot", None, "row"),
            P("row", "col"),
            P("row", "col"),
            P("row", "col"),
            P("col", "row"),
            P(("slot", "row"), None, None, "col"),
            P(),
            P(),
            P(),
            P("slot", None),
        ),
        out_specs=P("slot", "col", "row"),
        check_vma=False,
    )
```

```python
import functools
import math

import jax
import jax.numpy as jnp
import numpy as np
from jax import lax
from jax.experimental import pallas as pl
from jax.experimental.pallas import tpu as pltpu
from jax.sharding import PartitionSpec as P

HEAD_WIDTH = 128
NEGATIVE = -1e30
ROPE_BASE = 500000.0
MIB = 1024 * 1024
FAR = 1 << 28
F32 = jnp.float32
BF16 = jnp.bfloat16
VMEM = pl.BlockSpec(memory_space=pltpu.VMEM)
ANY = pl.BlockSpec(memory_space=pl.ANY)
HBM = pl.BlockSpec(memory_space=pltpu.HBM)
SMEM = pl.BlockSpec(memory_space=pltpu.SMEM)


def far_bits(i, row, slots):
    return slots // 2 + i + (1 - row) * (slots // 4)


def iota(shape, dim):
    return lax.broadcasted_iota(jnp.int32, shape, dim)


def divide(value, by):
    if by & (by - 1) == 0:
        shift = by.bit_length() - 1
        return lax.shift_right_logical(value, jnp.full_like(value, shift)), value & (by - 1)
    quotient = jnp.floor((value.astype(F32) + 0.5) * (1.0 / by)).astype(jnp.int32)
    return quotient, value - quotient * by


def earlier_count(flags):
    n = flags.shape[1]
    before = (iota((n, n), 0) < iota((n, n), 1)).astype(BF16)
    return jnp.dot(flags.astype(BF16), before, preferred_element_type=F32)


def pack_kernel(tiles, ranks, stretch_len, stretches_hbm, store_hbm, *refs):
    *outs, give_ref, stretches_ref, store_ref, ids_ref, sems = refs
    get_store = pltpu.make_async_copy(store_hbm, store_ref, sems.at[0])
    get_stretches = pltpu.make_async_copy(stretches_hbm, stretches_ref, sems.at[1])
    get_stretches.start()
    get_store.start()
    slot = lax.axis_index("slot")
    row = lax.axis_index("row")
    own = slot * lax.axis_size("row") + row
    slots, slot_tiles = stretches_ref.shape
    per_slot = ranks * 2 * stretch_len
    rows = slots * per_slot
    part, token = divide(iota((rows, 128), 0), stretch_len)
    part, rank_of_row = divide(part, ranks)
    kind = part & 1
    rank_here = iota((rows, 128), 1) == rank_of_row
    within = (kind * stretch_len + token)[:, :1]
    get_stretches.wait()
    owner, local = divide(stretches_ref[...], tiles)
    mine = (owner == own).astype(F32)
    rank = earlier_count(mine)
    lane = iota((slots, 128), 1)
    ids = jnp.zeros((slots, 128), F32)
    for k in range(ranks):
        picked = jnp.where(rank == k, mine * local.astype(F32), 0.0)
        ids = jnp.where(lane == k, jnp.sum(picked, axis=1, keepdims=True), ids)
    ids_ref[...] = ids
    ids = jnp.concatenate(
        [
            jnp.broadcast_to(ids_ref[pl.ds(slot ^ k, 1), :], (per_slot, 128))
            for k in list(range(slots // 2))
            + [far_bits(i, r, slots) for r in (row, 1 - row) for i in range(slots // 4)]
        ],
        axis=0,
    )
    stretch = jnp.sum(jnp.where(rank_here, ids, 0.0), axis=1, keepdims=True).astype(jnp.int32)
    source = stretch * (2 * stretch_len) + within
    store_rows = tiles * 2 * stretch_len
    pick = (iota((rows, store_rows), 1) == source).astype(F32).astype(BF16)
    get_store.wait()
    picked = jnp.dot(pick, store_ref[...], preferred_element_type=F32).astype(BF16)
    for i, out_ref in enumerate(outs):
        out_ref[...] = picked[i * per_slot : (i + 1) * per_slot]
    give_ref[...] = picked[len(outs) * per_slot :]


def fetch(pieces, sems):
    copies = [pltpu.make_async_copy(a, b, sems.at[i]) for i, (a, b) in enumerate(pieces)]
    for copy in copies:
        copy.start()
    return copies


def column_pieces(source, target, step):
    return [
        (source.at[:, pl.ds(start, step)], target.at[:, pl.ds(start, step)])
        for start in range(0, source.shape[1], step)
    ]


def project_kernel(step, after_ref, hidden_ref, wq_ref, wk_ref, wv_ref, out_ref):
    tokens = hidden_ref[...]
    base = 0
    for weight_ref in (wq_ref, wk_ref, wv_ref):
        for start in range(0, weight_ref.shape[1], step):
            out_ref[:, base : base + step] = jnp.dot(
                tokens, weight_ref[:, start : start + step], preferred_element_type=F32
            )
            base += step


def angle_tables(shift, freq):
    angle = shift.astype(F32) * freq
    low = iota(angle.shape, 1) < HEAD_WIDTH // 2
    sine = jnp.sin(angle)
    return jnp.cos(angle), jnp.where(low, -sine, sine)


def rotated(vectors, cosine, sine):
    return vectors * cosine + pltpu.roll(vectors, HEAD_WIDTH // 2, 1) * sine


def tables_kernel(
    tiles,
    ranks,
    stretch_len,
    row_total,
    stretches_ref,
    offsets_ref,
    counts_ref,
    positions_ref,
    freq_ref,
    cos_ref,
    sin_ref,
    bias_ref,
    token_cos_ref,
    token_sin_ref,
):
    slot = lax.axis_index("slot")
    row = lax.axis_index("row")
    freq = freq_ref[...]
    count = counts_ref[slot]
    arriving = tiles
    slot_tiles = stretches_ref.shape[1]
    stretches = stretches_ref[pl.ds(slot, 1), :]
    owner, _ = divide(stretches, tiles)
    slots = arriving // ranks
    place, rank_wanted = divide(iota((arriving, slot_tiles), 0), ranks)
    near = place < slots // 2
    beyond = place - slots // 2
    from_slot = slot ^ jnp.where(near, place, far_bits(beyond >> 1, row, slots))
    from_row = row ^ jnp.where(near, 0, beyond & 1)
    match = (owner == from_slot * row_total + from_row).astype(F32)
    rank = earlier_count(match)
    picked = jnp.where(rank == rank_wanted.astype(F32), match, 0.0)
    tile = jnp.sum(picked * iota((arriving, slot_tiles), 1).astype(F32), axis=1, keepdims=True)
    stretch = jnp.sum(picked * stretches.astype(F32), axis=1, keepdims=True)
    tile = tile.astype(jnp.int32)
    stretch = stretch.astype(jnp.int32)
    page_count = offsets_ref.shape[0]
    page, lane = divide(stretch, 128)
    in_lane = (iota((arriving, 128), 1) == lane).astype(BF16)
    offsets = offsets_ref[...]
    upper, lower = divide(offsets, 64)
    nt = (((1,), (1,)), ((), ()))
    upper = lax.dot_general(in_lane, upper.astype(BF16), nt, preferred_element_type=F32)
    lower = lax.dot_general(in_lane, lower.astype(BF16), nt, preferred_element_type=F32)
    in_page = (iota((arriving, page_count), 1) == page).astype(F32)
    offset = jnp.sum(in_page * (upper * 64.0 + lower), axis=1, keepdims=True).astype(jnp.int32)
    cosine, sine = angle_tables(tile * stretch_len - offset, freq)
    local_keys = arriving * stretch_len
    spread = lambda x: jnp.broadcast_to(
        x[:, None, :], (arriving, stretch_len, x.shape[1])
    ).reshape(local_keys, x.shape[1])
    cos_ref[...] = spread(cosine)
    sin_ref[...] = spread(sine)
    token_total = positions_ref.shape[1]
    share = token_total // row_total
    positions = positions_ref[...]
    group = bias_ref.shape[1] // token_total
    query_positions = jnp.concatenate([positions] * group, axis=1)
    wide = jnp.broadcast_to(tile, (arriving, 128))
    _, token = divide(iota((local_keys, 1), 0), stretch_len)
    key_positions = spread(wide)[:, :1] * stretch_len + token
    redone = jnp.sum(
        (key_positions == positions).astype(F32), axis=1, keepdims=True
    )
    usable = jnp.logical_and(key_positions < count * stretch_len, redone == 0.0)
    key_positions = jnp.where(usable, key_positions, FAR)
    bias_ref[:local_keys, :] = jnp.where(key_positions <= query_positions, 0.0, NEGATIVE)
    square = iota((token_total, token_total), 0) == iota((token_total, token_total), 1)
    column = jnp.sum(
        jnp.where(square, positions.astype(F32), 0.0), axis=1, keepdims=True
    ).astype(jnp.int32)
    new_positions = of_row(column, row, share)
    new_usable = new_positions < count * stretch_len
    new_positions = jnp.where(new_usable, new_positions, FAR)
    bias_ref[local_keys:, :] = jnp.where(new_positions <= query_positions, 0.0, NEGATIVE)
    token_cos_ref[...], token_sin_ref[...] = angle_tables(column, freq)


def of_row(value, row, share):
    kept = value[:share]
    for r in range(1, value.shape[0] // share):
        kept = jnp.where(row == r, value[r * share : (r + 1) * share], kept)
    return kept


def attend_kernel(stretch_rows, far_count, *refs):
    *arrived, cos_ref, sin_ref, bias_ref, token_cos_ref, token_sin_ref, both_ref, out_ref = refs
    arrived = arrived[far_count:][::-1] + arrived[:far_count]
    parts = [
        (ref, at) for ref in arrived for at in range(0, ref.shape[0], 2 * stretch_rows)
    ]
    row = lax.axis_index("row")
    token_total = token_cos_ref.shape[0]
    share = bias_ref.shape[0] - cos_ref.shape[0]
    group = bias_ref.shape[1] // token_total
    key_columns = arrived[0].shape[1]
    key_heads = key_columns // HEAD_WIDTH
    query_columns = group * key_columns
    scale = 1.0 / math.sqrt(HEAD_WIDTH)
    cosine = cos_ref[...]
    sine = sin_ref[...]
    token_cosine = token_cos_ref[...]
    token_sine = token_sin_ref[...]
    bias = bias_ref[...]

    def projected(start):
        cols = slice(start, start + HEAD_WIDTH)
        return both_ref[0, :, cols] + both_ref[1, :, cols]

    for head in range(key_heads):
        at = head * HEAD_WIDTH
        cols = slice(at, at + HEAD_WIDTH)
        queries = jnp.concatenate(
            [
                rotated(projected((head * group + j) * HEAD_WIDTH), token_cosine, token_sine)
                for j in range(group)
            ],
            axis=0,
        ).astype(BF16)
        new_keys = rotated(projected(query_columns + at), token_cosine, token_sine)
        new_values = projected(query_columns + key_columns + at)
        keys = jnp.concatenate([ref[at : at + stretch_rows, cols] for ref, at in parts], axis=0)
        keys = rotated(keys.astype(F32), cosine, sine).astype(BF16)
        keys = jnp.concatenate([keys, of_row(new_keys, row, share).astype(BF16)], axis=0)
        values = [
            ref[at + stretch_rows : at + 2 * stretch_rows, cols] for ref, at in parts
        ]
        values = jnp.concatenate(values + [of_row(new_values, row, share).astype(BF16)], axis=0)
        scores = lax.dot_general(
            keys, queries, (((1,), (1,)), ((), ())), preferred_element_type=F32
        )
        scores = scores * scale + bias
        peak = jnp.max(scores, axis=0, keepdims=True)
        probs = jnp.exp(scores - peak)
        total = jnp.sum(probs, axis=0, keepdims=True)
        out_ref[cols, :] = lax.dot_general(
            values, probs.astype(BF16), (((0,), (0,)), ((), ())), preferred_element_type=F32
        )
        base = key_heads * HEAD_WIDTH
        out_ref[base + head : base + head + 1, :] = peak
        out_ref[base + key_heads + head : base + key_heads + head + 1, :] = total


def output_kernel(step, key_heads, own_ref, other_ref, w_ref, keep_ref, send_ref, attended):
    token_total = attended.shape[0]
    group = own_ref.shape[1] // token_total
    base = key_heads * HEAD_WIDTH
    for head in range(key_heads):
        rows = slice(head * HEAD_WIDTH, (head + 1) * HEAD_WIDTH)
        at_peak = slice(base + head, base + head + 1)
        at_total = slice(base + key_heads + head, base + key_heads + head + 1)
        peak = jnp.maximum(own_ref[at_peak, :], other_ref[at_peak, :])
        own_scale = jnp.exp(own_ref[at_peak, :] - peak)
        other_scale = jnp.exp(other_ref[at_peak, :] - peak)
        total = own_ref[at_total, :] * own_scale + other_ref[at_total, :] * other_scale
        weighted = own_ref[rows, :] * own_scale + other_ref[rows, :] * other_scale
        result = jnp.transpose(weighted / total).astype(BF16)
        for j in range(group):
            start = (head * group + j) * HEAD_WIDTH
            attended[:, start : start + HEAD_WIDTH] = result[
                j * token_total : (j + 1) * token_total
            ]
    tokens = attended[...]
    share = keep_ref.shape[0]
    first = lax.axis_index("col") == 0
    for start in range(0, w_ref.shape[1], step):
        cols = slice(start, start + step)
        part = jnp.dot(tokens, w_ref[:, cols], preferred_element_type=F32)
        keep_ref[:, cols] = jnp.where(first, part[:share], part[share:])
        send_ref[:, cols] = jnp.where(first, part[share:], part[:share]).astype(BF16)


def cost(us):
    return pl.CostEstimate(flops=us * 1_000_000_000, bytes_accessed=1000, transcendentals=0)


def in_hbm(value):
    return pltpu.with_memory_space_constraint(value, pltpu.HBM)


def merge_kernel(count, near_count, *refs):
    kept, given, outs = refs[:count], refs[count], refs[count + 1 + near_count :]
    rows = kept[0].shape[0]
    for i in range(count):
        outs[i][:rows] = kept[i][...]
        outs[i][rows:] = given[i * rows : (i + 1) * rows]


def merge(kept, given, near, grant):
    count, near_count = len(kept), len(near)
    block = kept[0]
    results = pl.pallas_call(
        functools.partial(merge_kernel, count, near_count),
        out_shape=[jax.ShapeDtypeStruct((2 * block.shape[0], block.shape[1]), BF16)] * count
        + [jax.ShapeDtypeStruct(block.shape, BF16)] * near_count,
        in_specs=[VMEM] * (count + 1) + [ANY] * near_count,
        out_specs=[VMEM] * count + [ANY] * near_count,
        input_output_aliases={count + 1 + i: count + i for i in range(near_count)},
        compiler_params=params(grant),
        cost_estimate=cost(0),
        name="merge",
    )(*kept, given, *near)
    return *results[:count], results[count:]


def params(mib):
    return pltpu.CompilerParams(vmem_limit_bytes=mib * MIB)


def on_device(
    hidden,
    w_query,
    key_weight,
    value_weight,
    w_out,
    kv_store,
    stretch_offset,
    tile_stretch,
    slot_count,
    recomp_pos,
):
    slot_total = lax.axis_size("slot")
    row_total = lax.axis_size("row")
    tiles, _, stretch_len, key_columns = kv_store.shape
    slot_tiles = tile_stretch.shape[1]
    ranks = slot_tiles // (slot_total * row_total)
    width = hidden.shape[2]
    token_total = hidden.shape[1]
    query_columns = w_query.shape[1]
    key_heads = key_columns // HEAD_WIDTH
    group = query_columns // key_columns
    query_rows = group * token_total
    per_slot = ranks * 2 * stretch_len
    local_keys = tiles * stretch_len
    share = token_total // row_total
    all_keys = local_keys + share
    swap = [(0, 1), (1, 0)]
    grant = 16 if slot_total <= 8 else 40

    freq = np.arange(HEAD_WIDTH // 2, dtype=np.float64)
    freq = (ROPE_BASE ** (-2.0 * freq / HEAD_WIDTH)).astype(np.float32)
    freq = jnp.asarray(np.concatenate([freq, freq])[None, :])

    store_shape = (tiles * 2 * stretch_len, key_columns)
    step = key_columns
    half, quarter = slot_total // 2, slot_total // 4
    block = jax.ShapeDtypeStruct((per_slot, key_columns), BF16)
    *outgoing, give = pl.pallas_call(
        functools.partial(pack_kernel, tiles, ranks, stretch_len),
        out_shape=[block] * (half + quarter)
        + [jax.ShapeDtypeStruct((quarter * per_slot, key_columns), BF16)],
        in_specs=[HBM, HBM],
        out_specs=[VMEM] * (half + quarter + 1),
        scratch_shapes=[
            pltpu.VMEM(tile_stretch.shape, jnp.int32),
            pltpu.VMEM(store_shape, BF16),
            pltpu.VMEM((slot_total, 128), F32),
            pltpu.SemaphoreType.DMA((2,)),
        ],
        compiler_params=params(grant),
        cost_estimate=cost(8),
        name="pack",
    )(in_hbm(tile_stretch), in_hbm(kv_store.reshape(store_shape)))
    given = lax.ppermute(give, "row", swap)
    *merged, near_blocks = merge(outgoing[half:], given, outgoing[1:half], grant)
    far = []
    for i in range(quarter):
        pairs = [
            (s * row_total + r, (s ^ far_bits(i, r, slot_total)) * row_total + r)
            for s in range(slot_total)
            for r in range(row_total)
        ]
        far.append(lax.ppermute(merged[i], ("slot", "row"), pairs))
    near = [outgoing[0]] + [
        lax.ppermute(near_blocks[k - 1], "slot", [(s, s ^ k) for s in range(slot_total)])
        for k in range(1, half)
    ]

    projected = pl.pallas_call(
        functools.partial(project_kernel, step),
        out_shape=jax.ShapeDtypeStruct((token_total, query_columns + 2 * key_columns), F32),
        in_specs=[ANY] + [VMEM] * 4,
        out_specs=VMEM,
        compiler_params=params(grant),
        cost_estimate=cost(0),
        name="project",
    )(merged[0], hidden[0], w_query, key_weight, value_weight)
    both = lax.all_gather(projected, "row")

    tables = pl.pallas_call(
        functools.partial(tables_kernel, tiles, ranks, stretch_len, row_total),
        out_shape=(
            jax.ShapeDtypeStruct((local_keys, HEAD_WIDTH), F32),
            jax.ShapeDtypeStruct((local_keys, HEAD_WIDTH), F32),
            jax.ShapeDtypeStruct((all_keys, query_rows), F32),
            jax.ShapeDtypeStruct((token_total, HEAD_WIDTH), F32),
            jax.ShapeDtypeStruct((token_total, HEAD_WIDTH), F32),
        ),
        in_specs=[VMEM, VMEM, SMEM, VMEM, VMEM],
        out_specs=(VMEM,) * 5,
        compiler_params=params(grant),
        cost_estimate=cost(0),
        name="tables",
    )(tile_stretch, stretch_offset.reshape(-1, 128), slot_count, recomp_pos, freq)

    partial = pl.pallas_call(
        functools.partial(attend_kernel, ranks * stretch_len, quarter),
        out_shape=jax.ShapeDtypeStruct((key_heads * HEAD_WIDTH + 2 * key_heads, query_rows), F32),
        in_specs=[VMEM] * (quarter + half + 6),
        out_specs=VMEM,
        compiler_params=params(grant),
        cost_estimate=cost(8),
        name="attend",
    )(*far, *reversed(near), *tables, both)
    partial_other = lax.ppermute(partial, "row", swap)

    out_columns = w_out.shape[1]
    out_share = token_total // lax.axis_size("col")
    keep, send = pl.pallas_call(
        functools.partial(output_kernel, step, key_heads),
        out_shape=(
            jax.ShapeDtypeStruct((out_share, out_columns), F32),
            jax.ShapeDtypeStruct((out_share, out_columns), BF16),
        ),
        in_specs=[VMEM, VMEM, VMEM],
        out_specs=(VMEM, VMEM),
        scratch_shapes=[pltpu.VMEM((token_total, query_columns), BF16)],
        compiler_params=params(grant),
        name="output",
    )(partial, partial_other, w_out)
    received = lax.ppermute(send, "col", swap)
    return (keep + received.astype(F32)).astype(BF16)[None]


def solution(mesh):
    return jax.shard_map(
        on_device,
        mesh=mesh,
        in_specs=(
            P("slot", None, "row"),
            P("row", "col"),
            P("row", "col"),
            P("row", "col"),
            P("col", "row"),
            P(("slot", "row"), None, None, "col"),
            P(),
            P(),
            P(),
            P("slot", None),
        ),
        out_specs=P("slot", "col", "row"),
        check_vma=False,
    )
```

```python
import functools
import math

import jax
import jax.numpy as jnp
import numpy as np
from jax import lax
from jax.experimental import pallas as pl
from jax.experimental.pallas import tpu as pltpu
from jax.sharding import PartitionSpec as P

HEAD_WIDTH = 128
NEGATIVE = -1e30
ROPE_BASE = 500000.0
MIB = 1024 * 1024
FAR = 1 << 28
F32 = jnp.float32
BF16 = jnp.bfloat16
VMEM = pl.BlockSpec(memory_space=pltpu.VMEM)
ANY = pl.BlockSpec(memory_space=pl.ANY)
HBM = pl.BlockSpec(memory_space=pltpu.HBM)
SMEM = pl.BlockSpec(memory_space=pltpu.SMEM)


def far_bits(i, row, slots):
    return slots // 2 + i + (1 - row) * (slots // 4)


def iota(shape, dim):
    return lax.broadcasted_iota(jnp.int32, shape, dim)


def divide(value, by):
    if by & (by - 1) == 0:
        shift = by.bit_length() - 1
        return lax.shift_right_logical(value, jnp.full_like(value, shift)), value & (by - 1)
    quotient = jnp.floor((value.astype(F32) + 0.5) * (1.0 / by)).astype(jnp.int32)
    return quotient, value - quotient * by


def earlier_count(flags):
    n = flags.shape[1]
    before = (iota((n, n), 0) < iota((n, n), 1)).astype(BF16)
    return jnp.dot(flags.astype(BF16), before, preferred_element_type=F32)


def pack_kernel(tiles, ranks, stretch_len, stretches_hbm, store_hbm, *refs):
    *outs, give_ref, stretches_ref, store_ref, ids_ref, sems = refs
    get_store = pltpu.make_async_copy(store_hbm, store_ref, sems.at[0])
    get_stretches = pltpu.make_async_copy(stretches_hbm, stretches_ref, sems.at[1])
    get_stretches.start()
    get_store.start()
    slot = lax.axis_index("slot")
    row = lax.axis_index("row")
    own = slot * lax.axis_size("row") + row
    slots, slot_tiles = stretches_ref.shape
    per_slot = ranks * 2 * stretch_len
    rows = slots * per_slot
    part, token = divide(iota((rows, 128), 0), stretch_len)
    part, rank_of_row = divide(part, ranks)
    kind = part & 1
    rank_here = iota((rows, 128), 1) == rank_of_row
    within = (kind * stretch_len + token)[:, :1]
    get_stretches.wait()
    owner, local = divide(stretches_ref[...], tiles)
    mine = (owner == own).astype(F32)
    rank = earlier_count(mine)
    lane = iota((slots, 128), 1)
    ids = jnp.zeros((slots, 128), F32)
    for k in range(ranks):
        picked = jnp.where(rank == k, mine * local.astype(F32), 0.0)
        ids = jnp.where(lane == k, jnp.sum(picked, axis=1, keepdims=True), ids)
    ids_ref[...] = ids
    ids = jnp.concatenate(
        [
            jnp.broadcast_to(ids_ref[pl.ds(slot ^ k, 1), :], (per_slot, 128))
            for k in list(range(slots // 2))
            + [far_bits(i, r, slots) for r in (row, 1 - row) for i in range(slots // 4)]
        ],
        axis=0,
    )
    stretch = jnp.sum(jnp.where(rank_here, ids, 0.0), axis=1, keepdims=True).astype(jnp.int32)
    source = stretch * (2 * stretch_len) + within
    store_rows = tiles * 2 * stretch_len
    pick = (iota((rows, store_rows), 1) == source).astype(F32).astype(BF16)
    get_store.wait()
    picked = jnp.dot(pick, store_ref[...], preferred_element_type=F32).astype(BF16)
    for i, out_ref in enumerate(outs):
        out_ref[...] = picked[i * per_slot : (i + 1) * per_slot]
    give_ref[...] = picked[len(outs) * per_slot :]


def fetch(pieces, sems):
    copies = [pltpu.make_async_copy(a, b, sems.at[i]) for i, (a, b) in enumerate(pieces)]
    for copy in copies:
        copy.start()
    return copies


def column_pieces(source, target, step):
    return [
        (source.at[:, pl.ds(start, step)], target.at[:, pl.ds(start, step)])
        for start in range(0, source.shape[1], step)
    ]


def project_kernel(step, after_ref, hidden_ref, wq_ref, wk_ref, wv_ref, out_ref):
    tokens = hidden_ref[...]
    base = 0
    for weight_ref in (wq_ref, wk_ref, wv_ref):
        for start in range(0, weight_ref.shape[1], step):
            out_ref[:, base : base + step] = jnp.dot(
                tokens, weight_ref[:, start : start + step], preferred_element_type=F32
            )
            base += step


def angle_tables(shift, freq):
    angle = shift.astype(F32) * freq
    low = iota(angle.shape, 1) < HEAD_WIDTH // 2
    sine = jnp.sin(angle)
    return jnp.cos(angle), jnp.where(low, -sine, sine)


def rotated(vectors, cosine, sine):
    return vectors * cosine + pltpu.roll(vectors, HEAD_WIDTH // 2, 1) * sine


def tables_kernel(
    tiles,
    ranks,
    stretch_len,
    row_total,
    stretches_ref,
    offsets_ref,
    counts_ref,
    positions_ref,
    freq_ref,
    cos_ref,
    sin_ref,
    bias_ref,
    token_cos_ref,
    token_sin_ref,
):
    slot = lax.axis_index("slot")
    row = lax.axis_index("row")
    freq = freq_ref[...]
    count = counts_ref[slot]
    arriving = tiles
    slot_tiles = stretches_ref.shape[1]
    stretches = stretches_ref[pl.ds(slot, 1), :]
    owner, _ = divide(stretches, tiles)
    slots = arriving // ranks
    place, rank_wanted = divide(iota((arriving, slot_tiles), 0), ranks)
    near = place < slots // 2
    beyond = place - slots // 2
    from_slot = slot ^ jnp.where(near, place, far_bits(beyond >> 1, row, slots))
    from_row = row ^ jnp.where(near, 0, beyond & 1)
    match = (owner == from_slot * row_total + from_row).astype(F32)
    rank = earlier_count(match)
    picked = jnp.where(rank == rank_wanted.astype(F32), match, 0.0)
    tile = jnp.sum(picked * iota((arriving, slot_tiles), 1).astype(F32), axis=1, keepdims=True)
    stretch = jnp.sum(picked * stretches.astype(F32), axis=1, keepdims=True)
    tile = tile.astype(jnp.int32)
    stretch = stretch.astype(jnp.int32)
    page_count = offsets_ref.shape[0]
    page, lane = divide(stretch, 128)
    in_lane = (iota((arriving, 128), 1) == lane).astype(BF16)
    offsets = offsets_ref[...]
    upper, lower = divide(offsets, 64)
    nt = (((1,), (1,)), ((), ()))
    upper = lax.dot_general(in_lane, upper.astype(BF16), nt, preferred_element_type=F32)
    lower = lax.dot_general(in_lane, lower.astype(BF16), nt, preferred_element_type=F32)
    in_page = (iota((arriving, page_count), 1) == page).astype(F32)
    offset = jnp.sum(in_page * (upper * 64.0 + lower), axis=1, keepdims=True).astype(jnp.int32)
    cosine, sine = angle_tables(tile * stretch_len - offset, freq)
    local_keys = arriving * stretch_len
    spread = lambda x: jnp.broadcast_to(
        x[:, None, :], (arriving, stretch_len, x.shape[1])
    ).reshape(local_keys, x.shape[1])
    cos_ref[...] = spread(cosine)
    sin_ref[...] = spread(sine)
    token_total = positions_ref.shape[1]
    share = token_total // row_total
    positions = positions_ref[...]
    group = bias_ref.shape[1] // token_total
    query_positions = jnp.concatenate([positions] * group, axis=1)
    wide = jnp.broadcast_to(tile, (arriving, 128))
    _, token = divide(iota((local_keys, 1), 0), stretch_len)
    key_positions = spread(wide)[:, :1] * stretch_len + token
    redone = jnp.sum(
        (key_positions == positions).astype(F32), axis=1, keepdims=True
    )
    usable = jnp.logical_and(key_positions < count * stretch_len, redone == 0.0)
    key_positions = jnp.where(usable, key_positions, FAR)
    bias_ref[:local_keys, :] = jnp.where(key_positions <= query_positions, 0.0, NEGATIVE)
    square = iota((token_total, token_total), 0) == iota((token_total, token_total), 1)
    column = jnp.sum(
        jnp.where(square, positions.astype(F32), 0.0), axis=1, keepdims=True
    ).astype(jnp.int32)
    new_positions = of_row(column, row, share)
    new_usable = new_positions < count * stretch_len
    new_positions = jnp.where(new_usable, new_positions, FAR)
    bias_ref[local_keys:, :] = jnp.where(new_positions <= query_positions, 0.0, NEGATIVE)
    token_cos_ref[...], token_sin_ref[...] = angle_tables(column, freq)


def of_row(value, row, share):
    kept = value[:share]
    for r in range(1, value.shape[0] // share):
        kept = jnp.where(row == r, value[r * share : (r + 1) * share], kept)
    return kept


def attend_kernel(stretch_rows, far_count, *refs):
    *arrived, cos_ref, sin_ref, bias_ref, token_cos_ref, token_sin_ref, both_ref, out_ref = refs
    arrived = arrived[far_count:][::-1] + arrived[:far_count]
    parts = [
        (ref, at) for ref in arrived for at in range(0, ref.shape[0], 2 * stretch_rows)
    ]
    row = lax.axis_index("row")
    token_total = token_cos_ref.shape[0]
    share = bias_ref.shape[0] - cos_ref.shape[0]
    group = bias_ref.shape[1] // token_total
    key_columns = arrived[0].shape[1]
    key_heads = key_columns // HEAD_WIDTH
    query_columns = group * key_columns
    scale = 1.0 / math.sqrt(HEAD_WIDTH)
    cosine = cos_ref[...]
    sine = sin_ref[...]
    token_cosine = token_cos_ref[...]
    token_sine = token_sin_ref[...]
    bias = bias_ref[...]

    def projected(start):
        cols = slice(start, start + HEAD_WIDTH)
        return both_ref[0, :, cols] + both_ref[1, :, cols]

    all_scores, all_values = [], []
    for head in range(key_heads):
        at = head * HEAD_WIDTH
        cols = slice(at, at + HEAD_WIDTH)
        queries = jnp.concatenate(
            [
                rotated(projected((head * group + j) * HEAD_WIDTH), token_cosine, token_sine)
                for j in range(group)
            ],
            axis=0,
        ).astype(BF16)
        new_keys = rotated(projected(query_columns + at), token_cosine, token_sine)
        new_values = projected(query_columns + key_columns + at)
        keys = jnp.concatenate([ref[at : at + stretch_rows, cols] for ref, at in parts], axis=0)
        keys = rotated(keys.astype(F32), cosine, sine).astype(BF16)
        keys = jnp.concatenate([keys, of_row(new_keys, row, share).astype(BF16)], axis=0)
        values = [
            ref[at + stretch_rows : at + 2 * stretch_rows, cols] for ref, at in parts
        ]
        all_values.append(
            jnp.concatenate(values + [of_row(new_values, row, share).astype(BF16)], axis=0)
        )
        all_scores.append(
            lax.dot_general(
                keys, queries, (((1,), (1,)), ((), ())), preferred_element_type=F32
            )
        )
    all_probs = []
    base = key_heads * HEAD_WIDTH
    for head, scores in enumerate(all_scores):
        scores = scores * scale + bias
        peak = jnp.max(scores, axis=0, keepdims=True)
        probs = jnp.exp(scores - peak)
        out_ref[base + head : base + head + 1, :] = peak
        out_ref[base + key_heads + head : base + key_heads + head + 1, :] = jnp.sum(
            probs, axis=0, keepdims=True
        )
        all_probs.append(probs.astype(BF16))
    for head in range(key_heads):
        out_ref[head * HEAD_WIDTH : (head + 1) * HEAD_WIDTH, :] = lax.dot_general(
            all_values[head], all_probs[head], (((0,), (0,)), ((), ())), preferred_element_type=F32
        )


def output_kernel(step, key_heads, own_ref, other_ref, w_ref, keep_ref, send_ref, attended):
    token_total = attended.shape[0]
    group = own_ref.shape[1] // token_total
    base = key_heads * HEAD_WIDTH
    for head in range(key_heads):
        rows = slice(head * HEAD_WIDTH, (head + 1) * HEAD_WIDTH)
        at_peak = slice(base + head, base + head + 1)
        at_total = slice(base + key_heads + head, base + key_heads + head + 1)
        peak = jnp.maximum(own_ref[at_peak, :], other_ref[at_peak, :])
        own_scale = jnp.exp(own_ref[at_peak, :] - peak)
        other_scale = jnp.exp(other_ref[at_peak, :] - peak)
        total = own_ref[at_total, :] * own_scale + other_ref[at_total, :] * other_scale
        weighted = own_ref[rows, :] * own_scale + other_ref[rows, :] * other_scale
        result = jnp.transpose(weighted / total).astype(BF16)
        for j in range(group):
            start = (head * group + j) * HEAD_WIDTH
            attended[:, start : start + HEAD_WIDTH] = result[
                j * token_total : (j + 1) * token_total
            ]
    tokens = attended[...]
    share = keep_ref.shape[0]
    first = lax.axis_index("col") == 0
    for start in range(0, w_ref.shape[1], step):
        cols = slice(start, start + step)
        part = jnp.dot(tokens, w_ref[:, cols], preferred_element_type=F32)
        keep_ref[:, cols] = jnp.where(first, part[:share], part[share:])
        send_ref[:, cols] = jnp.where(first, part[share:], part[:share]).astype(BF16)


def cost(us):
    return pl.CostEstimate(flops=us * 1_000_000_000, bytes_accessed=1000, transcendentals=0)


def in_hbm(value):
    return pltpu.with_memory_space_constraint(value, pltpu.HBM)


def merge_kernel(count, near_count, *refs):
    kept, given, outs = refs[:count], refs[count], refs[count + 1 + near_count :]
    rows = kept[0].shape[0]
    for i in range(count):
        outs[i][:rows] = kept[i][...]
        outs[i][rows:] = given[i * rows : (i + 1) * rows]


def merge(kept, given, near, grant):
    count, near_count = len(kept), len(near)
    block = kept[0]
    results = pl.pallas_call(
        functools.partial(merge_kernel, count, near_count),
        out_shape=[jax.ShapeDtypeStruct((2 * block.shape[0], block.shape[1]), BF16)] * count
        + [jax.ShapeDtypeStruct(block.shape, BF16)] * near_count,
        in_specs=[VMEM] * (count + 1) + [ANY] * near_count,
        out_specs=[VMEM] * count + [ANY] * near_count,
        input_output_aliases={count + 1 + i: count + i for i in range(near_count)},
        compiler_params=params(grant),
        cost_estimate=cost(0),
        name="merge",
    )(*kept, given, *near)
    return *results[:count], results[count:]


def params(mib):
    return pltpu.CompilerParams(vmem_limit_bytes=mib * MIB)


def on_device(
    hidden,
    w_query,
    key_weight,
    value_weight,
    w_out,
    kv_store,
    stretch_offset,
    tile_stretch,
    slot_count,
    recomp_pos,
):
    slot_total = lax.axis_size("slot")
    row_total = lax.axis_size("row")
    tiles, _, stretch_len, key_columns = kv_store.shape
    slot_tiles = tile_stretch.shape[1]
    ranks = slot_tiles // (slot_total * row_total)
    width = hidden.shape[2]
    token_total = hidden.shape[1]
    query_columns = w_query.shape[1]
    key_heads = key_columns // HEAD_WIDTH
    group = query_columns // key_columns
    query_rows = group * token_total
    per_slot = ranks * 2 * stretch_len
    local_keys = tiles * stretch_len
    share = token_total // row_total
    all_keys = local_keys + share
    swap = [(0, 1), (1, 0)]
    grant = 16 if slot_total <= 8 else 40

    freq = np.arange(HEAD_WIDTH // 2, dtype=np.float64)
    freq = (ROPE_BASE ** (-2.0 * freq / HEAD_WIDTH)).astype(np.float32)
    freq = jnp.asarray(np.concatenate([freq, freq])[None, :])

    store_shape = (tiles * 2 * stretch_len, key_columns)
    step = key_columns
    half, quarter = slot_total // 2, slot_total // 4
    block = jax.ShapeDtypeStruct((per_slot, key_columns), BF16)
    *outgoing, give = pl.pallas_call(
        functools.partial(pack_kernel, tiles, ranks, stretch_len),
        out_shape=[block] * (half + quarter)
        + [jax.ShapeDtypeStruct((quarter * per_slot, key_columns), BF16)],
        in_specs=[HBM, HBM],
        out_specs=[VMEM] * (half + quarter + 1),
        scratch_shapes=[
            pltpu.VMEM(tile_stretch.shape, jnp.int32),
            pltpu.VMEM(store_shape, BF16),
            pltpu.VMEM((slot_total, 128), F32),
            pltpu.SemaphoreType.DMA((2,)),
        ],
        compiler_params=params(grant),
        cost_estimate=cost(8),
        name="pack",
    )(in_hbm(tile_stretch), in_hbm(kv_store.reshape(store_shape)))
    given = lax.ppermute(give, "row", swap)
    *merged, near_blocks = merge(outgoing[half:], given, outgoing[1:half], grant)
    far = []
    for i in range(quarter):
        pairs = [
            (s * row_total + r, (s ^ far_bits(i, r, slot_total)) * row_total + r)
            for s in range(slot_total)
            for r in range(row_total)
        ]
        far.append(lax.ppermute(merged[i], ("slot", "row"), pairs))
    near = [outgoing[0]] + [
        lax.ppermute(near_blocks[k - 1], "slot", [(s, s ^ k) for s in range(slot_total)])
        for k in range(1, half)
    ]

    projected = pl.pallas_call(
        functools.partial(project_kernel, step),
        out_shape=jax.ShapeDtypeStruct((token_total, query_columns + 2 * key_columns), F32),
        in_specs=[ANY] + [VMEM] * 4,
        out_specs=VMEM,
        compiler_params=params(grant),
        cost_estimate=cost(0),
        name="project",
    )(merged[0], hidden[0], w_query, key_weight, value_weight)
    both = lax.all_gather(projected, "row")

    tables = pl.pallas_call(
        functools.partial(tables_kernel, tiles, ranks, stretch_len, row_total),
        out_shape=(
            jax.ShapeDtypeStruct((local_keys, HEAD_WIDTH), F32),
            jax.ShapeDtypeStruct((local_keys, HEAD_WIDTH), F32),
            jax.ShapeDtypeStruct((all_keys, query_rows), F32),
            jax.ShapeDtypeStruct((token_total, HEAD_WIDTH), F32),
            jax.ShapeDtypeStruct((token_total, HEAD_WIDTH), F32),
        ),
        in_specs=[VMEM, VMEM, SMEM, VMEM, VMEM],
        out_specs=(VMEM,) * 5,
        compiler_params=params(grant),
        cost_estimate=cost(0),
        name="tables",
    )(tile_stretch, stretch_offset.reshape(-1, 128), slot_count, recomp_pos, freq)

    partial = pl.pallas_call(
        functools.partial(attend_kernel, ranks * stretch_len, quarter),
        out_shape=jax.ShapeDtypeStruct((key_heads * HEAD_WIDTH + 2 * key_heads, query_rows), F32),
        in_specs=[VMEM] * (quarter + half + 6),
        out_specs=VMEM,
        compiler_params=params(grant),
        cost_estimate=cost(8),
        name="attend",
    )(*far, *reversed(near), *tables, both)
    partial_other = lax.ppermute(partial, "row", swap)

    out_columns = w_out.shape[1]
    out_share = token_total // lax.axis_size("col")
    keep, send = pl.pallas_call(
        functools.partial(output_kernel, step, key_heads),
        out_shape=(
            jax.ShapeDtypeStruct((out_share, out_columns), F32),
            jax.ShapeDtypeStruct((out_share, out_columns), BF16),
        ),
        in_specs=[VMEM, VMEM, VMEM],
        out_specs=(VMEM, VMEM),
        scratch_shapes=[pltpu.VMEM((token_total, query_columns), BF16)],
        compiler_params=params(grant),
        name="output",
    )(partial, partial_other, w_out)
    received = lax.ppermute(send, "col", swap)
    return (keep + received.astype(F32)).astype(BF16)[None]


def solution(mesh):
    return jax.shard_map(
        on_device,
        mesh=mesh,
        in_specs=(
            P("slot", None, "row"),
            P("row", "col"),
            P("row", "col"),
            P("row", "col"),
            P("col", "row"),
            P(("slot", "row"), None, None, "col"),
            P(),
            P(),
            P(),
            P("slot", None),
        ),
        out_specs=P("slot", "col", "row"),
        check_vma=False,
    )
```

```python
import functools
import math

import jax
import jax.numpy as jnp
import numpy as np
from jax import lax
from jax.experimental import pallas as pl
from jax.experimental.pallas import tpu as pltpu
from jax.sharding import PartitionSpec as P

HEAD_WIDTH = 128
NEGATIVE = -1e30
ROPE_BASE = 500000.0
MIB = 1024 * 1024
FAR = 1 << 28
F32 = jnp.float32
BF16 = jnp.bfloat16
VMEM = pl.BlockSpec(memory_space=pltpu.VMEM)
ANY = pl.BlockSpec(memory_space=pl.ANY)
HBM = pl.BlockSpec(memory_space=pltpu.HBM)
SMEM = pl.BlockSpec(memory_space=pltpu.SMEM)


def exchanges(slots):
    if slots == 8:
        return [4, 6, 3], [(7, 5), (2, 1)]
    return [1], [(k, k - 1) for k in range(slots - 1, 1, -2)]


def for_row(pair, row):
    return pair[1] + (1 - row) * (pair[0] - pair[1])


def arrivals(slots):
    direct, shared = exchanges(slots)
    blocks = [(k, k, 0) for k in direct]
    blocks += [(*pair, flip) for pair in shared for flip in (0, 1)]
    return blocks + [(0, 0, 0)]


def iota(shape, dim):
    return lax.broadcasted_iota(jnp.int32, shape, dim)


def divide(value, by):
    if by & (by - 1) == 0:
        shift = by.bit_length() - 1
        return lax.shift_right_logical(value, jnp.full_like(value, shift)), value & (by - 1)
    quotient = jnp.floor((value.astype(F32) + 0.5) * (1.0 / by)).astype(jnp.int32)
    return quotient, value - quotient * by


def earlier_count(flags):
    n = flags.shape[1]
    before = (iota((n, n), 0) < iota((n, n), 1)).astype(BF16)
    return jnp.dot(flags.astype(BF16), before, preferred_element_type=F32)


def pack_kernel(tiles, ranks, stretch_len, stretches_hbm, store_hbm, *refs):
    *outs, give_ref, stretches_ref, store_ref, ids_ref, sems = refs
    get_store = pltpu.make_async_copy(store_hbm, store_ref, sems.at[0])
    get_stretches = pltpu.make_async_copy(stretches_hbm, stretches_ref, sems.at[1])
    get_stretches.start()
    get_store.start()
    slot = lax.axis_index("slot")
    row = lax.axis_index("row")
    own = slot * lax.axis_size("row") + row
    slots, slot_tiles = stretches_ref.shape
    per_slot = ranks * 2 * stretch_len
    rows = slots * per_slot
    part, token = divide(iota((rows, 128), 0), stretch_len)
    part, rank_of_row = divide(part, ranks)
    kind = part & 1
    rank_here = iota((rows, 128), 1) == rank_of_row
    within = (kind * stretch_len + token)[:, :1]
    get_stretches.wait()
    owner, local = divide(stretches_ref[...], tiles)
    mine = (owner == own).astype(F32)
    rank = earlier_count(mine)
    lane = iota((slots, 128), 1)
    ids = jnp.zeros((slots, 128), F32)
    for k in range(ranks):
        picked = jnp.where(rank == k, mine * local.astype(F32), 0.0)
        ids = jnp.where(lane == k, jnp.sum(picked, axis=1, keepdims=True), ids)
    ids_ref[...] = ids
    direct, shared = exchanges(slots)
    ids = jnp.concatenate(
        [
            jnp.broadcast_to(ids_ref[pl.ds(slot ^ k, 1), :], (per_slot, 128))
            for k in direct + [0] + [for_row(pair, r) for r in (row, 1 - row) for pair in shared]
        ],
        axis=0,
    )
    stretch = jnp.sum(jnp.where(rank_here, ids, 0.0), axis=1, keepdims=True).astype(jnp.int32)
    source = stretch * (2 * stretch_len) + within
    store_rows = tiles * 2 * stretch_len
    pick = (iota((rows, store_rows), 1) == source).astype(F32).astype(BF16)
    get_store.wait()
    picked = jnp.dot(pick, store_ref[...], preferred_element_type=F32).astype(BF16)
    for i, out_ref in enumerate(outs):
        out_ref[...] = picked[i * per_slot : (i + 1) * per_slot]
    give_ref[...] = picked[len(outs) * per_slot :]


def fetch(pieces, sems):
    copies = [pltpu.make_async_copy(a, b, sems.at[i]) for i, (a, b) in enumerate(pieces)]
    for copy in copies:
        copy.start()
    return copies


def column_pieces(source, target, step):
    return [
        (source.at[:, pl.ds(start, step)], target.at[:, pl.ds(start, step)])
        for start in range(0, source.shape[1], step)
    ]


def project_kernel(step, after_ref, hidden_ref, wq_ref, wk_ref, wv_ref, out_ref):
    tokens = hidden_ref[...]
    base = 0
    for weight_ref in (wq_ref, wk_ref, wv_ref):
        for start in range(0, weight_ref.shape[1], step):
            out_ref[:, base : base + step] = jnp.dot(
                tokens, weight_ref[:, start : start + step], preferred_element_type=F32
            )
            base += step


def sine_cosine(angle):
    turns = jnp.floor(angle * (2.0 / math.pi) + 0.5)
    rest = angle - turns * 1.5703125
    rest = rest - turns * 4.837512969970703125e-4
    rest = rest - turns * 7.54978995489188216e-8
    square = rest * rest
    sine = (-1.9515295891e-4 * square + 8.3321608736e-3) * square - 1.6666654611e-1
    sine = sine * square * rest + rest
    cosine = (2.443315711809948e-5 * square - 1.388731625493765e-3) * square
    cosine = (cosine + 4.166664568298827e-2) * square * square - 0.5 * square + 1.0
    quarter = turns.astype(jnp.int32) & 3
    odd = (quarter & 1) == 1
    sine, cosine = jnp.where(odd, cosine, sine), jnp.where(odd, sine, cosine)
    sine = jnp.where(quarter >= 2, -sine, sine)
    cosine = jnp.where(jnp.logical_or(quarter == 1, quarter == 2), -cosine, cosine)
    return sine, cosine


def angle_tables(shift, freq):
    angle = shift.astype(F32) * freq
    low = iota(angle.shape, 1) < HEAD_WIDTH // 2
    sine, cosine = sine_cosine(angle)
    return cosine, jnp.where(low, -sine, sine)


def rotated(vectors, cosine, sine):
    return vectors * cosine + pltpu.roll(vectors, HEAD_WIDTH // 2, 1) * sine


def tables_kernel(
    tiles,
    ranks,
    stretch_len,
    row_total,
    stretches_ref,
    offsets_ref,
    counts_ref,
    positions_ref,
    freq_ref,
    cos_ref,
    sin_ref,
    bias_ref,
    token_cos_ref,
    token_sin_ref,
):
    slot = lax.axis_index("slot")
    row = lax.axis_index("row")
    freq = freq_ref[...]
    count = counts_ref[slot]
    arriving = tiles
    slot_tiles = stretches_ref.shape[1]
    stretches = stretches_ref[pl.ds(slot, 1), :]
    owner, _ = divide(stretches, tiles)
    slots = arriving // ranks
    place, rank_wanted = divide(iota((arriving, slot_tiles), 0), ranks)
    bits, flip = jnp.zeros_like(place), jnp.zeros_like(place)
    for i, (first, second, other) in enumerate(arrivals(slots)):
        bits = jnp.where(place == i, for_row((first, second), row), bits)
        flip = jnp.where(place == i, other, flip)
    from_slot = slot ^ bits
    from_row = row ^ flip
    match = (owner == from_slot * row_total + from_row).astype(F32)
    rank = earlier_count(match)
    picked = jnp.where(rank == rank_wanted.astype(F32), match, 0.0)
    tile_ids = iota((1, slot_tiles), 1).astype(F32)
    tile = jnp.sum(picked * tile_ids, axis=1, keepdims=True)
    page, lane = divide(stretches, 128)
    in_lane = (iota((128, slot_tiles), 0) == lane).astype(F32).astype(BF16)
    upper, lower = divide(offsets_ref[...], 64)
    page_count = upper.shape[0]
    split = jnp.concatenate([upper, lower], axis=0).astype(F32).astype(BF16)
    split = jnp.dot(split, in_lane, preferred_element_type=F32)
    offset = split[:page_count] * 64.0 + split[page_count:]
    in_page = iota((page_count, slot_tiles), 0) == page
    offset = jnp.sum(jnp.where(in_page, offset, 0.0), axis=0, keepdims=True)
    shift = jnp.sum(picked * (tile_ids * stretch_len - offset), axis=1, keepdims=True)
    cosine, sine = angle_tables(shift, freq)
    local_keys = arriving * stretch_len
    spread = lambda x: jnp.broadcast_to(
        x[:, None, :], (arriving, stretch_len, x.shape[1])
    ).reshape(local_keys, x.shape[1])
    cos_ref[...] = spread(cosine)
    sin_ref[...] = spread(sine)
    token_total = positions_ref.shape[1]
    share = token_total // row_total
    positions = positions_ref[...]
    group = bias_ref.shape[1] // token_total
    query_positions = jnp.concatenate([positions] * group, axis=1)
    first = jnp.broadcast_to(tile * stretch_len, (arriving, 128))
    _, token = divide(iota((local_keys, 128), 0), stretch_len)
    key_positions = spread(first).astype(jnp.int32) + token
    redone = (key_positions[:, :token_total] == positions).astype(F32).astype(BF16)
    redone = jnp.dot(redone, jnp.ones((token_total, 128), BF16), preferred_element_type=F32)
    usable = jnp.logical_and(key_positions < count * stretch_len, redone == 0.0)
    key_positions = jnp.where(usable, key_positions, FAR)
    for start in range(0, bias_ref.shape[1], 128):
        cols = slice(start, start + 128)
        bias_ref[:local_keys, cols] = jnp.where(
            key_positions <= query_positions[:, cols], 0.0, NEGATIVE
        )
    square = iota((token_total, token_total), 0) == iota((token_total, token_total), 1)
    column = jnp.sum(
        jnp.where(square, positions.astype(F32), 0.0), axis=1, keepdims=True
    ).astype(jnp.int32)
    new_positions = of_row(column, row, share)
    new_usable = new_positions < count * stretch_len
    new_positions = jnp.where(new_usable, new_positions, FAR)
    bias_ref[local_keys:, :] = jnp.where(new_positions <= query_positions, 0.0, NEGATIVE)
    token_cos_ref[...], token_sin_ref[...] = angle_tables(column, freq)


def of_row(value, row, share):
    kept = value[:share]
    for r in range(1, value.shape[0] // share):
        kept = jnp.where(row == r, value[r * share : (r + 1) * share], kept)
    return kept


def attend_kernel(stretch_rows, *refs):
    *arrived, cos_ref, sin_ref, bias_ref, token_cos_ref, token_sin_ref, both_ref, out_ref = refs
    parts = [
        (ref, at) for ref in arrived for at in range(0, ref.shape[0], 2 * stretch_rows)
    ]
    row = lax.axis_index("row")
    token_total = token_cos_ref.shape[0]
    share = bias_ref.shape[0] - cos_ref.shape[0]
    group = bias_ref.shape[1] // token_total
    key_columns = arrived[0].shape[1]
    key_heads = key_columns // HEAD_WIDTH
    query_columns = group * key_columns
    scale = 1.0 / math.sqrt(HEAD_WIDTH)
    cosine = cos_ref[...]
    sine = sin_ref[...]
    token_cosine = token_cos_ref[...]
    token_sine = token_sin_ref[...]
    bias = bias_ref[...]

    def projected(start):
        cols = slice(start, start + HEAD_WIDTH)
        return both_ref[0, :, cols] + both_ref[1, :, cols]

    all_scores, all_values = [], []
    for head in range(key_heads):
        at = head * HEAD_WIDTH
        cols = slice(at, at + HEAD_WIDTH)
        queries = jnp.concatenate(
            [
                rotated(projected((head * group + j) * HEAD_WIDTH), token_cosine, token_sine)
                for j in range(group)
            ],
            axis=0,
        ).astype(BF16)
        new_keys = rotated(projected(query_columns + at), token_cosine, token_sine)
        new_values = projected(query_columns + key_columns + at)
        keys = jnp.concatenate([ref[at : at + stretch_rows, cols] for ref, at in parts], axis=0)
        keys = rotated(keys.astype(F32), cosine, sine).astype(BF16)
        keys = jnp.concatenate([keys, of_row(new_keys, row, share).astype(BF16)], axis=0)
        values = [
            ref[at + stretch_rows : at + 2 * stretch_rows, cols] for ref, at in parts
        ]
        all_values.append(
            jnp.concatenate(values + [of_row(new_values, row, share).astype(BF16)], axis=0)
        )
        all_scores.append(
            lax.dot_general(
                keys, queries, (((1,), (1,)), ((), ())), preferred_element_type=F32
            )
        )
    all_probs = []
    base = key_heads * HEAD_WIDTH
    for head, scores in enumerate(all_scores):
        scores = scores * scale + bias
        peak = jnp.max(scores, axis=0, keepdims=True)
        probs = jnp.exp(scores - peak)
        out_ref[base + head : base + head + 1, :] = peak
        out_ref[base + key_heads + head : base + key_heads + head + 1, :] = jnp.sum(
            probs, axis=0, keepdims=True
        )
        all_probs.append(probs.astype(BF16))
    for head in range(key_heads):
        out_ref[head * HEAD_WIDTH : (head + 1) * HEAD_WIDTH, :] = lax.dot_general(
            all_values[head], all_probs[head], (((0,), (0,)), ((), ())), preferred_element_type=F32
        )


def output_kernel(step, key_heads, own_ref, other_ref, w_ref, keep_ref, send_ref, attended):
    token_total = attended.shape[0]
    group = own_ref.shape[1] // token_total
    base = key_heads * HEAD_WIDTH
    for head in range(key_heads):
        rows = slice(head * HEAD_WIDTH, (head + 1) * HEAD_WIDTH)
        at_peak = slice(base + head, base + head + 1)
        at_total = slice(base + key_heads + head, base + key_heads + head + 1)
        peak = jnp.maximum(own_ref[at_peak, :], other_ref[at_peak, :])
        own_scale = jnp.exp(own_ref[at_peak, :] - peak)
        other_scale = jnp.exp(other_ref[at_peak, :] - peak)
        total = own_ref[at_total, :] * own_scale + other_ref[at_total, :] * other_scale
        weighted = own_ref[rows, :] * own_scale + other_ref[rows, :] * other_scale
        result = jnp.transpose(weighted / total).astype(BF16)
        for j in range(group):
            start = (head * group + j) * HEAD_WIDTH
            attended[:, start : start + HEAD_WIDTH] = result[
                j * token_total : (j + 1) * token_total
            ]
    tokens = attended[...]
    share = keep_ref.shape[0]
    first = lax.axis_index("col") == 0
    for start in range(0, w_ref.shape[1], step):
        cols = slice(start, start + step)
        part = jnp.dot(tokens, w_ref[:, cols], preferred_element_type=F32)
        keep_ref[:, cols] = jnp.where(first, part[:share], part[share:])
        send_ref[:, cols] = jnp.where(first, part[share:], part[:share]).astype(BF16)


def cost(us):
    return pl.CostEstimate(flops=us * 1_000_000_000, bytes_accessed=1000, transcendentals=0)


def in_hbm(value):
    return pltpu.with_memory_space_constraint(value, pltpu.HBM)


def merge_kernel(count, near_count, *refs):
    kept, given, outs = refs[:count], refs[count], refs[count + 1 + near_count :]
    rows = kept[0].shape[0]
    for i in range(count):
        outs[i][:rows] = kept[i][...]
        outs[i][rows:] = given[i * rows : (i + 1) * rows]


def merge(kept, given, near, grant):
    count, near_count = len(kept), len(near)
    block = kept[0]
    results = pl.pallas_call(
        functools.partial(merge_kernel, count, near_count),
        out_shape=[jax.ShapeDtypeStruct((2 * block.shape[0], block.shape[1]), BF16)] * count
        + [jax.ShapeDtypeStruct(block.shape, BF16)] * near_count,
        in_specs=[VMEM] * (count + 1) + [ANY] * near_count,
        out_specs=[VMEM] * count + [ANY] * near_count,
        input_output_aliases={count + 1 + i: count + i for i in range(near_count)},
        compiler_params=params(grant),
        cost_estimate=cost(0),
        name="merge",
    )(*kept, given, *near)
    return *results[:count], results[count:]


def params(mib):
    return pltpu.CompilerParams(vmem_limit_bytes=mib * MIB)


def on_device(
    hidden,
    w_query,
    key_weight,
    value_weight,
    w_out,
    kv_store,
    stretch_offset,
    tile_stretch,
    slot_count,
    recomp_pos,
):
    slot_total = lax.axis_size("slot")
    row_total = lax.axis_size("row")
    tiles, _, stretch_len, key_columns = kv_store.shape
    slot_tiles = tile_stretch.shape[1]
    ranks = slot_tiles // (slot_total * row_total)
    width = hidden.shape[2]
    token_total = hidden.shape[1]
    query_columns = w_query.shape[1]
    key_heads = key_columns // HEAD_WIDTH
    group = query_columns // key_columns
    query_rows = group * token_total
    per_slot = ranks * 2 * stretch_len
    local_keys = tiles * stretch_len
    share = token_total // row_total
    all_keys = local_keys + share
    swap = [(0, 1), (1, 0)]
    grant = 16 if slot_total <= 8 else 40

    freq = np.arange(HEAD_WIDTH // 2, dtype=np.float64)
    freq = (ROPE_BASE ** (-2.0 * freq / HEAD_WIDTH)).astype(np.float32)
    freq = jnp.asarray(np.concatenate([freq, freq])[None, :])

    store_shape = (tiles * 2 * stretch_len, key_columns)
    step = key_columns
    direct, shared = exchanges(slot_total)
    block = jax.ShapeDtypeStruct((per_slot, key_columns), BF16)
    *outgoing, give = pl.pallas_call(
        functools.partial(pack_kernel, tiles, ranks, stretch_len),
        out_shape=[block] * (len(direct) + 1 + len(shared))
        + [jax.ShapeDtypeStruct((len(shared) * per_slot, key_columns), BF16)],
        in_specs=[HBM, HBM],
        out_specs=[VMEM] * (len(direct) + len(shared) + 2),
        scratch_shapes=[
            pltpu.VMEM(tile_stretch.shape, jnp.int32),
            pltpu.VMEM(store_shape, BF16),
            pltpu.VMEM((slot_total, 128), F32),
            pltpu.SemaphoreType.DMA((2,)),
        ],
        compiler_params=params(grant),
        cost_estimate=cost(8),
        name="pack",
    )(in_hbm(tile_stretch), in_hbm(kv_store.reshape(store_shape)))
    own_block, kept = outgoing[len(direct)], outgoing[len(direct) + 1 :]
    given = lax.ppermute(give, "row", swap)
    early = [True for k in direct]
    late_blocks = [outgoing[i] for i in range(len(direct)) if not early[i]]
    *merged, late_blocks = merge(kept, given, late_blocks, grant)
    late_blocks = iter(late_blocks)
    arrived = []
    for i, k in enumerate(direct):
        sent = outgoing[i] if early[i] else next(late_blocks)
        arrived.append(lax.ppermute(sent, "slot", [(s, s ^ k) for s in range(slot_total)]))
    for sent, pair in zip(merged, shared):
        pairs = [
            (s * row_total + r, (s ^ pair[r]) * row_total + r)
            for s in range(slot_total)
            for r in range(row_total)
        ]
        arrived.append(lax.ppermute(sent, ("slot", "row"), pairs))
    arrived.append(own_block)

    projected = pl.pallas_call(
        functools.partial(project_kernel, step),
        out_shape=jax.ShapeDtypeStruct((token_total, query_columns + 2 * key_columns), F32),
        in_specs=[ANY] + [VMEM] * 4,
        out_specs=VMEM,
        compiler_params=params(grant),
        cost_estimate=cost(0),
        name="project",
    )(merged[0], hidden[0], w_query, key_weight, value_weight)
    both = lax.all_gather(projected, "row")

    tables = pl.pallas_call(
        functools.partial(tables_kernel, tiles, ranks, stretch_len, row_total),
        out_shape=(
            jax.ShapeDtypeStruct((local_keys, HEAD_WIDTH), F32),
            jax.ShapeDtypeStruct((local_keys, HEAD_WIDTH), F32),
            jax.ShapeDtypeStruct((all_keys, query_rows), F32),
            jax.ShapeDtypeStruct((token_total, HEAD_WIDTH), F32),
            jax.ShapeDtypeStruct((token_total, HEAD_WIDTH), F32),
        ),
        in_specs=[VMEM, VMEM, SMEM, VMEM, VMEM],
        out_specs=(VMEM,) * 5,
        compiler_params=params(grant),
        cost_estimate=cost(0),
        name="tables",
    )(tile_stretch, stretch_offset.reshape(-1, 128), slot_count, recomp_pos, freq)

    partial = pl.pallas_call(
        functools.partial(attend_kernel, ranks * stretch_len),
        out_shape=jax.ShapeDtypeStruct((key_heads * HEAD_WIDTH + 2 * key_heads, query_rows), F32),
        in_specs=[VMEM] * (len(direct) + len(shared) + 7),
        out_specs=VMEM,
        compiler_params=params(grant),
        cost_estimate=cost(8),
        name="attend",
    )(*arrived, *tables, both)
    partial_other = lax.ppermute(partial, "row", swap)

    out_columns = w_out.shape[1]
    out_share = token_total // lax.axis_size("col")
    keep, send = pl.pallas_call(
        functools.partial(output_kernel, step, key_heads),
        out_shape=(
            jax.ShapeDtypeStruct((out_share, out_columns), F32),
            jax.ShapeDtypeStruct((out_share, out_columns), BF16),
        ),
        in_specs=[VMEM, VMEM, VMEM],
        out_specs=(VMEM, VMEM),
        scratch_shapes=[pltpu.VMEM((token_total, query_columns), BF16)],
        compiler_params=params(grant),
        name="output",
    )(partial, partial_other, w_out)
    received = lax.ppermute(send, "col", swap)
    return (keep + received.astype(F32)).astype(BF16)[None]


def solution(mesh):
    return jax.shard_map(
        on_device,
        mesh=mesh,
        in_specs=(
            P("slot", None, "row"),
            P("row", "col"),
            P("row", "col"),
            P("row", "col"),
            P("col", "row"),
            P(("slot", "row"), None, None, "col"),
            P(),
            P(),
            P(),
            P("slot", None),
        ),
        out_specs=P("slot", "col", "row"),
        check_vma=False,
    )
```

```python
import functools
import math

import jax
import jax.numpy as jnp
import numpy as np
from jax import lax
from jax.experimental import pallas as pl
from jax.experimental.pallas import tpu as pltpu
from jax.sharding import PartitionSpec as P

HEAD_WIDTH = 128
NEGATIVE = -1e30
ROPE_BASE = 500000.0
MIB = 1024 * 1024
FAR = 1 << 28
F32 = jnp.float32
BF16 = jnp.bfloat16
VMEM = pl.BlockSpec(memory_space=pltpu.VMEM)
ANY = pl.BlockSpec(memory_space=pl.ANY)
HBM = pl.BlockSpec(memory_space=pltpu.HBM)
SMEM = pl.BlockSpec(memory_space=pltpu.SMEM)


def exchanges(slots):
    if slots == 8:
        return [4, 6, 3], [(2, 1), (7, 5)]
    return [1], [(k, k - 1) for k in range(slots - 1, 1, -2)]


def for_row(pair, row):
    return pair[1] + (1 - row) * (pair[0] - pair[1])


def arrivals(slots):
    direct, shared = exchanges(slots)
    blocks = [(k, k, 0) for k in direct + [0]]
    return blocks + [(*pair, flip) for pair in shared for flip in (0, 1)]


def iota(shape, dim):
    return lax.broadcasted_iota(jnp.int32, shape, dim)


def divide(value, by):
    if by & (by - 1) == 0:
        shift = by.bit_length() - 1
        return lax.shift_right_logical(value, jnp.full_like(value, shift)), value & (by - 1)
    quotient = jnp.floor((value.astype(F32) + 0.5) * (1.0 / by)).astype(jnp.int32)
    return quotient, value - quotient * by


def earlier_count(flags):
    n = flags.shape[1]
    before = (iota((n, n), 0) < iota((n, n), 1)).astype(BF16)
    return jnp.dot(flags.astype(BF16), before, preferred_element_type=F32)


def pack_kernel(tiles, ranks, stretch_len, stretches_hbm, store_hbm, *refs):
    *outs, give_ref, stretches_ref, store_ref, ids_ref, sems = refs
    get_store = pltpu.make_async_copy(store_hbm, store_ref, sems.at[0])
    get_stretches = pltpu.make_async_copy(stretches_hbm, stretches_ref, sems.at[1])
    get_stretches.start()
    get_store.start()
    slot = lax.axis_index("slot")
    row = lax.axis_index("row")
    own = slot * lax.axis_size("row") + row
    slots, slot_tiles = stretches_ref.shape
    per_slot = ranks * 2 * stretch_len
    rows = slots * per_slot
    part, token = divide(iota((rows, 128), 0), stretch_len)
    part, rank_of_row = divide(part, ranks)
    kind = part & 1
    rank_here = iota((rows, 128), 1) == rank_of_row
    within = (kind * stretch_len + token)[:, :1]
    get_stretches.wait()
    owner, local = divide(stretches_ref[...], tiles)
    mine = (owner == own).astype(F32)
    rank = earlier_count(mine)
    lane = iota((slots, 128), 1)
    ids = jnp.zeros((slots, 128), F32)
    for k in range(ranks):
        picked = jnp.where(rank == k, mine * local.astype(F32), 0.0)
        ids = jnp.where(lane == k, jnp.sum(picked, axis=1, keepdims=True), ids)
    ids_ref[...] = ids
    direct, shared = exchanges(slots)
    ids = jnp.concatenate(
        [
            jnp.broadcast_to(ids_ref[pl.ds(slot ^ k, 1), :], (per_slot, 128))
            for k in direct + [0] + [for_row(pair, r) for r in (row, 1 - row) for pair in shared]
        ],
        axis=0,
    )
    stretch = jnp.sum(jnp.where(rank_here, ids, 0.0), axis=1, keepdims=True).astype(jnp.int32)
    source = stretch * (2 * stretch_len) + within
    store_rows = tiles * 2 * stretch_len
    pick = (iota((rows, store_rows), 1) == source).astype(F32).astype(BF16)
    get_store.wait()
    picked = jnp.dot(pick, store_ref[...], preferred_element_type=F32).astype(BF16)
    for i, out_ref in enumerate(outs):
        out_ref[...] = picked[i * per_slot : (i + 1) * per_slot]
    give_ref[...] = picked[len(outs) * per_slot :]


def fetch(pieces, sems):
    copies = [pltpu.make_async_copy(a, b, sems.at[i]) for i, (a, b) in enumerate(pieces)]
    for copy in copies:
        copy.start()
    return copies


def column_pieces(source, target, step):
    return [
        (source.at[:, pl.ds(start, step)], target.at[:, pl.ds(start, step)])
        for start in range(0, source.shape[1], step)
    ]


def project_kernel(step, after_ref, hidden_ref, wq_ref, wk_ref, wv_ref, out_ref):
    tokens = hidden_ref[...]
    base = 0
    for weight_ref in (wq_ref, wk_ref, wv_ref):
        for start in range(0, weight_ref.shape[1], step):
            out_ref[:, base : base + step] = jnp.dot(
                tokens, weight_ref[:, start : start + step], preferred_element_type=F32
            )
            base += step


def sine_cosine(angle):
    turns = jnp.floor(angle * (2.0 / math.pi) + 0.5)
    rest = angle - turns * 1.5703125
    rest = rest - turns * 4.837512969970703125e-4
    rest = rest - turns * 7.54978995489188216e-8
    square = rest * rest
    sine = (-1.9515295891e-4 * square + 8.3321608736e-3) * square - 1.6666654611e-1
    sine = sine * square * rest + rest
    cosine = (2.443315711809948e-5 * square - 1.388731625493765e-3) * square
    cosine = (cosine + 4.166664568298827e-2) * square * square - 0.5 * square + 1.0
    quarter = turns.astype(jnp.int32) & 3
    odd = (quarter & 1) == 1
    sine, cosine = jnp.where(odd, cosine, sine), jnp.where(odd, sine, cosine)
    sine = jnp.where(quarter >= 2, -sine, sine)
    cosine = jnp.where(jnp.logical_or(quarter == 1, quarter == 2), -cosine, cosine)
    return sine, cosine


def angle_tables(shift, freq):
    angle = shift.astype(F32) * freq
    low = iota(angle.shape, 1) < HEAD_WIDTH // 2
    sine, cosine = sine_cosine(angle)
    return cosine, jnp.where(low, -sine, sine)


def rotated(vectors, cosine, sine):
    return vectors * cosine + pltpu.roll(vectors, HEAD_WIDTH // 2, 1) * sine


def tables_kernel(
    tiles,
    ranks,
    stretch_len,
    row_total,
    stretches_ref,
    offsets_ref,
    counts_ref,
    positions_ref,
    freq_ref,
    cos_ref,
    sin_ref,
    bias_ref,
    token_cos_ref,
    token_sin_ref,
):
    slot = lax.axis_index("slot")
    row = lax.axis_index("row")
    freq = freq_ref[...]
    count = counts_ref[slot]
    arriving = tiles
    slot_tiles = stretches_ref.shape[1]
    stretches = stretches_ref[pl.ds(slot, 1), :]
    owner, _ = divide(stretches, tiles)
    slots = arriving // ranks
    place, rank_wanted = divide(iota((arriving, slot_tiles), 0), ranks)
    bits, flip = jnp.zeros_like(place), jnp.zeros_like(place)
    for i, (first, second, other) in enumerate(arrivals(slots)):
        bits = jnp.where(place == i, for_row((first, second), row), bits)
        flip = jnp.where(place == i, other, flip)
    from_slot = slot ^ bits
    from_row = row ^ flip
    match = (owner == from_slot * row_total + from_row).astype(F32)
    rank = earlier_count(match)
    picked = jnp.where(rank == rank_wanted.astype(F32), match, 0.0)
    tile_ids = iota((1, slot_tiles), 1).astype(F32)
    tile = jnp.sum(picked * tile_ids, axis=1, keepdims=True)
    page, lane = divide(stretches, 128)
    in_lane = (iota((128, slot_tiles), 0) == lane).astype(F32).astype(BF16)
    upper, lower = divide(offsets_ref[...], 64)
    page_count = upper.shape[0]
    split = jnp.concatenate([upper, lower], axis=0).astype(F32).astype(BF16)
    split = jnp.dot(split, in_lane, preferred_element_type=F32)
    offset = split[:page_count] * 64.0 + split[page_count:]
    in_page = iota((page_count, slot_tiles), 0) == page
    offset = jnp.sum(jnp.where(in_page, offset, 0.0), axis=0, keepdims=True)
    shift = jnp.sum(picked * (tile_ids * stretch_len - offset), axis=1, keepdims=True)
    cosine, sine = angle_tables(shift, freq)
    local_keys = arriving * stretch_len
    spread = lambda x: jnp.broadcast_to(
        x[:, None, :], (arriving, stretch_len, x.shape[1])
    ).reshape(local_keys, x.shape[1])
    cos_ref[...] = spread(cosine)
    sin_ref[...] = spread(sine)
    token_total = positions_ref.shape[1]
    share = token_total // row_total
    positions = positions_ref[...]
    group = bias_ref.shape[1] // token_total
    query_positions = jnp.concatenate([positions] * group, axis=1)
    first = jnp.broadcast_to(tile * stretch_len, (arriving, 128))
    _, token = divide(iota((local_keys, 128), 0), stretch_len)
    key_positions = spread(first).astype(jnp.int32) + token
    redone = (key_positions[:, :token_total] == positions).astype(F32).astype(BF16)
    redone = jnp.dot(redone, jnp.ones((token_total, 128), BF16), preferred_element_type=F32)
    usable = jnp.logical_and(key_positions < count * stretch_len, redone == 0.0)
    key_positions = jnp.where(usable, key_positions, FAR)
    for start in range(0, bias_ref.shape[1], 128):
        cols = slice(start, start + 128)
        bias_ref[:local_keys, cols] = jnp.where(
            key_positions <= query_positions[:, cols], 0.0, NEGATIVE
        )
    square = iota((token_total, token_total), 0) == iota((token_total, token_total), 1)
    column = jnp.sum(
        jnp.where(square, positions.astype(F32), 0.0), axis=1, keepdims=True
    ).astype(jnp.int32)
    new_positions = of_row(column, row, share)
    new_usable = new_positions < count * stretch_len
    new_positions = jnp.where(new_usable, new_positions, FAR)
    bias_ref[local_keys:, :] = jnp.where(new_positions <= query_positions, 0.0, NEGATIVE)
    token_cos_ref[...], token_sin_ref[...] = angle_tables(column, freq)


def of_row(value, row, share):
    kept = value[:share]
    for r in range(1, value.shape[0] // share):
        kept = jnp.where(row == r, value[r * share : (r + 1) * share], kept)
    return kept


def block_parts(blocks, stretch_rows):
    return [(ref, at) for ref in blocks for at in range(0, ref.shape[0], 2 * stretch_rows)]


def keys_of(parts, stretch_rows, cols, cosine, sine):
    keys = jnp.concatenate([ref[at : at + stretch_rows, cols] for ref, at in parts], axis=0)
    return rotated(keys.astype(F32), cosine, sine).astype(BF16)


def values_of(parts, stretch_rows, cols):
    return [ref[at + stretch_rows : at + 2 * stretch_rows, cols] for ref, at in parts]


def scores_of(keys, queries, bias):
    nt = (((1,), (1,)), ((), ()))
    scores = lax.dot_general(keys, queries, nt, preferred_element_type=F32)
    return scores * (1.0 / math.sqrt(HEAD_WIDTH)) + bias


def queries_kernel(stretch_rows, *refs):
    *arrived, cos_ref, sin_ref, bias_ref, token_cos_ref, token_sin_ref, both_ref = refs[:-3]
    q_ref, scores_ref, values_ref = refs[-3:]
    parts = block_parts(arrived, stretch_rows)
    row = lax.axis_index("row")
    token_total = token_cos_ref.shape[0]
    local_keys = cos_ref.shape[0]
    share, count = values_ref.shape[0], len(parts) * stretch_rows
    query_rows = bias_ref.shape[1]
    group = query_rows // token_total
    key_columns = arrived[0].shape[1]
    key_heads = key_columns // HEAD_WIDTH
    query_columns = group * key_columns
    cosine, sine = cos_ref[:count, :], sin_ref[:count, :]
    token_cosine, token_sine = token_cos_ref[...], token_sin_ref[...]
    bias = jnp.concatenate([bias_ref[:count, :], bias_ref[local_keys:, :]], axis=0)

    def projected(start, width=HEAD_WIDTH):
        cols = slice(start, start + width)
        return both_ref[0, :, cols] + both_ref[1, :, cols]

    all_queries, all_scores = [], []
    for head in range(key_heads):
        at = head * HEAD_WIDTH
        queries = [
            rotated(projected((head * group + j) * HEAD_WIDTH), token_cosine, token_sine)
            for j in range(group)
        ]
        queries = jnp.concatenate(queries, axis=0).astype(BF16)
        new_keys = rotated(projected(query_columns + at), token_cosine, token_sine)
        keys = keys_of(parts, stretch_rows, slice(at, at + HEAD_WIDTH), cosine, sine)
        keys = jnp.concatenate([keys, of_row(new_keys, row, share).astype(BF16)], axis=0)
        all_queries.append(queries)
        all_scores.append(scores_of(keys, queries, bias))
    new_values = projected(query_columns + key_columns, key_columns)
    values_ref[...] = of_row(new_values, row, share).astype(BF16)
    for head in range(key_heads):
        q_ref[head * query_rows : (head + 1) * query_rows, :] = all_queries[head]
        scores_ref[head * (count + share) : (head + 1) * (count + share), :] = all_scores[head]


def attend_kernel(stretch_rows, first_blocks, *refs):
    *arrived, cos_ref, sin_ref, bias_ref, q_ref, scores_ref, values_ref, out_ref, send_ref = refs
    first = block_parts(arrived[:first_blocks], stretch_rows)
    later = block_parts(arrived[first_blocks:], stretch_rows)
    count, local_keys = len(first) * stretch_rows, cos_ref.shape[0]
    known = count + values_ref.shape[0]
    query_rows = bias_ref.shape[1]
    key_heads = arrived[0].shape[1] // HEAD_WIDTH
    cosine, sine = cos_ref[count:, :], sin_ref[count:, :]
    bias = bias_ref[count:local_keys, :]
    all_scores, all_values = [], []
    for head in range(key_heads):
        cols = slice(head * HEAD_WIDTH, (head + 1) * HEAD_WIDTH)
        keys = keys_of(later, stretch_rows, cols, cosine, sine)
        queries = q_ref[head * query_rows : (head + 1) * query_rows, :]
        scores = [scores_ref[head * known : (head + 1) * known, :]]
        scores.append(scores_of(keys, queries, bias))
        all_scores.append(jnp.concatenate(scores, axis=0))
        values = values_of(first, stretch_rows, cols) + [values_ref[:, cols]]
        values += values_of(later, stretch_rows, cols)
        all_values.append(jnp.concatenate(values, axis=0))
    all_probs = []
    stats = []
    for scores in all_scores:
        peak = jnp.max(scores, axis=0, keepdims=True)
        probs = jnp.exp(scores - peak)
        stats.append((peak, jnp.sum(probs, axis=0, keepdims=True)))
        all_probs.append(probs.astype(BF16))
    stats = jnp.concatenate([x[0] for x in stats] + [x[1] for x in stats], axis=0)
    base = key_heads * HEAD_WIDTH
    out_ref[base:, :] = stats
    for part in range(3):
        term = stats.astype(BF16)
        at = base + 16 * part
        send_ref[at : at + 16, :] = jnp.concatenate(
            [term.astype(F32), jnp.zeros_like(stats)], axis=0
        ).astype(BF16)
        stats = stats - term.astype(F32)
    for head in range(key_heads):
        weighted = lax.dot_general(
            all_values[head], all_probs[head], (((0,), (0,)), ((), ())), preferred_element_type=F32
        )
        rows = slice(head * HEAD_WIDTH, (head + 1) * HEAD_WIDTH)
        out_ref[rows, :] = weighted
        send_ref[rows, :] = weighted.astype(BF16)


def output_kernel(step, key_heads, own_ref, other_ref, w_ref, keep_ref, send_ref, attended):
    token_total = attended.shape[0]
    group = own_ref.shape[1] // token_total
    base = key_heads * HEAD_WIDTH
    results = []
    own_stats = own_ref[base:, :]
    terms = [
        other_ref[base + 16 * part : base + 16 * (part + 1), :].astype(F32) for part in range(3)
    ]
    other_stats = (terms[0] + terms[1] + terms[2])[: 2 * key_heads]
    peaks = jnp.maximum(own_stats[:key_heads], other_stats[:key_heads])
    own_scales = jnp.exp(own_stats[:key_heads] - peaks)
    other_scales = jnp.exp(other_stats[:key_heads] - peaks)
    totals = own_stats[key_heads:] * own_scales + other_stats[key_heads:] * other_scales
    for head in range(key_heads):
        rows = slice(head * HEAD_WIDTH, (head + 1) * HEAD_WIDTH)
        at = slice(head, head + 1)
        total = totals[at]
        weighted = own_ref[rows, :] * own_scales[at]
        weighted += other_ref[rows, :].astype(F32) * other_scales[at]
        results.append(jnp.transpose(weighted / total).astype(BF16))
    tokens = jnp.concatenate(
        [
            result[j * token_total : (j + 1) * token_total]
            for result in results
            for j in range(group)
        ],
        axis=1,
    )
    share = keep_ref.shape[0]
    first = lax.axis_index("col") == 0
    for start in range(0, w_ref.shape[1], step):
        cols = slice(start, start + step)
        part = jnp.dot(tokens, w_ref[:, cols], preferred_element_type=F32)
        keep_ref[:, cols] = jnp.where(first, part[:share], part[share:])
        send_ref[:, cols] = jnp.where(first, part[share:], part[:share]).astype(BF16)


def cost(us):
    return pl.CostEstimate(flops=us * 1_000_000_000, bytes_accessed=1000, transcendentals=0)


def in_hbm(value):
    return pltpu.with_memory_space_constraint(value, pltpu.HBM)


def merge_kernel(count, near_count, *refs):
    kept, given, outs = refs[:count], refs[count], refs[count + 1 + near_count :]
    rows = kept[0].shape[0]
    for i in range(count):
        outs[i][:rows] = kept[i][...]
        outs[i][rows:] = given[i * rows : (i + 1) * rows]


def merge(kept, given, near, grant):
    count, near_count = len(kept), len(near)
    block = kept[0]
    results = pl.pallas_call(
        functools.partial(merge_kernel, count, near_count),
        out_shape=[jax.ShapeDtypeStruct((2 * block.shape[0], block.shape[1]), BF16)] * count
        + [jax.ShapeDtypeStruct(block.shape, BF16)] * near_count,
        in_specs=[VMEM] * (count + 1) + [ANY] * near_count,
        out_specs=[VMEM] * count + [ANY] * near_count,
        input_output_aliases={count + 1 + i: count + i for i in range(near_count)},
        compiler_params=params(grant),
        cost_estimate=cost(0),
        name="merge",
    )(*kept, given, *near)
    return *results[:count], results[count:]


def params(mib):
    return pltpu.CompilerParams(vmem_limit_bytes=mib * MIB)


def on_device(
    hidden,
    w_query,
    key_weight,
    value_weight,
    w_out,
    kv_store,
    stretch_offset,
    tile_stretch,
    slot_count,
    recomp_pos,
):
    slot_total = lax.axis_size("slot")
    row_total = lax.axis_size("row")
    tiles, _, stretch_len, key_columns = kv_store.shape
    slot_tiles = tile_stretch.shape[1]
    ranks = slot_tiles // (slot_total * row_total)
    width = hidden.shape[2]
    token_total = hidden.shape[1]
    query_columns = w_query.shape[1]
    key_heads = key_columns // HEAD_WIDTH
    group = query_columns // key_columns
    query_rows = group * token_total
    per_slot = ranks * 2 * stretch_len
    local_keys = tiles * stretch_len
    share = token_total // row_total
    all_keys = local_keys + share
    swap = [(0, 1), (1, 0)]
    grant = 16 if slot_total <= 8 else 40

    freq = np.arange(HEAD_WIDTH // 2, dtype=np.float64)
    freq = (ROPE_BASE ** (-2.0 * freq / HEAD_WIDTH)).astype(np.float32)
    freq = jnp.asarray(np.concatenate([freq, freq])[None, :])

    store_shape = (tiles * 2 * stretch_len, key_columns)
    step = key_columns
    direct, shared = exchanges(slot_total)
    block = jax.ShapeDtypeStruct((per_slot, key_columns), BF16)
    *outgoing, give = pl.pallas_call(
        functools.partial(pack_kernel, tiles, ranks, stretch_len),
        out_shape=[block] * (len(direct) + 1 + len(shared))
        + [jax.ShapeDtypeStruct((len(shared) * per_slot, key_columns), BF16)],
        in_specs=[HBM, HBM],
        out_specs=[VMEM] * (len(direct) + len(shared) + 2),
        scratch_shapes=[
            pltpu.VMEM(tile_stretch.shape, jnp.int32),
            pltpu.VMEM(store_shape, BF16),
            pltpu.VMEM((slot_total, 128), F32),
            pltpu.SemaphoreType.DMA((2,)),
        ],
        compiler_params=params(grant),
        cost_estimate=cost(8),
        name="pack",
    )(in_hbm(tile_stretch), in_hbm(kv_store.reshape(store_shape)))
    own_block, kept = outgoing[len(direct)], outgoing[len(direct) + 1 :]
    given = lax.ppermute(give, "row", swap)
    early = [True for k in direct]
    late_blocks = [outgoing[i] for i in range(len(direct)) if not early[i]]
    *merged, late_blocks = merge(kept, given, late_blocks, grant)
    late_blocks = iter(late_blocks)
    arrived = []
    for i, k in enumerate(direct):
        sent = outgoing[i] if early[i] else next(late_blocks)
        arrived.append(lax.ppermute(sent, "slot", [(s, s ^ k) for s in range(slot_total)]))
    arrived.append(own_block)
    for sent, pair in zip(merged, shared):
        pairs = [
            (s * row_total + r, (s ^ pair[r]) * row_total + r)
            for s in range(slot_total)
            for r in range(row_total)
        ]
        arrived.append(lax.ppermute(sent, ("slot", "row"), pairs))

    projected = pl.pallas_call(
        functools.partial(project_kernel, step),
        out_shape=jax.ShapeDtypeStruct((token_total, query_columns + 2 * key_columns), F32),
        in_specs=[ANY] + [VMEM] * 4,
        out_specs=VMEM,
        compiler_params=params(grant),
        cost_estimate=cost(0),
        name="project",
    )(merged[0], hidden[0], w_query, key_weight, value_weight)
    both = lax.all_gather(projected, "row")

    tables = pl.pallas_call(
        functools.partial(tables_kernel, tiles, ranks, stretch_len, row_total),
        out_shape=(
            jax.ShapeDtypeStruct((local_keys, HEAD_WIDTH), F32),
            jax.ShapeDtypeStruct((local_keys, HEAD_WIDTH), F32),
            jax.ShapeDtypeStruct((all_keys, query_rows), F32),
            jax.ShapeDtypeStruct((token_total, HEAD_WIDTH), F32),
            jax.ShapeDtypeStruct((token_total, HEAD_WIDTH), F32),
        ),
        in_specs=[VMEM, VMEM, SMEM, VMEM, VMEM],
        out_specs=(VMEM,) * 5,
        compiler_params=params(grant),
        cost_estimate=cost(0),
        name="tables",
    )(tile_stretch, stretch_offset.reshape(-1, 128), slot_count, recomp_pos, freq)

    first_blocks = len(direct) + 1
    known = first_blocks * ranks * stretch_len + share
    queries, scores, new_values = pl.pallas_call(
        functools.partial(queries_kernel, ranks * stretch_len),
        out_shape=(
            jax.ShapeDtypeStruct((key_heads * query_rows, HEAD_WIDTH), BF16),
            jax.ShapeDtypeStruct((key_heads * known, query_rows), F32),
            jax.ShapeDtypeStruct((share, key_columns), BF16),
        ),
        in_specs=[VMEM] * (first_blocks + 6),
        out_specs=(VMEM,) * 3,
        compiler_params=params(grant),
        cost_estimate=cost(0),
        name="queries",
    )(*arrived[:first_blocks], *tables, both)
    partial, to_swap = pl.pallas_call(
        functools.partial(attend_kernel, ranks * stretch_len, first_blocks),
        out_shape=(
            jax.ShapeDtypeStruct((key_heads * HEAD_WIDTH + 2 * key_heads, query_rows), F32),
            jax.ShapeDtypeStruct((key_heads * HEAD_WIDTH + 3 * 16, query_rows), BF16),
        ),
        in_specs=[VMEM] * (len(direct) + len(shared) + 7),
        out_specs=(VMEM, VMEM),
        compiler_params=params(grant),
        cost_estimate=cost(0),
        name="attend",
    )(*arrived, *tables[:3], queries, scores, new_values)
    partial_other = lax.ppermute(to_swap, "row", swap)

    out_columns = w_out.shape[1]
    out_share = token_total // lax.axis_size("col")
    keep, send = pl.pallas_call(
        functools.partial(output_kernel, out_columns, key_heads),
        out_shape=(
            jax.ShapeDtypeStruct((out_share, out_columns), F32),
            jax.ShapeDtypeStruct((out_share, out_columns), BF16),
        ),
        in_specs=[VMEM, VMEM, VMEM],
        out_specs=(VMEM, VMEM),
        scratch_shapes=[pltpu.VMEM((token_total, query_columns), BF16)],
        compiler_params=params(grant),
        name="output",
    )(partial, partial_other, w_out)
    received = lax.ppermute(send, "col", swap)
    return (keep + received.astype(F32)).astype(BF16)[None]


def solution(mesh):
    return jax.shard_map(
        on_device,
        mesh=mesh,
        in_specs=(
            P("slot", None, "row"),
            P("row", "col"),
            P("row", "col"),
            P("row", "col"),
            P("col", "row"),
            P(("slot", "row"), None, None, "col"),
            P(),
            P(),
            P(),
            P("slot", None),
        ),
        out_specs=P("slot", "col", "row"),
        check_vma=False,
    )
```

```python
import functools
import math

import jax
import jax.numpy as jnp
import numpy as np
from jax import lax
from jax.experimental import pallas as pl
from jax.experimental.pallas import tpu as pltpu
from jax.sharding import PartitionSpec as P

HEAD_WIDTH = 128
NEGATIVE = -1e30
ROPE_BASE = 500000.0
MIB = 1024 * 1024
FAR = 1 << 28
F32 = jnp.float32
BF16 = jnp.bfloat16
VMEM = pl.BlockSpec(memory_space=pltpu.VMEM)
ANY = pl.BlockSpec(memory_space=pl.ANY)
HBM = pl.BlockSpec(memory_space=pltpu.HBM)
SMEM = pl.BlockSpec(memory_space=pltpu.SMEM)


def exchanges(slots):
    if slots == 8:
        return [4, 6, 3], [(2, 1), (7, 5)]
    return [1], [(k, k - 1) for k in range(slots - 1, 1, -2)]


def for_row(pair, row):
    return pair[1] + (1 - row) * (pair[0] - pair[1])


def arrivals(slots):
    direct, shared = exchanges(slots)
    blocks = [(k, k, 0) for k in direct + [0]]
    return blocks + [(*pair, flip) for pair in shared for flip in (0, 1)]


def iota(shape, dim):
    return lax.broadcasted_iota(jnp.int32, shape, dim)


def divide(value, by):
    if by & (by - 1) == 0:
        shift = by.bit_length() - 1
        return lax.shift_right_logical(value, jnp.full_like(value, shift)), value & (by - 1)
    quotient = jnp.floor((value.astype(F32) + 0.5) * (1.0 / by)).astype(jnp.int32)
    return quotient, value - quotient * by


def earlier_count(flags):
    n = flags.shape[1]
    before = (iota((n, n), 0) < iota((n, n), 1)).astype(BF16)
    return jnp.dot(flags.astype(BF16), before, preferred_element_type=F32)


def pack_kernel(tiles, ranks, stretch_len, stretches_hbm, store_hbm, *refs):
    *outs, give_ref, stretches_ref, store_ref, ids_ref, sems = refs
    get_store = pltpu.make_async_copy(store_hbm, store_ref, sems.at[0])
    get_stretches = pltpu.make_async_copy(stretches_hbm, stretches_ref, sems.at[1])
    get_stretches.start()
    get_store.start()
    slot = lax.axis_index("slot")
    row = lax.axis_index("row")
    own = slot * lax.axis_size("row") + row
    slots, slot_tiles = stretches_ref.shape
    per_slot = ranks * stretch_len
    rows = slots * per_slot
    part, token = divide(iota((rows, 128), 0), stretch_len)
    _, rank_of_row = divide(part, ranks)
    rank_here = iota((rows, 128), 1) == rank_of_row
    get_stretches.wait()
    owner, local = divide(stretches_ref[...], tiles)
    mine = (owner == own).astype(F32)
    rank = earlier_count(mine)
    lane = iota((slots, 128), 1)
    ids = jnp.zeros((slots, 128), F32)
    for k in range(ranks):
        picked = jnp.where(rank == k, mine * local.astype(F32), 0.0)
        ids = jnp.where(lane == k, jnp.sum(picked, axis=1, keepdims=True), ids)
    ids_ref[...] = ids
    direct, shared = exchanges(slots)
    ids = jnp.concatenate(
        [
            jnp.broadcast_to(ids_ref[pl.ds(slot ^ k, 1), :], (per_slot, 128))
            for k in direct + [0] + [for_row(pair, r) for r in (row, 1 - row) for pair in shared]
        ],
        axis=0,
    )
    stretch = jnp.sum(jnp.where(rank_here, ids, 0.0), axis=1, keepdims=True).astype(jnp.int32)
    source = stretch * stretch_len + token[:, :1]
    store_rows = tiles * stretch_len
    pick = (iota((rows, store_rows), 1) == source).astype(F32).astype(BF16)
    get_store.wait()
    columns = store_ref.shape[1]
    store = store_ref[...].astype(F32).reshape(tiles, 2, stretch_len, columns)
    keys, values = [
        jnp.dot(
            pick,
            store[:, kind].reshape(store_rows, columns).astype(BF16),
            preferred_element_type=F32,
        ).astype(BF16)
        for kind in range(2)
    ]
    for i, out_ref in enumerate(outs):
        out_ref[:per_slot] = keys[i * per_slot : (i + 1) * per_slot]
        out_ref[per_slot:] = values[i * per_slot : (i + 1) * per_slot]
    for i in range(len(shared)):
        at = (len(outs) + i) * per_slot
        give_ref[2 * i * per_slot : (2 * i + 1) * per_slot] = keys[at : at + per_slot]
        give_ref[(2 * i + 1) * per_slot : (2 * i + 2) * per_slot] = values[at : at + per_slot]


def fetch(pieces, sems):
    copies = [pltpu.make_async_copy(a, b, sems.at[i]) for i, (a, b) in enumerate(pieces)]
    for copy in copies:
        copy.start()
    return copies


def column_pieces(source, target, step):
    return [
        (source.at[:, pl.ds(start, step)], target.at[:, pl.ds(start, step)])
        for start in range(0, source.shape[1], step)
    ]


def project_kernel(step, after_ref, hidden_ref, wq_ref, wk_ref, wv_ref, out_ref):
    tokens = hidden_ref[...]
    base = 0
    for weight_ref in (wq_ref, wk_ref, wv_ref):
        for start in range(0, weight_ref.shape[1], step):
            out_ref[:, base : base + step] = jnp.dot(
                tokens, weight_ref[:, start : start + step], preferred_element_type=F32
            )
            base += step


def sine_cosine(angle):
    turns = jnp.floor(angle * (2.0 / math.pi) + 0.5)
    rest = angle - turns * 1.5703125
    rest = rest - turns * 4.837512969970703125e-4
    rest = rest - turns * 7.54978995489188216e-8
    square = rest * rest
    sine = (-1.9515295891e-4 * square + 8.3321608736e-3) * square - 1.6666654611e-1
    sine = sine * square * rest + rest
    cosine = (2.443315711809948e-5 * square - 1.388731625493765e-3) * square
    cosine = (cosine + 4.166664568298827e-2) * square * square - 0.5 * square + 1.0
    quarter = turns.astype(jnp.int32) & 3
    odd = (quarter & 1) == 1
    sine, cosine = jnp.where(odd, cosine, sine), jnp.where(odd, sine, cosine)
    sine = jnp.where(quarter >= 2, -sine, sine)
    cosine = jnp.where(jnp.logical_or(quarter == 1, quarter == 2), -cosine, cosine)
    return sine, cosine


def angle_tables(shift, freq):
    angle = shift.astype(F32) * freq
    low = iota(angle.shape, 1) < HEAD_WIDTH // 2
    sine, cosine = sine_cosine(angle)
    return cosine, jnp.where(low, -sine, sine)


def rotated(vectors, cosine, sine):
    return vectors * cosine + pltpu.roll(vectors, HEAD_WIDTH // 2, 1) * sine


def tables_kernel(
    tiles,
    ranks,
    stretch_len,
    row_total,
    stretches_ref,
    offsets_ref,
    counts_ref,
    positions_ref,
    freq_ref,
    cos_ref,
    sin_ref,
    bias_ref,
    token_cos_ref,
    token_sin_ref,
):
    slot = lax.axis_index("slot")
    row = lax.axis_index("row")
    freq = freq_ref[...]
    count = counts_ref[slot]
    arriving = tiles
    slot_tiles = stretches_ref.shape[1]
    stretches = stretches_ref[pl.ds(slot, 1), :]
    owner, _ = divide(stretches, tiles)
    slots = arriving // ranks
    place, rank_wanted = divide(iota((arriving, slot_tiles), 0), ranks)
    bits, flip = jnp.zeros_like(place), jnp.zeros_like(place)
    for i, (first, second, other) in enumerate(arrivals(slots)):
        bits = jnp.where(place == i, for_row((first, second), row), bits)
        flip = jnp.where(place == i, other, flip)
    from_slot = slot ^ bits
    from_row = row ^ flip
    match = (owner == from_slot * row_total + from_row).astype(F32)
    rank = earlier_count(match)
    picked = jnp.where(rank == rank_wanted.astype(F32), match, 0.0)
    tile_ids = iota((1, slot_tiles), 1).astype(F32)
    tile = jnp.sum(picked * tile_ids, axis=1, keepdims=True)
    page, lane = divide(stretches, 128)
    in_lane = (iota((128, slot_tiles), 0) == lane).astype(F32).astype(BF16)
    upper, lower = divide(offsets_ref[...], 64)
    page_count = upper.shape[0]
    split = jnp.concatenate([upper, lower], axis=0).astype(F32).astype(BF16)
    split = jnp.dot(split, in_lane, preferred_element_type=F32)
    offset = split[:page_count] * 64.0 + split[page_count:]
    in_page = iota((page_count, slot_tiles), 0) == page
    offset = jnp.sum(jnp.where(in_page, offset, 0.0), axis=0, keepdims=True)
    shift = jnp.sum(picked * (tile_ids * stretch_len - offset), axis=1, keepdims=True)
    cosine, sine = angle_tables(shift, freq)
    local_keys = arriving * stretch_len
    spread = lambda x: jnp.broadcast_to(
        x[:, None, :], (arriving, stretch_len, x.shape[1])
    ).reshape(local_keys, x.shape[1])
    cos_ref[...] = spread(cosine)
    sin_ref[...] = spread(sine)
    token_total = positions_ref.shape[1]
    share = token_total // row_total
    positions = positions_ref[...]
    group = bias_ref.shape[1] // token_total
    query_positions = jnp.concatenate([positions] * group, axis=1)
    first = jnp.broadcast_to(tile * stretch_len, (arriving, 128))
    _, token = divide(iota((local_keys, 128), 0), stretch_len)
    key_positions = spread(first).astype(jnp.int32) + token
    redone = (key_positions[:, :token_total] == positions).astype(F32).astype(BF16)
    redone = jnp.dot(redone, jnp.ones((token_total, 128), BF16), preferred_element_type=F32)
    usable = jnp.logical_and(key_positions < count * stretch_len, redone == 0.0)
    key_positions = jnp.where(usable, key_positions, FAR)
    for start in range(0, bias_ref.shape[1], 128):
        cols = slice(start, start + 128)
        bias_ref[:local_keys, cols] = jnp.where(
            key_positions <= query_positions[:, cols], 0.0, NEGATIVE
        )
    square = iota((token_total, token_total), 0) == iota((token_total, token_total), 1)
    column = jnp.sum(
        jnp.where(square, positions.astype(F32), 0.0), axis=1, keepdims=True
    ).astype(jnp.int32)
    new_positions = of_row(column, row, share)
    new_usable = new_positions < count * stretch_len
    new_positions = jnp.where(new_usable, new_positions, FAR)
    bias_ref[local_keys:, :] = jnp.where(new_positions <= query_positions, 0.0, NEGATIVE)
    token_cos_ref[...], token_sin_ref[...] = angle_tables(column, freq)


def of_row(value, row, share):
    kept = value[:share]
    for r in range(1, value.shape[0] // share):
        kept = jnp.where(row == r, value[r * share : (r + 1) * share], kept)
    return kept


def block_parts(blocks, stretch_rows):
    return [(ref, at) for ref in blocks for at in range(0, ref.shape[0], 2 * stretch_rows)]


def keys_of(parts, stretch_rows, cols, cosine, sine):
    keys = jnp.concatenate([ref[at : at + stretch_rows, cols] for ref, at in parts], axis=0)
    return rotated(keys.astype(F32), cosine, sine).astype(BF16)


def values_of(parts, stretch_rows, cols):
    return [ref[at + stretch_rows : at + 2 * stretch_rows, cols] for ref, at in parts]


def scores_of(keys, queries, bias):
    nt = (((1,), (1,)), ((), ()))
    scores = lax.dot_general(keys, queries, nt, preferred_element_type=F32)
    return scores * (1.0 / math.sqrt(HEAD_WIDTH)) + bias


def queries_kernel(stretch_rows, *refs):
    *arrived, cos_ref, sin_ref, bias_ref, token_cos_ref, token_sin_ref, both_ref = refs[:-3]
    q_ref, scores_ref, values_ref = refs[-3:]
    parts = block_parts(arrived, stretch_rows)
    row = lax.axis_index("row")
    token_total = token_cos_ref.shape[0]
    local_keys = cos_ref.shape[0]
    share, count = values_ref.shape[0], len(parts) * stretch_rows
    query_rows = bias_ref.shape[1]
    group = query_rows // token_total
    key_columns = arrived[0].shape[1]
    key_heads = key_columns // HEAD_WIDTH
    query_columns = group * key_columns
    cosine, sine = cos_ref[:count, :], sin_ref[:count, :]
    token_cosine, token_sine = token_cos_ref[...], token_sin_ref[...]
    bias = jnp.concatenate([bias_ref[:count, :], bias_ref[local_keys:, :]], axis=0)

    def projected(start, width=HEAD_WIDTH):
        cols = slice(start, start + width)
        return both_ref[0, :, cols] + both_ref[1, :, cols]

    all_queries, all_scores = [], []
    for head in range(key_heads):
        at = head * HEAD_WIDTH
        queries = [
            rotated(projected((head * group + j) * HEAD_WIDTH), token_cosine, token_sine)
            for j in range(group)
        ]
        queries = jnp.concatenate(queries, axis=0).astype(BF16)
        new_keys = rotated(projected(query_columns + at), token_cosine, token_sine)
        keys = keys_of(parts, stretch_rows, slice(at, at + HEAD_WIDTH), cosine, sine)
        keys = jnp.concatenate([keys, of_row(new_keys, row, share).astype(BF16)], axis=0)
        all_queries.append(queries)
        all_scores.append(scores_of(keys, queries, bias))
    new_values = projected(query_columns + key_columns, key_columns)
    values_ref[...] = of_row(new_values, row, share).astype(BF16)
    for head in range(key_heads):
        q_ref[head * query_rows : (head + 1) * query_rows, :] = all_queries[head]
        scores_ref[head * (count + share) : (head + 1) * (count + share), :] = all_scores[head]


def attend_kernel(stretch_rows, first_blocks, *refs):
    *arrived, cos_ref, sin_ref, bias_ref, q_ref, scores_ref, values_ref, out_ref, send_ref = refs
    first = block_parts(arrived[:first_blocks], stretch_rows)
    later = block_parts(arrived[first_blocks:], stretch_rows)
    count, local_keys = len(first) * stretch_rows, cos_ref.shape[0]
    known = count + values_ref.shape[0]
    query_rows = bias_ref.shape[1]
    key_heads = arrived[0].shape[1] // HEAD_WIDTH
    cosine, sine = cos_ref[count:, :], sin_ref[count:, :]
    bias = bias_ref[count:local_keys, :]
    all_scores, all_values = [], []
    for head in range(key_heads):
        cols = slice(head * HEAD_WIDTH, (head + 1) * HEAD_WIDTH)
        keys = keys_of(later, stretch_rows, cols, cosine, sine)
        queries = q_ref[head * query_rows : (head + 1) * query_rows, :]
        scores = [scores_ref[head * known : (head + 1) * known, :]]
        scores.append(scores_of(keys, queries, bias))
        all_scores.append(jnp.concatenate(scores, axis=0))
        values = values_of(first, stretch_rows, cols) + [values_ref[:, cols]]
        values += values_of(later, stretch_rows, cols)
        all_values.append(jnp.concatenate(values, axis=0))
    all_probs = []
    stats = []
    for scores in all_scores:
        peak = jnp.max(scores, axis=0, keepdims=True)
        probs = jnp.exp(scores - peak)
        stats.append((peak, jnp.sum(probs, axis=0, keepdims=True)))
        all_probs.append(probs.astype(BF16))
    stats = jnp.concatenate([x[0] for x in stats] + [x[1] for x in stats], axis=0)
    base = key_heads * HEAD_WIDTH
    out_ref[base:, :] = stats
    for part in range(3):
        term = stats.astype(BF16)
        at = base + 16 * part
        send_ref[at : at + 16, :] = jnp.concatenate(
            [term.astype(F32), jnp.zeros_like(stats)], axis=0
        ).astype(BF16)
        stats = stats - term.astype(F32)
    for head in range(key_heads):
        weighted = lax.dot_general(
            all_values[head], all_probs[head], (((0,), (0,)), ((), ())), preferred_element_type=F32
        )
        rows = slice(head * HEAD_WIDTH, (head + 1) * HEAD_WIDTH)
        out_ref[rows, :] = weighted
        send_ref[rows, :] = weighted.astype(BF16)


def output_kernel(step, key_heads, own_ref, other_ref, w_ref, keep_ref, send_ref, attended):
    token_total = attended.shape[0]
    group = own_ref.shape[1] // token_total
    base = key_heads * HEAD_WIDTH
    results = []
    own_stats = own_ref[base:, :]
    terms = [
        other_ref[base + 16 * part : base + 16 * (part + 1), :].astype(F32) for part in range(3)
    ]
    other_stats = (terms[0] + terms[1] + terms[2])[: 2 * key_heads]
    peaks = jnp.maximum(own_stats[:key_heads], other_stats[:key_heads])
    own_scales = jnp.exp(own_stats[:key_heads] - peaks)
    other_scales = jnp.exp(other_stats[:key_heads] - peaks)
    totals = own_stats[key_heads:] * own_scales + other_stats[key_heads:] * other_scales
    for head in range(key_heads):
        rows = slice(head * HEAD_WIDTH, (head + 1) * HEAD_WIDTH)
        at = slice(head, head + 1)
        total = totals[at]
        weighted = own_ref[rows, :] * own_scales[at]
        weighted += other_ref[rows, :].astype(F32) * other_scales[at]
        results.append(jnp.transpose(weighted / total).astype(BF16))
    tokens = jnp.concatenate(
        [
            result[j * token_total : (j + 1) * token_total]
            for result in results
            for j in range(group)
        ],
        axis=1,
    )
    share = keep_ref.shape[0]
    first = lax.axis_index("col") == 0
    for start in range(0, w_ref.shape[1], step):
        cols = slice(start, start + step)
        part = jnp.dot(tokens, w_ref[:, cols], preferred_element_type=F32)
        keep_ref[:, cols] = jnp.where(first, part[:share], part[share:])
        send_ref[:, cols] = jnp.where(first, part[share:], part[:share]).astype(BF16)


def cost(us):
    return pl.CostEstimate(flops=us * 1_000_000_000, bytes_accessed=1000, transcendentals=0)


def in_hbm(value):
    return pltpu.with_memory_space_constraint(value, pltpu.HBM)


def merge_kernel(count, near_count, *refs):
    kept, given, outs = refs[:count], refs[count], refs[count + 1 + near_count :]
    rows = kept[0].shape[0]
    for i in range(count):
        outs[i][:rows] = kept[i][...]
        outs[i][rows:] = given[i * rows : (i + 1) * rows]


def merge(kept, given, near, grant):
    count, near_count = len(kept), len(near)
    block = kept[0]
    results = pl.pallas_call(
        functools.partial(merge_kernel, count, near_count),
        out_shape=[jax.ShapeDtypeStruct((2 * block.shape[0], block.shape[1]), BF16)] * count
        + [jax.ShapeDtypeStruct(block.shape, BF16)] * near_count,
        in_specs=[VMEM] * (count + 1) + [ANY] * near_count,
        out_specs=[VMEM] * count + [ANY] * near_count,
        input_output_aliases={count + 1 + i: count + i for i in range(near_count)},
        compiler_params=params(grant),
        cost_estimate=cost(0),
        name="merge",
    )(*kept, given, *near)
    return *results[:count], results[count:]


def params(mib):
    return pltpu.CompilerParams(vmem_limit_bytes=mib * MIB)


def on_device(
    hidden,
    w_query,
    key_weight,
    value_weight,
    w_out,
    kv_store,
    stretch_offset,
    tile_stretch,
    slot_count,
    recomp_pos,
):
    slot_total = lax.axis_size("slot")
    row_total = lax.axis_size("row")
    tiles, _, stretch_len, key_columns = kv_store.shape
    slot_tiles = tile_stretch.shape[1]
    ranks = slot_tiles // (slot_total * row_total)
    width = hidden.shape[2]
    token_total = hidden.shape[1]
    query_columns = w_query.shape[1]
    key_heads = key_columns // HEAD_WIDTH
    group = query_columns // key_columns
    query_rows = group * token_total
    per_slot = ranks * 2 * stretch_len
    local_keys = tiles * stretch_len
    share = token_total // row_total
    all_keys = local_keys + share
    swap = [(0, 1), (1, 0)]
    grant = 16 if slot_total <= 8 else 40

    freq = np.arange(HEAD_WIDTH // 2, dtype=np.float64)
    freq = (ROPE_BASE ** (-2.0 * freq / HEAD_WIDTH)).astype(np.float32)
    freq = jnp.asarray(np.concatenate([freq, freq])[None, :])

    store_shape = (tiles * 2 * stretch_len, key_columns)
    step = key_columns
    direct, shared = exchanges(slot_total)
    block = jax.ShapeDtypeStruct((per_slot, key_columns), BF16)
    *outgoing, give = pl.pallas_call(
        functools.partial(pack_kernel, tiles, ranks, stretch_len),
        out_shape=[block] * (len(direct) + 1 + len(shared))
        + [jax.ShapeDtypeStruct((len(shared) * per_slot, key_columns), BF16)],
        in_specs=[HBM, HBM],
        out_specs=[VMEM] * (len(direct) + len(shared) + 2),
        scratch_shapes=[
            pltpu.VMEM(tile_stretch.shape, jnp.int32),
            pltpu.VMEM(store_shape, BF16),
            pltpu.VMEM((slot_total, 128), F32),
            pltpu.SemaphoreType.DMA((2,)),
        ],
        compiler_params=params(grant),
        cost_estimate=cost(8),
        name="pack",
    )(in_hbm(tile_stretch), in_hbm(kv_store.reshape(store_shape)))
    own_block, kept = outgoing[len(direct)], outgoing[len(direct) + 1 :]
    given = lax.ppermute(give, "row", swap)
    early = [True for k in direct]
    late_blocks = [outgoing[i] for i in range(len(direct)) if not early[i]]
    *merged, late_blocks = merge(kept, given, late_blocks, grant)
    late_blocks = iter(late_blocks)
    arrived = []
    for i, k in enumerate(direct):
        sent = outgoing[i] if early[i] else next(late_blocks)
        arrived.append(lax.ppermute(sent, "slot", [(s, s ^ k) for s in range(slot_total)]))
    arrived.append(own_block)
    for sent, pair in zip(merged, shared):
        pairs = [
            (s * row_total + r, (s ^ pair[r]) * row_total + r)
            for s in range(slot_total)
            for r in range(row_total)
        ]
        arrived.append(lax.ppermute(sent, ("slot", "row"), pairs))

    projected = pl.pallas_call(
        functools.partial(project_kernel, step),
        out_shape=jax.ShapeDtypeStruct((token_total, query_columns + 2 * key_columns), F32),
        in_specs=[ANY] + [VMEM] * 4,
        out_specs=VMEM,
        compiler_params=params(grant),
        cost_estimate=cost(0),
        name="project",
    )(merged[0], hidden[0], w_query, key_weight, value_weight)
    both = lax.all_gather(projected, "row")

    tables = pl.pallas_call(
        functools.partial(tables_kernel, tiles, ranks, stretch_len, row_total),
        out_shape=(
            jax.ShapeDtypeStruct((local_keys, HEAD_WIDTH), F32),
            jax.ShapeDtypeStruct((local_keys, HEAD_WIDTH), F32),
            jax.ShapeDtypeStruct((all_keys, query_rows), F32),
            jax.ShapeDtypeStruct((token_total, HEAD_WIDTH), F32),
            jax.ShapeDtypeStruct((token_total, HEAD_WIDTH), F32),
        ),
        in_specs=[VMEM, VMEM, SMEM, VMEM, VMEM],
        out_specs=(VMEM,) * 5,
        compiler_params=params(grant),
        cost_estimate=cost(0),
        name="tables",
    )(tile_stretch, stretch_offset.reshape(-1, 128), slot_count, recomp_pos, freq)

    first_blocks = len(direct) + 1
    known = first_blocks * ranks * stretch_len + share
    queries, scores, new_values = pl.pallas_call(
        functools.partial(queries_kernel, ranks * stretch_len),
        out_shape=(
            jax.ShapeDtypeStruct((key_heads * query_rows, HEAD_WIDTH), BF16),
            jax.ShapeDtypeStruct((key_heads * known, query_rows), F32),
            jax.ShapeDtypeStruct((share, key_columns), BF16),
        ),
        in_specs=[VMEM] * (first_blocks + 6),
        out_specs=(VMEM,) * 3,
        compiler_params=params(grant),
        cost_estimate=cost(0),
        name="queries",
    )(*arrived[:first_blocks], *tables, both)
    partial, to_swap = pl.pallas_call(
        functools.partial(attend_kernel, ranks * stretch_len, first_blocks),
        out_shape=(
            jax.ShapeDtypeStruct((key_heads * HEAD_WIDTH + 2 * key_heads, query_rows), F32),
            jax.ShapeDtypeStruct((key_heads * HEAD_WIDTH + 3 * 16, query_rows), BF16),
        ),
        in_specs=[VMEM] * (len(direct) + len(shared) + 7),
        out_specs=(VMEM, VMEM),
        compiler_params=params(grant),
        cost_estimate=cost(0),
        name="attend",
    )(*arrived, *tables[:3], queries, scores, new_values)
    partial_other = lax.ppermute(to_swap, "row", swap)

    out_columns = w_out.shape[1]
    out_share = token_total // lax.axis_size("col")
    keep, send = pl.pallas_call(
        functools.partial(output_kernel, out_columns, key_heads),
        out_shape=(
            jax.ShapeDtypeStruct((out_share, out_columns), F32),
            jax.ShapeDtypeStruct((out_share, out_columns), BF16),
        ),
        in_specs=[VMEM, VMEM, VMEM],
        out_specs=(VMEM, VMEM),
        scratch_shapes=[pltpu.VMEM((token_total, query_columns), BF16)],
        compiler_params=params(grant),
        name="output",
    )(partial, partial_other, w_out)
    received = lax.ppermute(send, "col", swap)
    return (keep + received.astype(F32)).astype(BF16)[None]


def solution(mesh):
    return jax.shard_map(
        on_device,
        mesh=mesh,
        in_specs=(
            P("slot", None, "row"),
            P("row", "col"),
            P("row", "col"),
            P("row", "col"),
            P("col", "row"),
            P(("slot", "row"), None, None, "col"),
            P(),
            P(),
            P(),
            P("slot", None),
        ),
        out_specs=P("slot", "col", "row"),
        check_vma=False,
    )
```

```python
import functools
import math

import jax
import jax.numpy as jnp
import numpy as np
from jax import lax
from jax.experimental import pallas as pl
from jax.experimental.pallas import tpu as pltpu
from jax.sharding import PartitionSpec as P

HEAD_WIDTH = 128
NEGATIVE = -1e30
ROPE_BASE = 500000.0
MIB = 1024 * 1024
FAR = 1 << 28
F32 = jnp.float32
BF16 = jnp.bfloat16
VMEM = pl.BlockSpec(memory_space=pltpu.VMEM)
ANY = pl.BlockSpec(memory_space=pl.ANY)
HBM = pl.BlockSpec(memory_space=pltpu.HBM)
SMEM = pl.BlockSpec(memory_space=pltpu.SMEM)


def exchanges(slots):
    if slots == 8:
        return [4, 6, 3], [(2, 1), (7, 5)]
    return [1], [(k, k - 1) for k in range(slots - 1, 1, -2)]


def for_row(pair, row):
    return pair[1] + (1 - row) * (pair[0] - pair[1])


def arrivals(slots):
    direct, shared = exchanges(slots)
    blocks = [(k, k, 0) for k in direct + [0]]
    return blocks + [(*pair, flip) for pair in shared for flip in (0, 1)]


def iota(shape, dim):
    return lax.broadcasted_iota(jnp.int32, shape, dim)


def divide(value, by):
    if by & (by - 1) == 0:
        shift = by.bit_length() - 1
        return lax.shift_right_logical(value, jnp.full_like(value, shift)), value & (by - 1)
    quotient = jnp.floor((value.astype(F32) + 0.5) * (1.0 / by)).astype(jnp.int32)
    return quotient, value - quotient * by


def earlier_count(flags):
    n = flags.shape[1]
    before = (iota((n, n), 0) < iota((n, n), 1)).astype(BF16)
    return jnp.dot(flags.astype(BF16), before, preferred_element_type=F32)


def pack_kernel(tiles, ranks, stretch_len, stretches_hbm, store_hbm, *refs):
    *outs, give_ref, stretches_ref, store_ref, ids_ref, sems = refs
    get_store = pltpu.make_async_copy(store_hbm, store_ref, sems.at[0])
    get_stretches = pltpu.make_async_copy(stretches_hbm, stretches_ref, sems.at[1])
    get_stretches.start()
    get_store.start()
    slot = lax.axis_index("slot")
    row = lax.axis_index("row")
    own = slot * lax.axis_size("row") + row
    slots, slot_tiles = stretches_ref.shape
    per_slot = ranks * stretch_len
    rows = slots * per_slot
    part, token = divide(iota((rows, 128), 0), stretch_len)
    _, rank_of_row = divide(part, ranks)
    rank_here = iota((rows, 128), 1) == rank_of_row
    get_stretches.wait()
    owner, local = divide(stretches_ref[...], tiles)
    mine = (owner == own).astype(F32)
    rank = earlier_count(mine)
    lane = iota((slots, 128), 1)
    ids = jnp.zeros((slots, 128), F32)
    for k in range(ranks):
        picked = jnp.where(rank == k, mine * local.astype(F32), 0.0)
        ids = jnp.where(lane == k, jnp.sum(picked, axis=1, keepdims=True), ids)
    ids_ref[...] = ids
    direct, shared = exchanges(slots)
    ids = jnp.concatenate(
        [
            jnp.broadcast_to(ids_ref[pl.ds(slot ^ k, 1), :], (per_slot, 128))
            for k in direct + [0] + [for_row(pair, r) for r in (row, 1 - row) for pair in shared]
        ],
        axis=0,
    )
    stretch = jnp.sum(jnp.where(rank_here, ids, 0.0), axis=1, keepdims=True).astype(jnp.int32)
    source = stretch * stretch_len + token[:, :1]
    store_rows = tiles * stretch_len
    pick = (iota((rows, store_rows), 1) == source).astype(F32).astype(BF16)
    get_store.wait()
    columns = store_ref.shape[1]
    store = store_ref[...].astype(F32).reshape(tiles, 2, stretch_len, columns)
    keys, values = [
        jnp.dot(
            pick,
            store[:, kind].reshape(store_rows, columns).astype(BF16),
            preferred_element_type=F32,
        ).astype(BF16)
        for kind in range(2)
    ]
    for i, out_ref in enumerate(outs):
        out_ref[:per_slot] = keys[i * per_slot : (i + 1) * per_slot]
        out_ref[per_slot:] = values[i * per_slot : (i + 1) * per_slot]
    for i in range(len(shared)):
        at = (len(outs) + i) * per_slot
        give_ref[2 * i * per_slot : (2 * i + 1) * per_slot] = keys[at : at + per_slot]
        give_ref[(2 * i + 1) * per_slot : (2 * i + 2) * per_slot] = values[at : at + per_slot]


def project_kernel(step, after_ref, hidden_ref, wq_ref, wk_ref, wv_ref, out_ref):
    tokens = hidden_ref[...]
    base = 0
    for weight_ref in (wq_ref, wk_ref, wv_ref):
        for start in range(0, weight_ref.shape[1], step):
            out_ref[:, base : base + step] = jnp.dot(
                tokens, weight_ref[:, start : start + step], preferred_element_type=F32
            )
            base += step


def sine_cosine(angle):
    turns = jnp.floor(angle * (2.0 / math.pi) + 0.5)
    rest = angle - turns * 1.5703125
    rest = rest - turns * 4.837512969970703125e-4
    rest = rest - turns * 7.54978995489188216e-8
    square = rest * rest
    sine = (-1.9515295891e-4 * square + 8.3321608736e-3) * square - 1.6666654611e-1
    sine = sine * square * rest + rest
    cosine = (2.443315711809948e-5 * square - 1.388731625493765e-3) * square
    cosine = (cosine + 4.166664568298827e-2) * square * square - 0.5 * square + 1.0
    quarter = turns.astype(jnp.int32) & 3
    odd = (quarter & 1) == 1
    sine, cosine = jnp.where(odd, cosine, sine), jnp.where(odd, sine, cosine)
    sine = jnp.where(quarter >= 2, -sine, sine)
    cosine = jnp.where(jnp.logical_or(quarter == 1, quarter == 2), -cosine, cosine)
    return sine, cosine


def angle_tables(shift, freq):
    angle = shift.astype(F32) * freq
    low = iota(angle.shape, 1) < HEAD_WIDTH // 2
    sine, cosine = sine_cosine(angle)
    return cosine, jnp.where(low, -sine, sine)


def rotated(vectors, cosine, sine):
    return vectors * cosine + pltpu.roll(vectors, HEAD_WIDTH // 2, 1) * sine


def tables_kernel(
    tiles,
    ranks,
    stretch_len,
    row_total,
    stretches_ref,
    offsets_ref,
    counts_ref,
    positions_ref,
    freq_ref,
    cos_ref,
    sin_ref,
    bias_ref,
    token_cos_ref,
    token_sin_ref,
):
    slot = lax.axis_index("slot")
    row = lax.axis_index("row")
    freq = freq_ref[...]
    count = counts_ref[slot]
    arriving = tiles
    slot_tiles = stretches_ref.shape[1]
    stretches = stretches_ref[pl.ds(slot, 1), :]
    owner, _ = divide(stretches, tiles)
    slots = arriving // ranks
    place, rank_wanted = divide(iota((arriving, slot_tiles), 0), ranks)
    bits, flip = jnp.zeros_like(place), jnp.zeros_like(place)
    for i, (first, second, other) in enumerate(arrivals(slots)):
        bits = jnp.where(place == i, for_row((first, second), row), bits)
        flip = jnp.where(place == i, other, flip)
    from_slot = slot ^ bits
    from_row = row ^ flip
    match = (owner == from_slot * row_total + from_row).astype(F32)
    rank = earlier_count(match)
    picked = jnp.where(rank == rank_wanted.astype(F32), match, 0.0)
    tile_ids = iota((1, slot_tiles), 1).astype(F32)
    tile = jnp.sum(picked * tile_ids, axis=1, keepdims=True)
    page, lane = divide(stretches, 128)
    in_lane = (iota((128, slot_tiles), 0) == lane).astype(F32).astype(BF16)
    upper, lower = divide(offsets_ref[...], 64)
    page_count = upper.shape[0]
    split = jnp.concatenate([upper, lower], axis=0).astype(F32).astype(BF16)
    split = jnp.dot(split, in_lane, preferred_element_type=F32)
    offset = split[:page_count] * 64.0 + split[page_count:]
    in_page = iota((page_count, slot_tiles), 0) == page
    offset = jnp.sum(jnp.where(in_page, offset, 0.0), axis=0, keepdims=True)
    shift = jnp.sum(picked * (tile_ids * stretch_len - offset), axis=1, keepdims=True)
    cosine, sine = angle_tables(shift, freq)
    local_keys = arriving * stretch_len
    spread = lambda x: jnp.broadcast_to(
        x[:, None, :], (arriving, stretch_len, x.shape[1])
    ).reshape(local_keys, x.shape[1])
    cos_ref[...] = spread(cosine)
    sin_ref[...] = spread(sine)
    token_total = positions_ref.shape[1]
    share = token_total // row_total
    positions = positions_ref[...]
    group = bias_ref.shape[1] // token_total
    query_positions = jnp.concatenate([positions] * group, axis=1)
    first = jnp.broadcast_to(tile * stretch_len, (arriving, 128))
    _, token = divide(iota((local_keys, 128), 0), stretch_len)
    key_positions = spread(first).astype(jnp.int32) + token
    redone = (key_positions[:, :token_total] == positions).astype(F32).astype(BF16)
    redone = jnp.dot(redone, jnp.ones((token_total, 128), BF16), preferred_element_type=F32)
    usable = jnp.logical_and(key_positions < count * stretch_len, redone == 0.0)
    key_positions = jnp.where(usable, key_positions, FAR)
    for start in range(0, bias_ref.shape[1], 128):
        cols = slice(start, start + 128)
        bias_ref[:local_keys, cols] = jnp.where(
            key_positions <= query_positions[:, cols], 0.0, NEGATIVE
        )
    square = iota((token_total, token_total), 0) == iota((token_total, token_total), 1)
    column = jnp.sum(
        jnp.where(square, positions.astype(F32), 0.0), axis=1, keepdims=True
    ).astype(jnp.int32)
    new_positions = of_row(column, row, share)
    new_usable = new_positions < count * stretch_len
    new_positions = jnp.where(new_usable, new_positions, FAR)
    bias_ref[local_keys:, :] = jnp.where(new_positions <= query_positions, 0.0, NEGATIVE)
    token_cos_ref[...], token_sin_ref[...] = angle_tables(column, freq)


def of_row(value, row, share):
    kept = value[:share]
    for r in range(1, value.shape[0] // share):
        kept = jnp.where(row == r, value[r * share : (r + 1) * share], kept)
    return kept


def block_parts(blocks, stretch_rows):
    return [(ref, at) for ref in blocks for at in range(0, ref.shape[0], 2 * stretch_rows)]


def keys_of(parts, stretch_rows, cols, cosine, sine):
    keys = jnp.concatenate([ref[at : at + stretch_rows, cols] for ref, at in parts], axis=0)
    return rotated(keys.astype(F32), cosine, sine).astype(BF16)


def values_of(parts, stretch_rows, cols):
    return [ref[at + stretch_rows : at + 2 * stretch_rows, cols] for ref, at in parts]


def scores_of(keys, queries, bias):
    nt = (((1,), (1,)), ((), ()))
    scores = lax.dot_general(keys, queries, nt, preferred_element_type=F32)
    return scores * (1.0 / math.sqrt(HEAD_WIDTH)) + bias


def queries_kernel(stretch_rows, *refs):
    *arrived, cos_ref, sin_ref, bias_ref, token_cos_ref, token_sin_ref, both_ref = refs[:-3]
    q_ref, scores_ref, values_ref = refs[-3:]
    parts = block_parts(arrived, stretch_rows)
    row = lax.axis_index("row")
    token_total = token_cos_ref.shape[0]
    local_keys = cos_ref.shape[0]
    share, count = values_ref.shape[0], len(parts) * stretch_rows
    query_rows = bias_ref.shape[1]
    group = query_rows // token_total
    key_columns = arrived[0].shape[1]
    key_heads = key_columns // HEAD_WIDTH
    query_columns = group * key_columns
    cosine, sine = cos_ref[:count, :], sin_ref[:count, :]
    token_cosine, token_sine = token_cos_ref[...], token_sin_ref[...]
    bias = jnp.concatenate([bias_ref[:count, :], bias_ref[local_keys:, :]], axis=0)

    def projected(start, width=HEAD_WIDTH):
        cols = slice(start, start + width)
        return both_ref[0, :, cols] + both_ref[1, :, cols]

    all_queries, all_scores = [], []
    for head in range(key_heads):
        at = head * HEAD_WIDTH
        queries = [
            rotated(projected((head * group + j) * HEAD_WIDTH), token_cosine, token_sine)
            for j in range(group)
        ]
        queries = jnp.concatenate(queries, axis=0).astype(BF16)
        new_keys = rotated(projected(query_columns + at), token_cosine, token_sine)
        keys = keys_of(parts, stretch_rows, slice(at, at + HEAD_WIDTH), cosine, sine)
        keys = jnp.concatenate([keys, of_row(new_keys, row, share).astype(BF16)], axis=0)
        all_queries.append(queries)
        all_scores.append(scores_of(keys, queries, bias))
    new_values = projected(query_columns + key_columns, key_columns)
    values_ref[...] = of_row(new_values, row, share).astype(BF16)
    for head in range(key_heads):
        q_ref[head * query_rows : (head + 1) * query_rows, :] = all_queries[head]
        scores_ref[head * (count + share) : (head + 1) * (count + share), :] = all_scores[head]


def attend_kernel(stretch_rows, first_blocks, *refs):
    *arrived, cos_ref, sin_ref, bias_ref, q_ref, scores_ref, values_ref, out_ref, send_ref = refs
    first = block_parts(arrived[:first_blocks], stretch_rows)
    later = block_parts(arrived[first_blocks:], stretch_rows)
    count, local_keys = len(first) * stretch_rows, cos_ref.shape[0]
    known = count + values_ref.shape[0]
    query_rows = bias_ref.shape[1]
    key_heads = arrived[0].shape[1] // HEAD_WIDTH
    cosine, sine = cos_ref[count:, :], sin_ref[count:, :]
    bias = bias_ref[count:local_keys, :]
    all_scores, all_values = [], []
    for head in range(key_heads):
        cols = slice(head * HEAD_WIDTH, (head + 1) * HEAD_WIDTH)
        keys = keys_of(later, stretch_rows, cols, cosine, sine)
        queries = q_ref[head * query_rows : (head + 1) * query_rows, :]
        scores = [scores_ref[head * known : (head + 1) * known, :]]
        scores.append(scores_of(keys, queries, bias))
        all_scores.append(jnp.concatenate(scores, axis=0))
        values = values_of(first, stretch_rows, cols) + [values_ref[:, cols]]
        values += values_of(later, stretch_rows, cols)
        all_values.append(jnp.concatenate(values, axis=0))
    all_probs = []
    stats = []
    for scores in all_scores:
        peak = jnp.max(scores, axis=0, keepdims=True)
        probs = jnp.exp(scores - peak)
        stats.append((peak, jnp.sum(probs, axis=0, keepdims=True)))
        all_probs.append(probs.astype(BF16))
    stats = jnp.concatenate([x[0] for x in stats] + [x[1] for x in stats], axis=0)
    base = key_heads * HEAD_WIDTH
    out_ref[base:, :] = stats
    for part in range(3):
        term = stats.astype(BF16)
        at = base + 16 * part
        send_ref[at : at + 16, :] = jnp.concatenate(
            [term.astype(F32), jnp.zeros_like(stats)], axis=0
        ).astype(BF16)
        stats = stats - term.astype(F32)
    for head in range(key_heads):
        weighted = lax.dot_general(
            all_values[head], all_probs[head], (((0,), (0,)), ((), ())), preferred_element_type=F32
        )
        rows = slice(head * HEAD_WIDTH, (head + 1) * HEAD_WIDTH)
        out_ref[rows, :] = weighted
        send_ref[rows, :] = weighted.astype(BF16)


def output_kernel(key_heads, own_ref, other_ref, w_ref, keep_ref, send_ref):
    token_total = keep_ref.shape[0] * lax.axis_size("col")
    group = own_ref.shape[1] // token_total
    base = key_heads * HEAD_WIDTH
    results = []
    own_stats = own_ref[base:, :]
    terms = [
        other_ref[base + 16 * part : base + 16 * (part + 1), :].astype(F32) for part in range(3)
    ]
    other_stats = (terms[0] + terms[1] + terms[2])[: 2 * key_heads]
    peaks = jnp.maximum(own_stats[:key_heads], other_stats[:key_heads])
    own_scales = jnp.exp(own_stats[:key_heads] - peaks)
    other_scales = jnp.exp(other_stats[:key_heads] - peaks)
    totals = own_stats[key_heads:] * own_scales + other_stats[key_heads:] * other_scales
    for head in range(key_heads):
        rows = slice(head * HEAD_WIDTH, (head + 1) * HEAD_WIDTH)
        at = slice(head, head + 1)
        total = totals[at]
        weighted = own_ref[rows, :] * own_scales[at]
        weighted += other_ref[rows, :].astype(F32) * other_scales[at]
        results.append(jnp.transpose(weighted / total).astype(BF16))
    tokens = jnp.concatenate(
        [
            result[j * token_total : (j + 1) * token_total]
            for result in results
            for j in range(group)
        ],
        axis=1,
    )
    share = keep_ref.shape[0]
    first = lax.axis_index("col") == 0
    part = jnp.dot(tokens, w_ref[...], preferred_element_type=F32)
    keep_ref[...] = jnp.where(first, part[:share], part[share:])
    send_ref[...] = jnp.where(first, part[share:], part[:share]).astype(BF16)


def cost(us):
    return pl.CostEstimate(flops=us * 1_000_000_000, bytes_accessed=1000, transcendentals=0)


def in_hbm(value):
    return pltpu.with_memory_space_constraint(value, pltpu.HBM)


def merge_kernel(*refs):
    count = len(refs) // 2
    kept, given, outs = refs[:count], refs[count], refs[count + 1 :]
    rows = kept[0].shape[0]
    for i in range(count):
        outs[i][:rows] = kept[i][...]
        outs[i][rows:] = given[i * rows : (i + 1) * rows]


def merge(kept, given, grant):
    rows, columns = kept[0].shape
    return pl.pallas_call(
        merge_kernel,
        out_shape=[jax.ShapeDtypeStruct((2 * rows, columns), BF16)] * len(kept),
        in_specs=[VMEM] * (len(kept) + 1),
        out_specs=[VMEM] * len(kept),
        compiler_params=params(grant),
        cost_estimate=cost(0),
        name="merge",
    )(*kept, given)


def params(mib):
    return pltpu.CompilerParams(vmem_limit_bytes=mib * MIB)


def on_device(
    hidden,
    w_query,
    key_weight,
    value_weight,
    w_out,
    kv_store,
    stretch_offset,
    tile_stretch,
    slot_count,
    recomp_pos,
):
    slot_total = lax.axis_size("slot")
    row_total = lax.axis_size("row")
    tiles, _, stretch_len, key_columns = kv_store.shape
    slot_tiles = tile_stretch.shape[1]
    ranks = slot_tiles // (slot_total * row_total)
    token_total = hidden.shape[1]
    query_columns = w_query.shape[1]
    key_heads = key_columns // HEAD_WIDTH
    group = query_columns // key_columns
    query_rows = group * token_total
    per_slot = ranks * 2 * stretch_len
    local_keys = tiles * stretch_len
    share = token_total // row_total
    all_keys = local_keys + share
    swap = [(0, 1), (1, 0)]
    grant = 16 if slot_total <= 8 else 40

    freq = np.arange(HEAD_WIDTH // 2, dtype=np.float64)
    freq = (ROPE_BASE ** (-2.0 * freq / HEAD_WIDTH)).astype(np.float32)
    freq = jnp.asarray(np.concatenate([freq, freq])[None, :])

    store_shape = (tiles * 2 * stretch_len, key_columns)
    step = key_columns
    direct, shared = exchanges(slot_total)
    block = jax.ShapeDtypeStruct((per_slot, key_columns), BF16)
    *outgoing, give = pl.pallas_call(
        functools.partial(pack_kernel, tiles, ranks, stretch_len),
        out_shape=[block] * (len(direct) + 1 + len(shared))
        + [jax.ShapeDtypeStruct((len(shared) * per_slot, key_columns), BF16)],
        in_specs=[HBM, HBM],
        out_specs=[VMEM] * (len(direct) + len(shared) + 2),
        scratch_shapes=[
            pltpu.VMEM(tile_stretch.shape, jnp.int32),
            pltpu.VMEM(store_shape, BF16),
            pltpu.VMEM((slot_total, 128), F32),
            pltpu.SemaphoreType.DMA((2,)),
        ],
        compiler_params=params(grant),
        cost_estimate=cost(8),
        name="pack",
    )(in_hbm(tile_stretch), in_hbm(kv_store.reshape(store_shape)))
    own_block, kept = outgoing[len(direct)], outgoing[len(direct) + 1 :]
    given = lax.ppermute(give, "row", swap)
    merged = merge(kept, given, grant)
    arrived = [
        lax.ppermute(block, "slot", [(s, s ^ k) for s in range(slot_total)])
        for block, k in zip(outgoing, direct)
    ]
    arrived.append(own_block)
    for sent, pair in zip(merged, shared):
        pairs = [
            (s * row_total + r, (s ^ pair[r]) * row_total + r)
            for s in range(slot_total)
            for r in range(row_total)
        ]
        arrived.append(lax.ppermute(sent, ("slot", "row"), pairs))

    projected = pl.pallas_call(
        functools.partial(project_kernel, step),
        out_shape=jax.ShapeDtypeStruct((token_total, query_columns + 2 * key_columns), F32),
        in_specs=[ANY] + [VMEM] * 4,
        out_specs=VMEM,
        compiler_params=params(grant),
        cost_estimate=cost(0),
        name="project",
    )(merged[0], hidden[0], w_query, key_weight, value_weight)
    both = lax.all_gather(projected, "row")

    tables = pl.pallas_call(
        functools.partial(tables_kernel, tiles, ranks, stretch_len, row_total),
        out_shape=(
            jax.ShapeDtypeStruct((local_keys, HEAD_WIDTH), F32),
            jax.ShapeDtypeStruct((local_keys, HEAD_WIDTH), F32),
            jax.ShapeDtypeStruct((all_keys, query_rows), F32),
            jax.ShapeDtypeStruct((token_total, HEAD_WIDTH), F32),
            jax.ShapeDtypeStruct((token_total, HEAD_WIDTH), F32),
        ),
        in_specs=[VMEM, VMEM, SMEM, VMEM, VMEM],
        out_specs=(VMEM,) * 5,
        compiler_params=params(grant),
        cost_estimate=cost(0),
        name="tables",
    )(tile_stretch, stretch_offset.reshape(-1, 128), slot_count, recomp_pos, freq)

    first_blocks = len(direct) + 1
    known = first_blocks * ranks * stretch_len + share
    queries, scores, new_values = pl.pallas_call(
        functools.partial(queries_kernel, ranks * stretch_len),
        out_shape=(
            jax.ShapeDtypeStruct((key_heads * query_rows, HEAD_WIDTH), BF16),
            jax.ShapeDtypeStruct((key_heads * known, query_rows), F32),
            jax.ShapeDtypeStruct((share, key_columns), BF16),
        ),
        in_specs=[VMEM] * (first_blocks + 6),
        out_specs=(VMEM,) * 3,
        compiler_params=params(grant),
        cost_estimate=cost(0),
        name="queries",
    )(*arrived[:first_blocks], *tables, both)
    partial, to_swap = pl.pallas_call(
        functools.partial(attend_kernel, ranks * stretch_len, first_blocks),
        out_shape=(
            jax.ShapeDtypeStruct((key_heads * HEAD_WIDTH + 2 * key_heads, query_rows), F32),
            jax.ShapeDtypeStruct((key_heads * HEAD_WIDTH + 3 * 16, query_rows), BF16),
        ),
        in_specs=[VMEM] * (len(direct) + len(shared) + 7),
        out_specs=(VMEM, VMEM),
        compiler_params=params(grant),
        cost_estimate=cost(0),
        name="attend",
    )(*arrived, *tables[:3], queries, scores, new_values)
    partial_other = lax.ppermute(to_swap, "row", swap)

    out_columns = w_out.shape[1]
    out_share = token_total // lax.axis_size("col")
    keep, send = pl.pallas_call(
        functools.partial(output_kernel, key_heads),
        out_shape=(
            jax.ShapeDtypeStruct((out_share, out_columns), F32),
            jax.ShapeDtypeStruct((out_share, out_columns), BF16),
        ),
        in_specs=[VMEM, VMEM, VMEM],
        out_specs=(VMEM, VMEM),
        compiler_params=params(grant),
        name="output",
    )(partial, partial_other, w_out)
    received = lax.ppermute(send, "col", swap)
    return (keep + received.astype(F32)).astype(BF16)[None]


def solution(mesh):
    return jax.shard_map(
        on_device,
        mesh=mesh,
        in_specs=(
            P("slot", None, "row"),
            P("row", "col"),
            P("row", "col"),
            P("row", "col"),
            P("col", "row"),
            P(("slot", "row"), None, None, "col"),
            P(),
            P(),
            P(),
            P("slot", None),
        ),
        out_specs=P("slot", "col", "row"),
        check_vma=False,
    )
```

```python
import functools
import math

import jax
import jax.numpy as jnp
import numpy as np
from jax import lax
from jax.experimental import pallas as pl
from jax.experimental.pallas import tpu as pltpu
from jax.sharding import PartitionSpec as P

HEAD_WIDTH = 128
NEGATIVE = -1e30
ROPE_BASE = 500000.0
MIB = 1024 * 1024
FAR = 1 << 28
F32 = jnp.float32
BF16 = jnp.bfloat16
VMEM = pl.BlockSpec(memory_space=pltpu.VMEM)
ANY = pl.BlockSpec(memory_space=pl.ANY)
HBM = pl.BlockSpec(memory_space=pltpu.HBM)
SMEM = pl.BlockSpec(memory_space=pltpu.SMEM)


def exchanges(slots):
    if slots == 8:
        return [4, 6, 3], [(2, 1), (7, 5)]
    return [1], [(k, k - 1) for k in range(slots - 1, 1, -2)]


def for_row(pair, row):
    return pair[1] + (1 - row) * (pair[0] - pair[1])


def arrivals(slots):
    direct, shared = exchanges(slots)
    blocks = [(k, k, 0) for k in direct + [0]]
    return blocks + [(*pair, flip) for pair in shared for flip in (0, 1)]


def iota(shape, dim):
    return lax.broadcasted_iota(jnp.int32, shape, dim)


def divide(value, by):
    if by & (by - 1) == 0:
        shift = by.bit_length() - 1
        return lax.shift_right_logical(value, jnp.full_like(value, shift)), value & (by - 1)
    quotient = jnp.floor((value.astype(F32) + 0.5) * (1.0 / by)).astype(jnp.int32)
    return quotient, value - quotient * by


def earlier_count(flags):
    n = flags.shape[1]
    before = (iota((n, n), 0) < iota((n, n), 1)).astype(BF16)
    return jnp.dot(flags.astype(BF16), before, preferred_element_type=F32)


def pack_kernel(tiles, ranks, stretch_len, stretches_hbm, store_hbm, *refs):
    *outs, give_ref, stretches_ref, store_ref, ids_ref, sems = refs
    get_store = pltpu.make_async_copy(store_hbm, store_ref, sems.at[0])
    get_stretches = pltpu.make_async_copy(stretches_hbm, stretches_ref, sems.at[1])
    get_stretches.start(priority=1)
    get_store.start(priority=1)
    slot = lax.axis_index("slot")
    row = lax.axis_index("row")
    own = slot * lax.axis_size("row") + row
    slots, slot_tiles = stretches_ref.shape
    per_slot = ranks * stretch_len
    rows = slots * per_slot
    part, token = divide(iota((rows, 128), 0), stretch_len)
    _, rank_of_row = divide(part, ranks)
    rank_here = iota((rows, 128), 1) == rank_of_row
    get_stretches.wait()
    owner, local = divide(stretches_ref[...], tiles)
    mine = (owner == own).astype(F32)
    rank = earlier_count(mine)
    lane = iota((slots, 128), 1)
    ids = jnp.zeros((slots, 128), F32)
    for k in range(ranks):
        picked = jnp.where(rank == k, mine * local.astype(F32), 0.0)
        ids = jnp.where(lane == k, jnp.sum(picked, axis=1, keepdims=True), ids)
    ids_ref[...] = ids
    direct, shared = exchanges(slots)
    ids = jnp.concatenate(
        [
            jnp.broadcast_to(ids_ref[pl.ds(slot ^ k, 1), :], (per_slot, 128))
            for k in direct + [0] + [for_row(pair, r) for r in (row, 1 - row) for pair in shared]
        ],
        axis=0,
    )
    stretch = jnp.sum(jnp.where(rank_here, ids, 0.0), axis=1, keepdims=True).astype(jnp.int32)
    source = stretch * stretch_len + token[:, :1]
    store_rows = tiles * stretch_len
    pick = (iota((rows, store_rows), 1) == source).astype(F32).astype(BF16)
    get_store.wait()
    columns = store_ref.shape[1]
    store = store_ref[...].astype(F32).reshape(tiles, 2, stretch_len, columns)
    keys, values = [
        jnp.dot(
            pick,
            store[:, kind].reshape(store_rows, columns).astype(BF16),
            preferred_element_type=F32,
        ).astype(BF16)
        for kind in range(2)
    ]
    for i, out_ref in enumerate(outs):
        out_ref[:per_slot] = keys[i * per_slot : (i + 1) * per_slot]
        out_ref[per_slot:] = values[i * per_slot : (i + 1) * per_slot]
    for i in range(len(shared)):
        at = (len(outs) + i) * per_slot
        give_ref[2 * i * per_slot : (2 * i + 1) * per_slot] = keys[at : at + per_slot]
        give_ref[(2 * i + 1) * per_slot : (2 * i + 2) * per_slot] = values[at : at + per_slot]


def project_kernel(step, after_ref, hidden_ref, wq_ref, wk_ref, wv_ref, out_ref):
    tokens = hidden_ref[...]
    base = 0
    for weight_ref in (wq_ref, wk_ref, wv_ref):
        for start in range(0, weight_ref.shape[1], step):
            out_ref[:, base : base + step] = jnp.dot(
                tokens, weight_ref[:, start : start + step], preferred_element_type=F32
            )
            base += step


def sine_cosine(angle):
    turns = jnp.floor(angle * (2.0 / math.pi) + 0.5)
    rest = angle - turns * 1.5703125
    rest = rest - turns * 4.837512969970703125e-4
    rest = rest - turns * 7.54978995489188216e-8
    square = rest * rest
    sine = (-1.9515295891e-4 * square + 8.3321608736e-3) * square - 1.6666654611e-1
    sine = sine * square * rest + rest
    cosine = (2.443315711809948e-5 * square - 1.388731625493765e-3) * square
    cosine = (cosine + 4.166664568298827e-2) * square * square - 0.5 * square + 1.0
    quarter = turns.astype(jnp.int32) & 3
    odd = (quarter & 1) == 1
    sine, cosine = jnp.where(odd, cosine, sine), jnp.where(odd, sine, cosine)
    sine = jnp.where(quarter >= 2, -sine, sine)
    cosine = jnp.where(jnp.logical_or(quarter == 1, quarter == 2), -cosine, cosine)
    return sine, cosine


def angle_tables(shift, freq):
    angle = shift.astype(F32) * freq
    low = iota(angle.shape, 1) < HEAD_WIDTH // 2
    sine, cosine = sine_cosine(angle)
    return cosine, jnp.where(low, -sine, sine)


def rotated(vectors, cosine, sine):
    return vectors * cosine + pltpu.roll(vectors, HEAD_WIDTH // 2, 1) * sine


def tables_kernel(
    tiles,
    ranks,
    stretch_len,
    row_total,
    stretches_ref,
    offsets_ref,
    counts_ref,
    positions_ref,
    freq_ref,
    cos_ref,
    sin_ref,
    bias_ref,
    token_cos_ref,
    token_sin_ref,
):
    slot = lax.axis_index("slot")
    row = lax.axis_index("row")
    freq = freq_ref[...]
    count = counts_ref[slot]
    arriving = tiles
    slot_tiles = stretches_ref.shape[1]
    stretches = stretches_ref[pl.ds(slot, 1), :]
    owner, _ = divide(stretches, tiles)
    slots = arriving // ranks
    place, rank_wanted = divide(iota((arriving, slot_tiles), 0), ranks)
    bits, flip = jnp.zeros_like(place), jnp.zeros_like(place)
    for i, (first, second, other) in enumerate(arrivals(slots)):
        bits = jnp.where(place == i, for_row((first, second), row), bits)
        flip = jnp.where(place == i, other, flip)
    from_slot = slot ^ bits
    from_row = row ^ flip
    match = (owner == from_slot * row_total + from_row).astype(F32)
    rank = earlier_count(match)
    picked = jnp.where(rank == rank_wanted.astype(F32), match, 0.0)
    tile_ids = iota((1, slot_tiles), 1).astype(F32)
    tile = jnp.sum(picked * tile_ids, axis=1, keepdims=True)
    page, lane = divide(stretches, 128)
    in_lane = (iota((128, slot_tiles), 0) == lane).astype(F32).astype(BF16)
    upper, lower = divide(offsets_ref[...], 64)
    page_count = upper.shape[0]
    split = jnp.concatenate([upper, lower], axis=0).astype(F32).astype(BF16)
    split = jnp.dot(split, in_lane, preferred_element_type=F32)
    offset = split[:page_count] * 64.0 + split[page_count:]
    in_page = iota((page_count, slot_tiles), 0) == page
    offset = jnp.sum(jnp.where(in_page, offset, 0.0), axis=0, keepdims=True)
    shift = jnp.sum(picked * (tile_ids * stretch_len - offset), axis=1, keepdims=True)
    cosine, sine = angle_tables(shift, freq)
    local_keys = arriving * stretch_len
    spread = lambda x: jnp.broadcast_to(
        x[:, None, :], (arriving, stretch_len, x.shape[1])
    ).reshape(local_keys, x.shape[1])
    cos_ref[...] = spread(cosine)
    sin_ref[...] = spread(sine)
    token_total = positions_ref.shape[1]
    share = token_total // row_total
    positions = positions_ref[...]
    group = bias_ref.shape[1] // token_total
    query_positions = jnp.concatenate([positions] * group, axis=1)
    first = jnp.broadcast_to(tile * stretch_len, (arriving, 128))
    _, token = divide(iota((local_keys, 128), 0), stretch_len)
    key_positions = spread(first).astype(jnp.int32) + token
    redone = (key_positions[:, :token_total] == positions).astype(F32).astype(BF16)
    redone = jnp.dot(redone, jnp.ones((token_total, 128), BF16), preferred_element_type=F32)
    usable = jnp.logical_and(key_positions < count * stretch_len, redone == 0.0)
    key_positions = jnp.where(usable, key_positions, FAR)
    for start in range(0, bias_ref.shape[1], 128):
        cols = slice(start, start + 128)
        bias_ref[:local_keys, cols] = jnp.where(
            key_positions <= query_positions[:, cols], 0.0, NEGATIVE
        )
    square = iota((token_total, token_total), 0) == iota((token_total, token_total), 1)
    column = jnp.sum(
        jnp.where(square, positions.astype(F32), 0.0), axis=1, keepdims=True
    ).astype(jnp.int32)
    new_positions = of_row(column, row, share)
    new_usable = new_positions < count * stretch_len
    new_positions = jnp.where(new_usable, new_positions, FAR)
    bias_ref[local_keys:, :] = jnp.where(new_positions <= query_positions, 0.0, NEGATIVE)
    token_cos_ref[...], token_sin_ref[...] = angle_tables(column, freq)


def of_row(value, row, share):
    kept = value[:share]
    for r in range(1, value.shape[0] // share):
        kept = jnp.where(row == r, value[r * share : (r + 1) * share], kept)
    return kept


def block_parts(blocks, stretch_rows):
    return [(ref, at) for ref in blocks for at in range(0, ref.shape[0], 2 * stretch_rows)]


def keys_of(parts, stretch_rows, cols, cosine, sine):
    keys = jnp.concatenate([ref[at : at + stretch_rows, cols] for ref, at in parts], axis=0)
    return rotated(keys.astype(F32), cosine, sine).astype(BF16)


def values_of(parts, stretch_rows, cols):
    return [ref[at + stretch_rows : at + 2 * stretch_rows, cols] for ref, at in parts]


def scores_of(keys, queries, bias):
    nt = (((1,), (1,)), ((), ()))
    scores = lax.dot_general(keys, queries, nt, preferred_element_type=F32)
    return scores * (1.0 / math.sqrt(HEAD_WIDTH)) + bias


def queries_kernel(stretch_rows, *refs):
    *arrived, cos_ref, sin_ref, bias_ref, token_cos_ref, token_sin_ref, both_ref = refs[:-3]
    q_ref, scores_ref, values_ref = refs[-3:]
    parts = block_parts(arrived, stretch_rows)
    row = lax.axis_index("row")
    token_total = token_cos_ref.shape[0]
    local_keys = cos_ref.shape[0]
    share, count = values_ref.shape[0], len(parts) * stretch_rows
    query_rows = bias_ref.shape[1]
    group = query_rows // token_total
    key_columns = arrived[0].shape[1]
    key_heads = key_columns // HEAD_WIDTH
    query_columns = group * key_columns
    cosine, sine = cos_ref[:count, :], sin_ref[:count, :]
    token_cosine, token_sine = token_cos_ref[...], token_sin_ref[...]
    bias = jnp.concatenate([bias_ref[:count, :], bias_ref[local_keys:, :]], axis=0)

    def projected(start, width=HEAD_WIDTH):
        cols = slice(start, start + width)
        return both_ref[0, :, cols] + both_ref[1, :, cols]

    all_queries, all_scores = [], []
    for head in range(key_heads):
        at = head * HEAD_WIDTH
        queries = [
            rotated(projected((head * group + j) * HEAD_WIDTH), token_cosine, token_sine)
            for j in range(group)
        ]
        queries = jnp.concatenate(queries, axis=0).astype(BF16)
        new_keys = rotated(projected(query_columns + at), token_cosine, token_sine)
        keys = keys_of(parts, stretch_rows, slice(at, at + HEAD_WIDTH), cosine, sine)
        keys = jnp.concatenate([keys, of_row(new_keys, row, share).astype(BF16)], axis=0)
        all_queries.append(queries)
        all_scores.append(scores_of(keys, queries, bias))
    new_values = projected(query_columns + key_columns, key_columns)
    values_ref[...] = of_row(new_values, row, share).astype(BF16)
    for head in range(key_heads):
        q_ref[head * query_rows : (head + 1) * query_rows, :] = all_queries[head]
        scores_ref[head * (count + share) : (head + 1) * (count + share), :] = all_scores[head]


def attend_kernel(stretch_rows, first_blocks, *refs):
    *arrived, cos_ref, sin_ref, bias_ref, q_ref, scores_ref, values_ref, out_ref, send_ref = refs
    first = block_parts(arrived[:first_blocks], stretch_rows)
    later = block_parts(arrived[first_blocks:], stretch_rows)
    count, local_keys = len(first) * stretch_rows, cos_ref.shape[0]
    known = count + values_ref.shape[0]
    query_rows = bias_ref.shape[1]
    key_heads = arrived[0].shape[1] // HEAD_WIDTH
    cosine, sine = cos_ref[count:, :], sin_ref[count:, :]
    bias = bias_ref[count:local_keys, :]
    all_scores, all_values = [], []
    for head in range(key_heads):
        cols = slice(head * HEAD_WIDTH, (head + 1) * HEAD_WIDTH)
        keys = keys_of(later, stretch_rows, cols, cosine, sine)
        queries = q_ref[head * query_rows : (head + 1) * query_rows, :]
        scores = [scores_ref[head * known : (head + 1) * known, :]]
        scores.append(scores_of(keys, queries, bias))
        all_scores.append(jnp.concatenate(scores, axis=0))
        values = values_of(first, stretch_rows, cols) + [values_ref[:, cols]]
        values += values_of(later, stretch_rows, cols)
        all_values.append(jnp.concatenate(values, axis=0))
    all_probs = []
    stats = []
    for scores in all_scores:
        peak = jnp.max(scores, axis=0, keepdims=True)
        probs = jnp.exp(scores - peak)
        stats.append((peak, jnp.sum(probs, axis=0, keepdims=True)))
        all_probs.append(probs.astype(BF16))
    stats = jnp.concatenate([x[0] for x in stats] + [x[1] for x in stats], axis=0)
    base = key_heads * HEAD_WIDTH
    out_ref[base:, :] = stats
    for part in range(3):
        term = stats.astype(BF16)
        at = base + 16 * part
        send_ref[at : at + 16, :] = jnp.concatenate(
            [term.astype(F32), jnp.zeros_like(stats)], axis=0
        ).astype(BF16)
        stats = stats - term.astype(F32)
    for head in range(key_heads):
        weighted = lax.dot_general(
            all_values[head], all_probs[head], (((0,), (0,)), ((), ())), preferred_element_type=F32
        )
        rows = slice(head * HEAD_WIDTH, (head + 1) * HEAD_WIDTH)
        out_ref[rows, :] = weighted
        send_ref[rows, :] = weighted.astype(BF16)


def output_kernel(key_heads, own_ref, other_ref, w_ref, keep_ref, send_ref):
    token_total = keep_ref.shape[0] * lax.axis_size("col")
    group = own_ref.shape[1] // token_total
    base = key_heads * HEAD_WIDTH
    results = []
    own_stats = own_ref[base:, :]
    terms = [
        other_ref[base + 16 * part : base + 16 * (part + 1), :].astype(F32) for part in range(3)
    ]
    other_stats = (terms[0] + terms[1] + terms[2])[: 2 * key_heads]
    peaks = jnp.maximum(own_stats[:key_heads], other_stats[:key_heads])
    own_scales = jnp.exp(own_stats[:key_heads] - peaks)
    other_scales = jnp.exp(other_stats[:key_heads] - peaks)
    totals = own_stats[key_heads:] * own_scales + other_stats[key_heads:] * other_scales
    for head in range(key_heads):
        rows = slice(head * HEAD_WIDTH, (head + 1) * HEAD_WIDTH)
        at = slice(head, head + 1)
        total = totals[at]
        weighted = own_ref[rows, :] * own_scales[at]
        weighted += other_ref[rows, :].astype(F32) * other_scales[at]
        results.append(jnp.transpose(weighted / total).astype(BF16))
    tokens = jnp.concatenate(
        [
            result[j * token_total : (j + 1) * token_total]
            for result in results
            for j in range(group)
        ],
        axis=1,
    )
    share = keep_ref.shape[0]
    first = lax.axis_index("col") == 0
    part = jnp.dot(tokens, w_ref[...], preferred_element_type=F32)
    keep_ref[...] = jnp.where(first, part[:share], part[share:])
    send_ref[...] = jnp.where(first, part[share:], part[:share]).astype(BF16)


def cost(us):
    return pl.CostEstimate(flops=us * 1_000_000_000, bytes_accessed=1000, transcendentals=0)


def in_hbm(value):
    return pltpu.with_memory_space_constraint(value, pltpu.HBM)


def merge_kernel(*refs):
    count = len(refs) // 2
    kept, given, outs = refs[:count], refs[count], refs[count + 1 :]
    rows = kept[0].shape[0]
    for i in range(count):
        outs[i][:rows] = kept[i][...]
        outs[i][rows:] = given[i * rows : (i + 1) * rows]


def merge(kept, given, grant):
    rows, columns = kept[0].shape
    return pl.pallas_call(
        merge_kernel,
        out_shape=[jax.ShapeDtypeStruct((2 * rows, columns), BF16)] * len(kept),
        in_specs=[VMEM] * (len(kept) + 1),
        out_specs=[VMEM] * len(kept),
        compiler_params=params(grant),
        cost_estimate=cost(0),
        name="merge",
    )(*kept, given)


def params(mib):
    return pltpu.CompilerParams(vmem_limit_bytes=mib * MIB)


def on_device(
    hidden,
    w_query,
    key_weight,
    value_weight,
    w_out,
    kv_store,
    stretch_offset,
    tile_stretch,
    slot_count,
    recomp_pos,
):
    slot_total = lax.axis_size("slot")
    row_total = lax.axis_size("row")
    tiles, _, stretch_len, key_columns = kv_store.shape
    slot_tiles = tile_stretch.shape[1]
    ranks = slot_tiles // (slot_total * row_total)
    token_total = hidden.shape[1]
    query_columns = w_query.shape[1]
    key_heads = key_columns // HEAD_WIDTH
    group = query_columns // key_columns
    query_rows = group * token_total
    per_slot = ranks * 2 * stretch_len
    local_keys = tiles * stretch_len
    share = token_total // row_total
    all_keys = local_keys + share
    swap = [(0, 1), (1, 0)]
    grant = 16 if slot_total <= 8 else 40

    freq = np.arange(HEAD_WIDTH // 2, dtype=np.float64)
    freq = (ROPE_BASE ** (-2.0 * freq / HEAD_WIDTH)).astype(np.float32)
    freq = jnp.asarray(np.concatenate([freq, freq])[None, :])

    store_shape = (tiles * 2 * stretch_len, key_columns)
    step = key_columns
    direct, shared = exchanges(slot_total)
    block = jax.ShapeDtypeStruct((per_slot, key_columns), BF16)
    *outgoing, give = pl.pallas_call(
        functools.partial(pack_kernel, tiles, ranks, stretch_len),
        out_shape=[block] * (len(direct) + 1 + len(shared))
        + [jax.ShapeDtypeStruct((len(shared) * per_slot, key_columns), BF16)],
        in_specs=[HBM, HBM],
        out_specs=[VMEM] * (len(direct) + len(shared) + 2),
        scratch_shapes=[
            pltpu.VMEM(tile_stretch.shape, jnp.int32),
            pltpu.VMEM(store_shape, BF16),
            pltpu.VMEM((slot_total, 128), F32),
            pltpu.SemaphoreType.DMA((2,)),
        ],
        compiler_params=params(grant),
        cost_estimate=cost(8),
        name="pack",
    )(in_hbm(tile_stretch), in_hbm(kv_store.reshape(store_shape)))
    own_block, kept = outgoing[len(direct)], outgoing[len(direct) + 1 :]
    given = lax.ppermute(give, "row", swap)
    merged = merge(kept, given, grant)
    arrived = [
        lax.ppermute(block, "slot", [(s, s ^ k) for s in range(slot_total)])
        for block, k in zip(outgoing, direct)
    ]
    arrived.append(own_block)
    for sent, pair in zip(merged, shared):
        pairs = [
            (s * row_total + r, (s ^ pair[r]) * row_total + r)
            for s in range(slot_total)
            for r in range(row_total)
        ]
        arrived.append(lax.ppermute(sent, ("slot", "row"), pairs))

    projected = pl.pallas_call(
        functools.partial(project_kernel, step),
        out_shape=jax.ShapeDtypeStruct((token_total, query_columns + 2 * key_columns), F32),
        in_specs=[ANY] + [VMEM] * 4,
        out_specs=VMEM,
        compiler_params=params(grant),
        cost_estimate=cost(0),
        name="project",
    )(merged[0], hidden[0], w_query, key_weight, value_weight)
    both = lax.all_gather(projected, "row")

    tables = pl.pallas_call(
        functools.partial(tables_kernel, tiles, ranks, stretch_len, row_total),
        out_shape=(
            jax.ShapeDtypeStruct((local_keys, HEAD_WIDTH), F32),
            jax.ShapeDtypeStruct((local_keys, HEAD_WIDTH), F32),
            jax.ShapeDtypeStruct((all_keys, query_rows), F32),
            jax.ShapeDtypeStruct((token_total, HEAD_WIDTH), F32),
            jax.ShapeDtypeStruct((token_total, HEAD_WIDTH), F32),
        ),
        in_specs=[VMEM, VMEM, SMEM, VMEM, VMEM],
        out_specs=(VMEM,) * 5,
        compiler_params=params(grant),
        cost_estimate=cost(0),
        name="tables",
    )(tile_stretch, stretch_offset.reshape(-1, 128), slot_count, recomp_pos, freq)

    first_blocks = len(direct) + 1
    known = first_blocks * ranks * stretch_len + share
    queries, scores, new_values = pl.pallas_call(
        functools.partial(queries_kernel, ranks * stretch_len),
        out_shape=(
            jax.ShapeDtypeStruct((key_heads * query_rows, HEAD_WIDTH), BF16),
            jax.ShapeDtypeStruct((key_heads * known, query_rows), F32),
            jax.ShapeDtypeStruct((share, key_columns), BF16),
        ),
        in_specs=[VMEM] * (first_blocks + 6),
        out_specs=(VMEM,) * 3,
        compiler_params=params(grant),
        cost_estimate=cost(0),
        name="queries",
    )(*arrived[:first_blocks], *tables, both)
    partial, to_swap = pl.pallas_call(
        functools.partial(attend_kernel, ranks * stretch_len, first_blocks),
        out_shape=(
            jax.ShapeDtypeStruct((key_heads * HEAD_WIDTH + 2 * key_heads, query_rows), F32),
            jax.ShapeDtypeStruct((key_heads * HEAD_WIDTH + 3 * 16, query_rows), BF16),
        ),
        in_specs=[VMEM] * (len(direct) + len(shared) + 7),
        out_specs=(VMEM, VMEM),
        compiler_params=params(grant),
        cost_estimate=cost(0),
        name="attend",
    )(*arrived, *tables[:3], queries, scores, new_values)
    partial_other = lax.ppermute(to_swap, "row", swap)

    out_columns = w_out.shape[1]
    out_share = token_total // lax.axis_size("col")
    keep, send = pl.pallas_call(
        functools.partial(output_kernel, key_heads),
        out_shape=(
            jax.ShapeDtypeStruct((out_share, out_columns), F32),
            jax.ShapeDtypeStruct((out_share, out_columns), BF16),
        ),
        in_specs=[VMEM, VMEM, VMEM],
        out_specs=(VMEM, VMEM),
        compiler_params=params(grant),
        name="output",
    )(partial, partial_other, w_out)
    received = lax.ppermute(send, "col", swap)
    return (keep + received.astype(F32)).astype(BF16)[None]


def solution(mesh):
    return jax.shard_map(
        on_device,
        mesh=mesh,
        in_specs=(
            P("slot", None, "row"),
            P("row", "col"),
            P("row", "col"),
            P("row", "col"),
            P("col", "row"),
            P(("slot", "row"), None, None, "col"),
            P(),
            P(),
            P(),
            P("slot", None),
        ),
        out_specs=P("slot", "col", "row"),
        check_vma=False,
    )
```
